256 devices in a mesh: face: 8 (over x, y_hi), tile: 32 (over y_lo, z, core).
Axes of the slice: x: 4, y: 4 (y_hi: 2, y_lo: 2; y = y_hi * 2 + y_lo), z: 8, core: 2. Of those that a mesh axis runs over, the one named last changes fastest.
Arguments:
- features: bfloat16 [8, 256, 256, 256], P('face', 'tile'), may hold values from -2000 to 2000
- cotangent: bfloat16 [8, 256, 256, 256], P('face', 'tile'), may hold values from -10 to 10
- w_fine: bfloat16 [9, 256, 256], replicated, may hold values from -0.125 to 0.125
- w_coarse: bfloat16 [9, 256, 256], replicated, may hold values from -0.125 to 0.125
- gain: float32 [256], replicated, may hold values from 0.1 to 1.9
- neighbors: int32 [8, 4], replicated, may hold values from 0 to 7, as said below
- neighbor_edges: int32 [8, 4], replicated, may hold values from 0 to 3, as said below
Outputs:
- output: bfloat16 [8, 256, 256, 256], P('face', 'tile')
- grad_features: float32 [8, 256, 256, 256], P('face', 'tile')
- grad_w_fine: float32 [9, 256, 256], P(None, 'tile')
- grad_w_coarse: float32 [9, 256, 256], P(None, 'tile')
- grad_gain: float32 [256], replicated
The draws below stay inside these ranges and needn't reach their ends.
Inputs may be any that keep to these rules, and one draw needn't show every extreme that they name: The right edge of face f meets the left edge of face neighbors[f,1], and the left neighbours name f back; these column gluings form one cycle through all faces. Top and bottom edges are glued in pairs: the face named at an edge names f back at the edge given by neighbor_edges. A face's top may meet its own bottom. neighbor_edges[f,1] is 3 and neighbor_edges[f,3] is 1; the entries at the top and bottom edges are 0 or 2.
All inputs are finite; a program needn't handle non-finite values.
Results may differ from the reference program's by a relative error of at most 0.012.
Values may be sent and summed in bfloat16 or wider, within the bound.
A program may use at most 128 MiB of HBM per device.

```python
import jax
import jax.numpy as jnp
from jax import lax

C = 256
GROUPS = 32
RD = 8
NF = 8
FS = 256


def face_tables(key):
    column_key, rim_key = jax.random.split(key)
    order = jax.random.permutation(column_key, NF).astype(jnp.int32)
    right_face = jnp.zeros((NF,), jnp.int32).at[order].set(jnp.roll(order, -1))
    left_face = jnp.zeros((NF,), jnp.int32).at[order].set(jnp.roll(order, 1))
    slots = jax.random.permutation(rim_key, 2 * NF).astype(jnp.int32)
    first_slots = slots[0::2]
    second_slots = slots[1::2]
    partner = jnp.zeros((2 * NF,), jnp.int32).at[first_slots].set(second_slots).at[second_slots].set(first_slots)
    top_partner = partner[0::2]
    bottom_partner = partner[1::2]
    neighbors = jnp.stack([top_partner // 2, right_face, bottom_partner // 2, left_face], axis=1)
    edges = jnp.stack([top_partner % 2 * 2, jnp.full((NF,), 3, jnp.int32), bottom_partner % 2 * 2, jnp.full((NF,), 1, jnp.int32)], axis=1)
    return (neighbors.astype(jnp.int32), edges.astype(jnp.int32))


def marked_cells(key):
    key = jax.random.fold_in(key, 97)
    blocks = FS // RD
    chosen_face = jax.random.randint(key, (blocks,), 0, NF)
    row_block = jnp.arange(FS) // RD
    chan_block = jnp.arange(C) // (C // blocks)
    face_match = jnp.arange(NF)[:, None] == chosen_face[row_block][None, :]
    chan_match = chan_block[None, :] == row_block[:, None]
    return face_match[:, :, None, None] & chan_match[None, :, None, :]


def draw_neighbors(key, part):
    tables = face_tables(key)
    return tables[0]


def draw_neighbor_edges(key, part):
    tables = face_tables(key)
    return tables[1]


def draw_features(key, part):
    marked = marked_cells(key)
    key = jax.random.fold_in(key, 11)
    row_key, column_key, channel_key, base_key = jax.random.split(key, 4)
    position = (jnp.arange(NF, dtype=jnp.float32)[:, None] * FS + jnp.arange(FS, dtype=jnp.float32)[None, :]) / (NF * FS)
    shape = (NF, FS, FS, C)
    row_scale = jnp.exp(0.55 * position + 1.15 * jax.random.uniform(row_key, (NF, FS)))
    base = jnp.clip(jax.random.normal(base_key, shape), -5.0, 5.0)
    column_scale = jnp.exp(1.15 * jax.random.uniform(column_key, (FS,)))
    channel_scale = jnp.exp(1.15 * jax.random.uniform(channel_key, (C,)))
    values = base * row_scale[:, :, None, None] * column_scale[None, None, :, None] * channel_scale
    heavy = 64.0 * (base + 1.5) * channel_scale
    values = jnp.where(marked, heavy, values)
    return values.astype(jnp.bfloat16)


def draw_cotangent(key, part):
    marked = marked_cells(key)
    key = jax.random.fold_in(key, 23)
    offset_key, base_key, sign_key, size_key = jax.random.split(key, 4)
    shape = (NF, FS, FS, C)
    offset = jax.random.uniform(offset_key, (C,), minval=-1.5, maxval=1.5)
    extra_sign = 2.0 * jax.random.randint(sign_key, (C,), 0, 2).astype(jnp.float32) - 1.0
    extra = extra_sign * jax.random.uniform(size_key, (C,), minval=2.0, maxval=3.0)
    base = jnp.clip(jax.random.normal(base_key, shape), -5.0, 5.0)
    values = base + offset + jnp.where(marked, extra, 0.0)
    return values.astype(jnp.bfloat16)


def noise(rng, shape, spread, bound, held_as=jnp.bfloat16):
    array = spread * jax.random.normal(rng, shape, jnp.float32)
    return jnp.clip(array, min=-bound, max=bound).astype(held_as)


def setup_inputs(seed: int = 0) -> dict:
    streams_of = jax.random.split(jax.random.key(seed), 8)
    return {
        "features": draw_features(jax.random.fold_in(streams_of[7], 71), 0),
        "cotangent": draw_cotangent(jax.random.fold_in(streams_of[7], 71), 0),
        "w_fine": noise(streams_of[2], (9, C, C), (9 * C) ** -0.5, 0.125),
        "w_coarse": noise(streams_of[3], (9, C, C), (9 * C) ** -0.5, 0.125),
        "gain": jnp.clip(1.0 + 0.18 * jax.random.normal(streams_of[4], (C,), jnp.float32), 0.1, 1.9),
        "neighbors": draw_neighbors(jax.random.fold_in(streams_of[7], 71), 0),
        "neighbor_edges": draw_neighbor_edges(jax.random.fold_in(streams_of[7], 71), 0),
    }


def silu_slope(values):
    sigma = jax.nn.sigmoid(values)
    return sigma * (1.0 + values * (1.0 - sigma))

def glue(left_rec, right_rec, top_rec, bottom_rec, neighbors, neighbor_edges):
    left_side = right_rec[neighbors[:, 3]]
    right_side = left_rec[neighbors[:, 1]]
    top_edge = neighbor_edges[:, 0][:, None, None]
    bottom_edge = neighbor_edges[:, 2][:, None, None]
    top_side = jnp.where(top_edge == 2, bottom_rec[neighbors[:, 0]], top_rec[neighbors[:, 0]][:, ::-1])
    bottom_side = jnp.where(bottom_edge == 0, top_rec[neighbors[:, 2]], bottom_rec[neighbors[:, 2]][:, ::-1])
    return (left_side, right_side, top_side, bottom_side)

def pad_glued(field, neighbors, neighbor_edges):
    left_side, right_side, top_side, bottom_side = glue(field[:, :, 0], field[:, :, -1], field[:, 0], field[:, -1], neighbors, neighbor_edges)
    padded = jnp.pad(field, ((0, 0), (1, 1), (1, 1), (0, 0)))
    padded = padded.at[:, 1:-1, 0].set(left_side)
    padded = padded.at[:, 1:-1, -1].set(right_side)
    padded = padded.at[:, 0, 1:-1].set(top_side)
    padded = padded.at[:, -1, 1:-1].set(bottom_side)
    return padded

def convolve(padded, weights):
    side = padded.shape[1] - 2
    total = jnp.zeros(padded.shape[:1] + (side, side, weights.shape[2]), jnp.float32)
    for tap in range(9):
        row_step, col_step = divmod(tap, 3)
        tap_slice = padded[:, row_step:row_step + side, col_step:col_step + side]
        total = total + jnp.dot(tap_slice, weights[tap], preferred_element_type=jnp.float32)
    return total

def convolve_back(grad, weights, neighbors, neighbor_edges):
    side = grad.shape[1]
    widened = jnp.pad(grad, ((0, 0), (2, 2), (2, 2), (0, 0)))
    full = jnp.zeros(grad.shape[:1] + (side + 2, side + 2, weights.shape[1]), jnp.float32)
    for tap in range(9):
        row_step = tap // 3 - 1
        col_step = tap % 3 - 1
        tap_slice = widened[:, 1 - row_step:1 - row_step + side + 2, 1 - col_step:1 - col_step + side + 2]
        full = full + jnp.dot(tap_slice, weights[tap].T, preferred_element_type=jnp.float32)
    left_rec = full[:, 1:-1, 0].astype(jnp.bfloat16)
    right_rec = full[:, 1:-1, -1].astype(jnp.bfloat16)
    top_rec = full[:, 0, 1:-1].astype(jnp.bfloat16)
    bottom_rec = full[:, -1, 1:-1].astype(jnp.bfloat16)
    left_side, right_side, top_side, bottom_side = glue(left_rec, right_rec, top_rec, bottom_rec, neighbors, neighbor_edges)
    result = full[:, 1:-1, 1:-1]
    result = result.at[:, :, 0].add(left_side.astype(jnp.float32))
    result = result.at[:, :, -1].add(right_side.astype(jnp.float32))
    result = result.at[:, 0, :].add(top_side.astype(jnp.float32))
    result = result.at[:, -1, :].add(bottom_side.astype(jnp.float32))
    return result

def weight_grad(padded, grad):
    side = grad.shape[1]
    terms = []
    for tap in range(9):
        row_step, col_step = divmod(tap, 3)
        tap_slice = padded[:, row_step:row_step + side, col_step:col_step + side]
        terms.append(lax.dot_general(tap_slice, grad, (((0, 1, 2), (0, 1, 2)), ((), ())), preferred_element_type=jnp.float32))
    return jnp.stack(terms)

def pool_sum(values):
    faces, side = (values.shape[0], values.shape[1])
    return lax.optimization_barrier(jnp.sum(values.reshape(faces, side // 2, 2, side // 2, 2, values.shape[3]), axis=(2, 4)))

def upsample(values):
    return jnp.repeat(jnp.repeat(values, 2, axis=1), 2, axis=2)

def reference(features, cotangent, w_fine, w_coarse, gain, neighbors, neighbor_edges):
    cells = NF * FS * FS
    group_size = C // GROUPS
    count = cells * group_size
    values = features.astype(jnp.float32)
    sums = lax.optimization_barrier(jnp.sum(lax.optimization_barrier(jnp.sum(values, axis=(0, 1, 2))).reshape(GROUPS, group_size), axis=1))
    squares = lax.optimization_barrier(jnp.sum(lax.optimization_barrier(jnp.sum(values * values, axis=(0, 1, 2))).reshape(GROUPS, group_size), axis=1))
    group_mean = sums / count
    inverse = lax.rsqrt(squares / count - group_mean * group_mean + 1e-05)
    mean_chan = jnp.repeat(group_mean, group_size)
    inverse_chan = jnp.repeat(inverse, group_size)
    normed = (values - mean_chan) * inverse_chan
    act = normed * gain
    hidden = jax.nn.silu(act).astype(jnp.bfloat16)
    hidden_pad = pad_glued(hidden, neighbors, neighbor_edges)
    fine = convolve(hidden_pad, w_fine).astype(jnp.bfloat16)
    pooled = pool_sum(fine.astype(jnp.float32)) * 0.25
    coarse_in = jax.nn.silu(pooled).astype(jnp.bfloat16)
    coarse_pad = pad_glued(coarse_in, neighbors, neighbor_edges)
    coarse_out = convolve(coarse_pad, w_coarse)
    output = (fine.astype(jnp.float32) + upsample(coarse_out)).astype(jnp.bfloat16)
    upstream = cotangent.astype(jnp.float32)
    grad_coarse_out = pool_sum(upstream).astype(jnp.bfloat16)
    grad_coarse_in = convolve_back(grad_coarse_out, w_coarse, neighbors, neighbor_edges)
    grad_pooled = grad_coarse_in * silu_slope(pooled)
    grad_fine = (upstream + upsample(grad_pooled) * 0.25).astype(jnp.bfloat16)
    grad_hidden = convolve_back(grad_fine, w_fine, neighbors, neighbor_edges)
    grad_act = grad_hidden * silu_slope(act)
    slope_sum = lax.optimization_barrier(jnp.sum(grad_act * normed, axis=(0, 1, 2)))
    shift_sum = lax.optimization_barrier(jnp.sum(grad_act, axis=(0, 1, 2)))
    grad_gain = slope_sum / cells
    group_shift = lax.optimization_barrier(jnp.sum((gain * shift_sum).reshape(GROUPS, group_size), axis=1)) / count
    group_slope = lax.optimization_barrier(jnp.sum((gain * slope_sum).reshape(GROUPS, group_size), axis=1)) / count
    grad_features = inverse_chan * (gain * grad_act - jnp.repeat(group_shift, group_size) - normed * jnp.repeat(group_slope, group_size))
    grad_w_fine = weight_grad(hidden_pad, grad_fine) / cells
    grad_w_coarse = weight_grad(coarse_pad, grad_coarse_out) / cells
    return (output, grad_features, grad_w_fine, grad_w_coarse, grad_gain)
```

```python
import functools

import jax
import jax.numpy as jnp
from jax import lax
from jax.experimental import pallas as pl
from jax.experimental.pallas import tpu as pltpu
from jax.sharding import PartitionSpec as P

BF = jnp.bfloat16
F32 = jnp.float32
MESH = pl.DeviceIdType.MESH
NF = 8
NT = 32
NZ = 16
RD = 8
FS = 256
CS = 128
C = 256
GROUP = 8
SLOTS = 16
CELLS = NF * FS * FS
VMEM_LIMIT = 60 * 1024 * 1024

VM = pl.BlockSpec(memory_space=pltpu.VMEM)
SM = pl.BlockSpec(memory_space=pltpu.SMEM)
DMA = pltpu.SemaphoreType.DMA


def remote(src, dst, send, recv, face, tile):
    return pltpu.make_async_remote_copy(
        src_ref=src,
        dst_ref=dst,
        send_sem=send,
        recv_sem=recv,
        device_id=(face, tile),
        device_id_type=MESH,
    )


def place():
    return lax.axis_index("face"), lax.axis_index("tile")


def is_rim(tile):
    return (tile == 0) | (tile == NT - 1)


def slot_device(slot):
    return lax.div(slot, 2), (NT - 1) * lax.rem(slot, 2)


def my_slot(face, tile):
    return 2 * face + jnp.where(tile == NT - 1, 1, 0)


def multiple(value, of):
    return pl.multiple_of(value * of, of)


def signal(barrier, face, tile):
    pl.semaphore_signal(barrier, inc=1, device_id=(face, tile), device_id_type=MESH)


def line_a(face, tile, step):
    mine = lax.rem(tile, NZ)
    other = lax.rem(mine + step, NZ)
    return mine, other, (face, tile - mine + other)


def line_b(face, tile, step):
    mine = face * 2 + lax.div(tile, NZ)
    other = lax.rem(mine + step, 2 * NF)
    return mine, other, (lax.div(other, 2), lax.rem(other, 2) * NZ + lax.rem(tile, NZ))


def barrier_signal(halos):
    face, tile = place()
    barrier = pltpu.get_barrier_semaphore()

    @pl.loop(1, NZ)
    def _(step):
        for line in (line_a, line_b):
            _, _, device = line(face, tile, step)
            signal(barrier, *device)

    if halos:
        signal(barrier, face, lax.rem(tile + 1, NT))
        signal(barrier, face, lax.rem(tile + NT - 1, NT))

        @pl.when(is_rim(tile))
        def _():
            mine = my_slot(face, tile)

            @pl.loop(1, SLOTS)
            def _(step):
                signal(barrier, *slot_device(lax.rem(mine + step, SLOTS)))


def barrier_wait(halos, more=0):
    _, tile = place()
    barrier = pltpu.get_barrier_semaphore()
    if not halos:
        pl.semaphore_wait(barrier, 2 * (NZ - 1) + more)
        return

    @pl.when(is_rim(tile))
    def _():
        pl.semaphore_wait(barrier, 2 * (NZ - 1) + 2 + SLOTS - 1)

    @pl.when(~is_rim(tile))
    def _():
        pl.semaphore_wait(barrier, 2 * (NZ - 1) + 2)


def sum_start(line, own, buf, send, recv):
    face, tile = place()

    @pl.loop(1, NZ)
    def _(step):
        mine, other, device = line(face, tile, step)
        remote(own, buf.at[mine], send.at[other], recv.at[mine], *device).start()

    mine, _, _ = line(face, tile, 0)
    buf[mine] = own[...]


def sum_finish(line, own, buf, send, recv):
    face, tile = place()

    @pl.loop(1, NZ)
    def _(step):
        _, other, device = line(face, tile, step)
        copy = remote(own, buf.at[other], send.at[other], recv.at[other], *device)
        copy.wait_recv()
        copy.wait_send()

    total = buf[0]
    for i in range(1, NZ):
        total = total + buf[i]
    return total


SUM_SCRATCH = [
    pltpu.VMEM((8, C), F32),
    pltpu.VMEM((8, C), F32),
    pltpu.VMEM((NZ, 8, C), F32),
    pltpu.VMEM((NZ, 8, C), F32),
    DMA((NZ,)),
    DMA((NZ,)),
    DMA((NZ,)),
    DMA((NZ,)),
]


HALO_SCRATCH = [
    pltpu.VMEM((SLOTS, 16, C), BF),
    pltpu.VMEM((SLOTS, 16, 128), BF),
    pltpu.VMEM((SLOTS, 16, C), BF),
    pltpu.VMEM((SLOTS, 16, 128), BF),
    pltpu.VMEM((32, C), F32),
    pltpu.VMEM((32, C), BF),
    pltpu.VMEM((NF, 32, C), BF),
    DMA((4,)),
    DMA((4,)),
    DMA((SLOTS,)),
    DMA((SLOTS,)),
    DMA((SLOTS,)),
    DMA((SLOTS,)),
    DMA((SLOTS,)),
    DMA((SLOTS,)),
    DMA((SLOTS,)),
    DMA((SLOTS,)),
    DMA((NF,)),
    DMA((NF,)),
    DMA((4,)),
]


class Halo:
    def __init__(self, fine, coarse, outs, scratch, tables):
        self.fine, self.coarse = fine, coarse
        self.hf, self.hc, self.r2f, self.r2c, self.sides = outs
        (
            self.r1f,
            self.r1c,
            self.stf,
            self.stc,
            self.rows,
            self.srec,
            self.sall,
            self.hs,
            self.hr,
            self.f1s,
            self.f1r,
            self.c1s,
            self.c1r,
            self.f2s,
            self.f2r,
            self.c2s,
            self.c2r,
            self.ss,
            self.sr,
            self.own,
        ) = scratch
        self.nb, self.ed = tables
        self.face, self.tile = place()

    def rows_copies(self):
        up = lax.rem(self.tile + 1, NT)
        down = lax.rem(self.tile + NT - 1, NT)
        plan = (
            (self.fine.at[RD - 1], self.hf.at[0], up),
            (self.fine.at[0], self.hf.at[1], down),
            (self.coarse.at[RD // 2 - 1], self.hc.at[0], up),
            (self.coarse.at[0], self.hc.at[1], down),
        )
        return [
            remote(src, dst, self.hs.at[i], self.hr.at[i], self.face, to)
            for i, (src, dst, to) in enumerate(plan)
        ]

    def chunk(self, slot):
        fine_row = jnp.where(self.tile == 0, 0, RD - 1)
        coarse_row = jnp.where(self.tile == 0, 0, RD // 2 - 1)
        return (
            self.fine.at[fine_row, pl.ds(multiple(slot, 16), 16), :],
            self.coarse.at[
                coarse_row,
                pl.ds(multiple(lax.div(slot, 2), 16), 16),
                pl.ds(multiple(lax.rem(slot, 2), 128), 128),
            ],
        )

    def landing(self, slot):
        return (
            self.r2f.at[pl.ds(multiple(slot, 16), 16), :],
            self.r2c.at[
                pl.ds(multiple(lax.div(slot, 2), 16), 16),
                pl.ds(multiple(lax.rem(slot, 2), 128), 128),
            ],
        )

    def hop1(self, step):
        mine = my_slot(self.face, self.tile)
        other = lax.rem(mine + step, SLOTS)
        device = slot_device(other)
        src_f, src_c = self.chunk(other)
        return (
            remote(src_f, self.r1f.at[mine], self.f1s.at[other], self.f1r.at[mine], *device),
            remote(src_c, self.r1c.at[mine], self.c1s.at[other], self.c1r.at[mine], *device),
        )

    def hop1_wait(self, step):
        mine = my_slot(self.face, self.tile)
        other = lax.rem(mine + step, SLOTS)
        device = slot_device(other)
        src_f, src_c = self.chunk(other)
        for copy in (
            remote(src_f, self.r1f.at[other], self.f1s.at[other], self.f1r.at[other], *device),
            remote(src_c, self.r1c.at[other], self.c1s.at[other], self.c1r.at[other], *device),
        ):
            copy.wait_recv()
            copy.wait_send()

    def hop2(self, step):
        mine = my_slot(self.face, self.tile)
        other = lax.rem(mine + step, SLOTS)
        device = slot_device(other)
        dst_f, dst_c = self.landing(mine)
        return (
            remote(self.stf.at[other], dst_f, self.f2s.at[other], self.f2r.at[mine], *device),
            remote(self.stc.at[other], dst_c, self.c2s.at[other], self.c2r.at[mine], *device),
        )

    def hop2_wait(self, step):
        mine = my_slot(self.face, self.tile)
        other = lax.rem(mine + step, SLOTS)
        device = slot_device(other)
        dst_f, dst_c = self.landing(other)
        for copy in (
            remote(self.stf.at[other], dst_f, self.f2s.at[other], self.f2r.at[other], *device),
            remote(self.stc.at[other], dst_c, self.c2s.at[other], self.c2r.at[other], *device),
        ):
            copy.wait_recv()
            copy.wait_send()

    def start(self):
        for copy in self.rows_copies():
            copy.start()

        @pl.when(is_rim(self.tile))
        def _():
            @pl.loop(1, SLOTS)
            def _(step):
                for copy in self.hop1(step):
                    copy.start()

            mine = my_slot(self.face, self.tile)
            src_f, src_c = self.chunk(mine)
            keep = (
                pltpu.make_async_copy(src_f, self.r1f.at[mine], self.own.at[0]),
                pltpu.make_async_copy(src_c, self.r1c.at[mine], self.own.at[1]),
            )
            for copy in keep:
                copy.start()
            for copy in keep:
                copy.wait()

    def middle(self):
        for copy in self.rows_copies():
            copy.wait_recv()
            copy.wait_send()
        fine_rows = [self.hf.at[0]] + [self.fine.at[r] for r in range(RD)] + [self.hf.at[1]]
        coarse_rows = [self.hc.at[0]] + [self.coarse.at[r] for r in range(RD // 2)]
        coarse_rows += [self.hc.at[1]]
        for i, row in enumerate(fine_rows + coarse_rows):
            side = row.shape[0]
            self.rows[i : i + 1, :] = row[0:16, :].astype(F32)[0:1]
            self.rows[16 + i : 17 + i, :] = row[side - 16 : side, :].astype(F32)[15:16]
        self.srec[...] = self.rows[...].astype(BF)

        @pl.loop(1, NF)
        def _(step):
            other = lax.rem(self.face + step, NF)
            remote(
                self.srec,
                self.sall.at[self.face],
                self.ss.at[other],
                self.sr.at[self.face],
                other,
                self.tile,
            ).start()

        self.sall[self.face] = self.srec[...]

        @pl.when(is_rim(self.tile))
        def _():
            mine = my_slot(self.face, self.tile)

            @pl.loop(1, SLOTS)
            def _(step):
                self.hop1_wait(step)

            @pl.loop(0, SLOTS)
            def _(slot):
                face, edge = lax.div(slot, 2), 2 * lax.rem(slot, 2)
                source = 2 * self.nb[face, edge] + lax.div(self.ed[face, edge], 2)
                self.stf[slot] = self.r1f[source]
                self.stc[slot] = self.r1c[source]

            @pl.loop(1, SLOTS)
            def _(step):
                for copy in self.hop2(step):
                    copy.start()

            dst_f, dst_c = self.landing(mine)
            keep = (
                pltpu.make_async_copy(self.stf.at[mine], dst_f, self.own.at[2]),
                pltpu.make_async_copy(self.stc.at[mine], dst_c, self.own.at[3]),
            )
            for copy in keep:
                copy.start()
            for copy in keep:
                copy.wait()

    def finish(self):
        @pl.loop(1, NF)
        def _(step):
            other = lax.rem(self.face + step, NF)
            copy = remote(
                self.srec,
                self.sall.at[other],
                self.ss.at[other],
                self.sr.at[other],
                other,
                self.tile,
            )
            copy.wait_recv()
            copy.wait_send()

        left_face, right_face = self.nb[self.face, 3], self.nb[self.face, 1]
        self.sides[0:16, :] = self.sall[left_face, 16:32, :]
        self.sides[16:32, :] = self.sall[right_face, 0:16, :]

        @pl.when(is_rim(self.tile))
        def _():
            @pl.loop(1, SLOTS)
            def _(step):
                self.hop2_wait(step)


HALO_OUTS = [
    jax.ShapeDtypeStruct((2, FS, C), BF),
    jax.ShapeDtypeStruct((2, CS, C), BF),
    jax.ShapeDtypeStruct((FS, C), BF),
    jax.ShapeDtypeStruct((CS, C), BF),
    jax.ShapeDtypeStruct((32, C), BF),
]


def iota(shape, dim):
    return lax.broadcasted_iota(jnp.int32, shape, dim)


def dot(a, b):
    return jnp.dot(a, b, preferred_element_type=F32)


def sigmoid(values):
    return 0.5 * jnp.tanh(0.5 * values) + 0.5


def pool_matrix():
    row, col = iota((CS, 2 * FS), 0), iota((CS, 2 * FS), 1)
    return jnp.where(lax.div(lax.rem(col, FS), 2) == row, 1.0, 0.0).astype(BF)


def spread_matrix():
    row, col = iota((FS, 2 * CS), 0), iota((FS, 2 * CS), 1)
    return jnp.where(lax.rem(col, CS) == lax.div(row, 2), 1.0, 0.0).astype(BF)


def spread(matrix, values):
    high = values.astype(BF)
    low = (values - high.astype(F32)).astype(BF)
    return dot(matrix, jnp.concatenate([high, low], axis=0))


def rim_matrix(side, flip):
    row, col = iota((side, side), 0), iota((side, side), 1)
    source = jnp.where(flip, side - 1 - row, row)
    return jnp.where(col == source, 1.0, 0.0).astype(BF)


def store_shifted(ref, row, values, left, right):
    n = values.shape[0]
    position = iota(values.shape, 0)
    before = jnp.where(position == 0, left, pltpu.roll(values, 1, 0))
    after = jnp.where(position == n - 1, right, pltpu.roll(values, n - 1, 0))
    ref[row, :, 0:C] = before.astype(BF)
    ref[row, :, C : 2 * C] = values.astype(BF)
    ref[row, :, 2 * C : 3 * C] = after.astype(BF)


def group_sum(values):
    lane = iota(values.shape, 1)
    for width in (1, 2, 4):
        up = pltpu.roll(values, width, 1)
        down = pltpu.roll(values, C - width, 1)
        values = values + jnp.where(lax.rem(lax.div(lane, width), 2) == 0, down, up)
    return values


def norm_vectors(total):
    grouped = group_sum(total) / (CELLS * GROUP)
    mean, second = grouped[0:1], grouped[1:2]
    return mean, lax.rsqrt(second - mean * mean + 1e-05)


def edge_flags(ed_ref):
    face, tile = place()
    first, last = tile == 0, tile == NT - 1
    flip_top = first & (ed_ref[face, 0] != 2)
    flip_bottom = last & (ed_ref[face, 2] != 0)
    return first, last, flip_top, flip_bottom


def masked_sides(sides, first, last):
    row = lax.rem(iota(sides.shape, 0), 16)
    top = (row == 0) | (row == RD + 2)
    bottom = (row == RD + 1) | (row == 15)
    zero = (top & first) | (bottom & last)
    return jnp.where(zero, 0.0, sides)


def halo_row(halo, rim, edge, at_rim, flip):
    side = halo.shape[1]
    across = dot(rim_matrix(side, flip), rim[...])
    return jnp.where(at_rim, across, halo[edge].astype(F32))


def back_weights(w_ref, out_ref):
    for k in range(3):
        for m in range(3):
            tap = w_ref[8 - (3 * k + m)].astype(F32)
            out_ref[k, m * C : (m + 1) * C, :] = tap.T.astype(BF)


def halo_weights(wt_ref, flip_top, flip_bottom):
    def turned(k):
        return jnp.concatenate(
            [wt_ref[k, (2 - m) * C : (3 - m) * C, :] for m in range(3)], axis=0
        )

    top = jnp.where(flip_top, turned(2), wt_ref[0])
    bottom = jnp.where(flip_bottom, turned(0), wt_ref[2])
    return top, bottom


def rows_of(ref, start, count):
    _, side, width = ref.shape
    return ref[pl.ds(start, count)].reshape(count * side, width)


def first_kernel(
    feat, cot, wf, wc, nb, ed, hf, hc, r2f, r2c, sides, gco, total, wtf, wtc, *scratch
):
    own_a, own_b, buf_a, buf_b, sa, ra, sb, rb = scratch[:8]
    halo = Halo(feat, gco, (hf, hc, r2f, r2c, sides), scratch[8:], (nb, ed))
    barrier_signal(True)

    matrix = pool_matrix()
    own_a[...] = jnp.zeros_like(own_a)

    @pl.loop(0, RD // 2)
    def _(i):
        gco[i] = dot(matrix, rows_of(cot, 2 * i, 2)).astype(BF)
        values = rows_of(feat, 2 * i, 2).astype(F32)
        own_a[0:1, :] += jnp.sum(values, axis=0, keepdims=True)
        own_a[1:2, :] += jnp.sum(values * values, axis=0, keepdims=True)

    barrier_wait(True)
    sum_start(line_a, own_a, buf_a, sa, ra)
    halo.start()
    back_weights(wc, wtc)
    own_b[...] = sum_finish(line_a, own_a, buf_a, sa, ra)
    sum_start(line_b, own_b, buf_b, sb, rb)
    halo.middle()
    back_weights(wf, wtf)
    total[...] = sum_finish(line_b, own_b, buf_b, sb, rb)
    halo.finish()


def forward_kernel(
    feat, cot, wf, wtc, gain, ed, hf, hc, r2f, r2c, sides, gco, total,
    x3, fine, coarse_in, grad_fine, u3, gci
):
    first, last, flip_top, flip_bottom = edge_flags(ed)
    mean, inverse = norm_vectors(total[...])
    scale = gain[...]

    def hidden(raw):
        act = (raw - mean) * inverse * scale
        return act * sigmoid(act)

    edge = sides[...].astype(F32)
    edge_hidden = masked_sides(hidden(edge), first, last)
    edge_coarse = masked_sides(edge, first, last)

    def put(i, raw):
        store_shifted(
            x3, i, hidden(raw).astype(BF).astype(F32), edge_hidden[i : i + 1],
            edge_hidden[16 + i : 17 + i],
        )

    put(0, halo_row(hf, r2f, 0, first, flip_top))
    for r in range(RD):
        put(r + 1, feat[r].astype(F32))
    put(RD + 1, halo_row(hf, r2f, 1, last, flip_bottom))

    half = RD // 2
    for i in range(half + 2):
        if i == 0:
            row = halo_row(hc, r2c, 0, first, flip_top)
        elif i == half + 1:
            row = halo_row(hc, r2c, 1, last, flip_bottom)
        else:
            row = gco[i - 1].astype(F32)
        j = RD + 2 + i
        store_shifted(u3, i, row, edge_coarse[j : j + 1], edge_coarse[16 + j : 17 + j])
    top, bottom = halo_weights(wtc, flip_top, flip_bottom)
    gci[...] = dot(rows_of(u3, 1, half), wtc[1]).reshape(half, CS, C)
    gci[1:half] += dot(rows_of(u3, 1, half - 1), wtc[0]).reshape(half - 1, CS, C)
    gci[0 : half - 1] += dot(rows_of(u3, 2, half - 1), wtc[2]).reshape(half - 1, CS, C)
    gci[0] += dot(u3[0], top)
    gci[half - 1] += dot(u3[half + 1], bottom)

    pool, widen = pool_matrix(), spread_matrix()

    @pl.loop(0, half)
    def _(i):
        total = dot(rows_of(x3, 2 * i, 2), wf[0])
        total += dot(rows_of(x3, 2 * i + 1, 2), wf[1])
        total += dot(rows_of(x3, 2 * i + 2, 2), wf[2])
        out = total.astype(BF)
        fine[pl.ds(2 * i, 2)] = out.reshape(2, FS, C)
        pooled = 0.25 * dot(pool, out)
        gate = sigmoid(pooled)
        coarse_in[i] = (pooled * gate).astype(BF)
        slope = gate * (1.0 + pooled * (1.0 - gate))
        wide = spread(widen, gci[i] * slope * 0.25)
        for r in range(2):
            grad_fine[2 * i + r] = (cot[2 * i + r].astype(F32) + wide).astype(BF)


def second_kernel(
    grad_fine, coarse_in, nb, ed, hf, hc, r2f, r2c, sides, *scratch
):
    halo = Halo(grad_fine, coarse_in, (hf, hc, r2f, r2c, sides), scratch, (nb, ed))
    barrier_signal(True)
    barrier_wait(True)
    halo.start()
    halo.middle()
    halo.finish()


def backward_kernel(
    feat, x3, fine, coarse_in, grad_fine, gco, wc, wtf, gain, total, ed,
    hf, hc, r2f, r2c, sides, output, ga, sums, shares, c3, u3, gt, gct
):
    first, last, flip_top, flip_bottom = edge_flags(ed)
    mean, inverse = norm_vectors(total[...])
    scale = gain[...]
    half = RD // 2
    edge = masked_sides(sides[...].astype(F32), first, last)

    for i in range(half + 2):
        if i == 0:
            row = halo_row(hc, r2c, 0, first, flip_top)
        elif i == half + 1:
            row = halo_row(hc, r2c, 1, last, flip_bottom)
        else:
            row = coarse_in[i - 1].astype(F32)
        j = RD + 2 + i
        store_shifted(c3, i, row, edge[j : j + 1], edge[16 + j : 17 + j])

    for i in range(RD + 2):
        if i == 0:
            row = halo_row(hf, r2f, 0, first, flip_top)
        elif i == RD + 1:
            row = halo_row(hf, r2f, 1, last, flip_bottom)
        else:
            row = grad_fine[i - 1].astype(F32)
        store_shifted(u3, i, row, edge[i : i + 1], edge[16 + i : 17 + i])

    for r in range(RD):
        gt[:, r * FS : (r + 1) * FS] = grad_fine[r].astype(F32).T.astype(BF)
    for r in range(half):
        gct[:, r * CS : (r + 1) * CS] = gco[r].astype(F32).T.astype(BF)
    for k in range(3):
        fine_part = dot(gt[...], rows_of(x3, k, RD))
        coarse_part = dot(gct[...], rows_of(c3, k, half))
        for m in range(3):
            tap = 3 * k + m
            pair = [
                part[:, m * C : (m + 1) * C].T.reshape(NT, 8, C)
                for part in (fine_part, coarse_part)
            ]
            shares[:, 16 * tap : 16 * tap + 16, :] = jnp.concatenate(pair, axis=1).astype(BF)

    widen = spread_matrix()

    @pl.loop(0, half)
    def _(i):
        out = dot(c3[i], wc[0]) + dot(c3[i + 1], wc[1]) + dot(c3[i + 2], wc[2])
        wide = spread(widen, out)
        for r in range(2):
            output[2 * i + r] = (fine[2 * i + r].astype(F32) + wide).astype(BF)

    top, bottom = halo_weights(wtf, flip_top, flip_bottom)
    ga[1 : RD - 1] = jnp.zeros((RD - 2, FS, C), F32)
    ga[0] = dot(u3[0], top)
    ga[RD - 1] = dot(u3[RD + 1], bottom)
    u3[0] = jnp.zeros_like(u3[0])
    u3[RD + 1] = jnp.zeros_like(u3[0])
    sums[...] = jnp.zeros_like(sums)

    @pl.loop(0, half)
    def _(i):
        grad = dot(rows_of(u3, 2 * i, 2), wtf[0])
        grad += dot(rows_of(u3, 2 * i + 1, 2), wtf[1])
        grad += dot(rows_of(u3, 2 * i + 2, 2), wtf[2])
        grad += rows_of(ga, 2 * i, 2)
        normed = (rows_of(feat, 2 * i, 2).astype(F32) - mean) * inverse
        act = normed * scale
        gate = sigmoid(act)
        grad = grad * (gate * (1.0 + act * (1.0 - gate)))
        ga[pl.ds(2 * i, 2)] = grad.reshape(2, FS, C)
        sums[0:1, :] += jnp.sum(grad * normed, axis=0, keepdims=True)
        sums[1:2, :] += jnp.sum(grad, axis=0, keepdims=True)


UNITS = 144


def reduce_kernel(
    shares, sums, grads, total, own_a, own_b, buf_a, buf_b, sa, ra, sb, rb,
    r0, part, r1, block, r2, s0, q0, s1, q1, s2, q2
):
    face, tile = place()
    core, chip = lax.rem(tile, 2), lax.div(tile, 2)
    sibling = tile + 1 - 2 * core
    barrier = pltpu.get_barrier_semaphore()
    barrier_signal(False)

    far = lax.rem(tile + NZ, NT)
    far_base = far - lax.rem(far, NZ)

    @pl.loop(0, NZ // 2)
    def _(z):
        signal(barrier, face, far_base + 2 * z + core)

    own_a[...] = sums[...]
    barrier_wait(False, NZ // 2)

    def swap(q):
        return remote(
            shares.at[pl.ds(4 * q, 4), 1 - core],
            r0.at[pl.ds(4 * q, 4)],
            s0.at[q],
            q0.at[q],
            face,
            sibling,
        )

    for q in range(4):
        swap(q).start()
    sum_start(line_a, own_a, buf_a, sa, ra)

    def scatter(other, slot):
        return remote(
            part.at[other], r1.at[slot], s1.at[other], q1.at[slot], face, 2 * other + core
        )

    for q in range(4):
        swap(q).wait_recv()

        @pl.loop(4 * q, 4 * q + 4)
        def _(j):
            both = shares[j, core].astype(F32) + r0[j].astype(F32)
            part[j] = both.astype(BF)

            @pl.when(j != chip)
            def _():
                scatter(j, chip).start()

    own_b[...] = sum_finish(line_a, own_a, buf_a, sa, ra)
    sum_start(line_b, own_b, buf_b, sb, rb)
    r1[chip] = part[chip]

    @pl.loop(1, 16)
    def _(step):
        other = lax.rem(chip + step, 16)
        scatter(other, other).wait_recv()

    acc = r1[0].astype(F32)
    for j in range(1, 16):
        acc = acc + r1[j].astype(F32)
    block[...] = acc.astype(BF)

    def share(other, slot):
        return remote(block, r2.at[slot], s2.at[other], q2.at[slot], other, tile)

    @pl.loop(1, NF)
    def _(step):
        share(lax.rem(face + step, NF), face).start()

    r2[face] = block[...]
    total[...] = sum_finish(line_b, own_b, buf_b, sb, rb)

    @pl.loop(1, NF)
    def _(step):
        other = lax.rem(face + step, NF)
        share(other, other).wait_recv()

    acc = r2[0].astype(F32)
    for j in range(1, NF):
        acc = acc + r2[j].astype(F32)
    grads[...] = acc * (1.0 / CELLS)

    for q in range(4):
        swap(q).wait_send()

    @pl.loop(1, 16)
    def _(step):
        other = lax.rem(chip + step, 16)
        scatter(other, other).wait_send()

    @pl.loop(1, NF)
    def _(step):
        other = lax.rem(face + step, NF)
        share(other, other).wait_send()


def last_kernel(feat, ga, gain, total, sums, grad_features, grad_gain):
    mean, inverse = norm_vectors(total[...])
    scale = gain[...]
    slope_sum, shift_sum = sums[0:1], sums[1:2]
    grad_gain[...] = slope_sum / CELLS
    row = iota((8, C), 0)
    weighted = sums[...] * scale
    grouped = group_sum(weighted) / (CELLS * GROUP)
    group_slope, group_shift = grouped[0:1], grouped[1:2]
    normed = (feat[0].astype(F32) - mean) * inverse
    grad_features[0] = inverse * (scale * ga[0] - group_shift - normed * group_slope)


def shape(dims, dtype):
    return jax.ShapeDtypeStruct(dims, dtype)


def call(kernel, ins, outs, scratch, collective=None, **more):
    params = {"vmem_limit_bytes": VMEM_LIMIT}
    if collective is not None:
        params.update(collective_id=collective, has_side_effects=True)
    return pl.pallas_call(
        kernel,
        in_specs=ins,
        out_specs=[VM] * len(outs),
        out_shape=outs,
        scratch_shapes=scratch,
        compiler_params=pltpu.CompilerParams(**params),
        **more,
    )


def on_device(features, cotangent, w_fine, w_coarse, gain, neighbors, neighbor_edges):
    feat, cot = features[0], cotangent[0]
    half = RD // 2
    gain_row = gain[None]
    w_fine_rows = w_fine.reshape(3, 3 * C, C)
    w_coarse_rows = w_coarse.reshape(3, 3 * C, C)

    hf, hc, r2f, r2c, sides, gco, total, wtf, wtc = call(
        first_kernel,
        [VM] * 4 + [SM] * 2,
        HALO_OUTS
        + [
            shape((half, CS, C), BF),
            shape((8, C), F32),
            shape((3, 3 * C, C), BF),
            shape((3, 3 * C, C), BF),
        ],
        SUM_SCRATCH + HALO_SCRATCH,
        collective=1,
    )(feat, cot, w_fine, w_coarse, neighbors, neighbor_edges)

    x3, fine, coarse_in, grad_fine = call(
        forward_kernel,
        [VM] * 5 + [SM] + [VM] * 7,
        [
            shape((RD + 2, FS, 3 * C), BF),
            shape((RD, FS, C), BF),
            shape((half, CS, C), BF),
            shape((RD, FS, C), BF),
        ],
        [pltpu.VMEM((half + 2, CS, 3 * C), BF), pltpu.VMEM((half, CS, C), F32)],
    )(
        feat, cot, w_fine_rows, wtc, gain_row, neighbor_edges,
        hf, hc, r2f, r2c, sides, gco, total,
    )

    hf2, hc2, r2f2, r2c2, sides2 = call(
        second_kernel, [VM] * 2 + [SM] * 2, HALO_OUTS, HALO_SCRATCH, collective=2
    )(grad_fine, coarse_in, neighbors, neighbor_edges)

    output, ga, sums, shares = call(
        backward_kernel,
        [VM] * 10 + [SM] + [VM] * 5,
        [
            shape((RD, FS, C), BF),
            shape((RD, FS, C), F32),
            shape((8, C), F32),
            shape((NT, UNITS, C), BF),
        ],
        [
            pltpu.VMEM((half + 2, CS, 3 * C), BF),
            pltpu.VMEM((RD + 2, FS, 3 * C), BF),
            pltpu.VMEM((C, RD * FS), BF),
            pltpu.VMEM((C, half * CS), BF),
        ],
    )(
        feat, x3, fine, coarse_in, grad_fine, gco, w_coarse_rows, wtf, gain_row, total,
        neighbor_edges, hf2, hc2, r2f2, r2c2, sides2,
    )

    grads, all_sums = call(
        reduce_kernel,
        [VM] * 2,
        [shape((UNITS, C), F32), shape((8, C), F32)],
        SUM_SCRATCH
        + [
            pltpu.VMEM((16, UNITS, C), BF),
            pltpu.VMEM((16, UNITS, C), BF),
            pltpu.VMEM((16, UNITS, C), BF),
            pltpu.VMEM((UNITS, C), BF),
            pltpu.VMEM((NF, UNITS, C), BF),
            DMA((4,)),
            DMA((4,)),
            DMA((16,)),
            DMA((16,)),
            DMA((NF,)),
            DMA((NF,)),
        ],
        collective=3,
    )(shares.reshape(16, 2, UNITS, C), sums)

    row = pl.BlockSpec((1, FS, C), lambda i: (i, 0, 0))
    vector = pl.BlockSpec((1, C), lambda i: (0, 0))
    block = pl.BlockSpec((8, C), lambda i: (0, 0))
    grad_features, grad_gain = pl.pallas_call(
        last_kernel,
        grid=(RD,),
        in_specs=[row, row, vector, block, block],
        out_specs=[row, vector],
        out_shape=[shape((RD, FS, C), F32), shape((1, C), F32)],
        compiler_params=pltpu.CompilerParams(vmem_limit_bytes=VMEM_LIMIT),
    )(feat, ga, gain_row, total, all_sums)

    grads = grads.reshape(9, 2, 8, C)
    return (output[None], grad_features[None], grads[:, 0], grads[:, 1], grad_gain[0])


def solution(mesh):
    return jax.shard_map(
        on_device,
        mesh=mesh,
        in_specs=(
            P("face", "tile", None, None),
            P("face", "tile", None, None),
            P(),
            P(),
            P(),
            P(),
            P(),
        ),
        out_specs=(
            P("face", "tile", None, None),
            P("face", "tile", None, None),
            P(None, "tile", None),
            P(None, "tile", None),
            P(),
        ),
        check_vma=False,
    )
```

```python
import jax
import jax.numpy as jnp
from jax import lax
from jax.experimental import pallas as pl
from jax.experimental.pallas import tpu as pltpu
from jax.sharding import PartitionSpec as P

BF = jnp.bfloat16
F32 = jnp.float32
MESH = pl.DeviceIdType.MESH
NF = 8
NT = 32
NZ = 16
RD = 8
FS = 256
CS = 128
C = 256
GROUP = 8
SLOTS = 16
CELLS = NF * FS * FS
VMEM_LIMIT = 60 * 1024 * 1024

VM = pl.BlockSpec(memory_space=pltpu.VMEM)
SM = pl.BlockSpec(memory_space=pltpu.SMEM)
DMA = pltpu.SemaphoreType.DMA


def remote(src, dst, send, recv, face, tile):
    return pltpu.make_async_remote_copy(
        src_ref=src,
        dst_ref=dst,
        send_sem=send,
        recv_sem=recv,
        device_id=(face, tile),
        device_id_type=MESH,
    )


def place():
    return lax.axis_index("face"), lax.axis_index("tile")


def is_rim(tile):
    return (tile == 0) | (tile == NT - 1)


def slot_device(slot):
    return lax.div(slot, 2), (NT - 1) * lax.rem(slot, 2)


def my_slot(face, tile):
    return 2 * face + jnp.where(tile == NT - 1, 1, 0)


def multiple(value, of):
    return pl.multiple_of(value * of, of)


def signal(barrier, face, tile):
    pl.semaphore_signal(barrier, inc=1, device_id=(face, tile), device_id_type=MESH)


def line_a(face, tile, step):
    mine = lax.rem(tile, NZ)
    other = lax.rem(mine + step, NZ)
    return mine, other, (face, tile - mine + other)


def line_b(face, tile, step):
    mine = face * 2 + lax.div(tile, NZ)
    other = lax.rem(mine + step, 2 * NF)
    return mine, other, (lax.div(other, 2), lax.rem(other, 2) * NZ + lax.rem(tile, NZ))


def barrier_signal():
    face, tile = place()
    barrier = pltpu.get_barrier_semaphore()
    across = lax.rem(tile + NZ, NT)
    across = across - lax.rem(across, NZ) + lax.rem(tile, 2)

    @pl.loop(1, NZ)
    def _(step):
        for line in (line_a, line_b):
            _, _, device = line(face, tile, step)
            signal(barrier, *device)

    @pl.loop(0, NZ // 2)
    def _(z):
        signal(barrier, face, across + 2 * z)

    signal(barrier, face, lax.rem(tile + 1, NT))
    signal(barrier, face, lax.rem(tile + NT - 1, NT))

    @pl.when(is_rim(tile))
    def _():
        mine = my_slot(face, tile)

        @pl.loop(1, SLOTS)
        def _(step):
            signal(barrier, *slot_device(lax.rem(mine + step, SLOTS)))


def barrier_wait():
    _, tile = place()
    barrier = pltpu.get_barrier_semaphore()
    count = 2 * (NZ - 1) + NZ // 2 + 2

    @pl.when(is_rim(tile))
    def _():
        pl.semaphore_wait(barrier, count + SLOTS - 1)

    @pl.when(~is_rim(tile))
    def _():
        pl.semaphore_wait(barrier, count)


def sum_start(line, own, buf, send, recv):
    face, tile = place()

    @pl.loop(1, NZ)
    def _(step):
        mine, other, device = line(face, tile, step)
        remote(own, buf.at[mine], send.at[other], recv.at[mine], *device).start()

    mine, _, _ = line(face, tile, 0)
    buf[mine] = own[...]


def sum_finish(line, own, buf, send, recv):
    face, tile = place()

    @pl.loop(1, NZ)
    def _(step):
        _, other, device = line(face, tile, step)
        copy = remote(own, buf.at[other], send.at[other], recv.at[other], *device)
        copy.wait_recv()
        copy.wait_send()

    total = buf[0]
    for i in range(1, NZ):
        total = total + buf[i]
    return total


SUM_SCRATCH = [
    pltpu.VMEM((8, C), F32),
    pltpu.VMEM((8, C), F32),
    pltpu.VMEM((NZ, 8, C), F32),
    pltpu.VMEM((NZ, 8, C), F32),
    DMA((NZ,)),
    DMA((NZ,)),
    DMA((NZ,)),
    DMA((NZ,)),
]


HALO_SCRATCH = [
    pltpu.VMEM((2, FS, C), BF),
    pltpu.VMEM((2, CS, C), BF),
    pltpu.VMEM((FS, C), BF),
    pltpu.VMEM((CS, C), BF),
    pltpu.VMEM((32, C), BF),
    pltpu.VMEM((SLOTS, 16, C), BF),
    pltpu.VMEM((SLOTS, 16, 128), BF),
    pltpu.VMEM((SLOTS, 16, C), BF),
    pltpu.VMEM((SLOTS, 16, 128), BF),
    pltpu.VMEM((32, C), F32),
    pltpu.VMEM((32, C), BF),
    pltpu.VMEM((NF, 32, C), BF),
    DMA((4,)),
    DMA((4,)),
    DMA((SLOTS,)),
    DMA((SLOTS,)),
    DMA((SLOTS,)),
    DMA((SLOTS,)),
    DMA((SLOTS,)),
    DMA((SLOTS,)),
    DMA((SLOTS,)),
    DMA((SLOTS,)),
    DMA((NF,)),
    DMA((NF,)),
    DMA((4,)),
]


class Halo:
    def __init__(self, fine, coarse, scratch, tables):
        self.fine, self.coarse = fine, coarse
        (
            self.hf,
            self.hc,
            self.r2f,
            self.r2c,
            self.sides,
            self.r1f,
            self.r1c,
            self.stf,
            self.stc,
            self.rows,
            self.srec,
            self.sall,
            self.hs,
            self.hr,
            self.f1s,
            self.f1r,
            self.c1s,
            self.c1r,
            self.f2s,
            self.f2r,
            self.c2s,
            self.c2r,
            self.ss,
            self.sr,
            self.own,
        ) = scratch
        self.nb, self.ed = tables
        self.face, self.tile = place()

    def rows_copies(self):
        up = lax.rem(self.tile + 1, NT)
        down = lax.rem(self.tile + NT - 1, NT)
        plan = (
            (self.fine.at[RD - 1], self.hf.at[0], up),
            (self.fine.at[0], self.hf.at[1], down),
            (self.coarse.at[RD // 2 - 1], self.hc.at[0], up),
            (self.coarse.at[0], self.hc.at[1], down),
        )
        return [
            remote(src, dst, self.hs.at[i], self.hr.at[i], self.face, to)
            for i, (src, dst, to) in enumerate(plan)
        ]

    def chunk(self, slot):
        fine_row = jnp.where(self.tile == 0, 0, RD - 1)
        coarse_row = jnp.where(self.tile == 0, 0, RD // 2 - 1)
        return (
            self.fine.at[fine_row, pl.ds(multiple(slot, 16), 16), :],
            self.coarse.at[
                coarse_row,
                pl.ds(multiple(lax.div(slot, 2), 16), 16),
                pl.ds(multiple(lax.rem(slot, 2), 128), 128),
            ],
        )

    def landing(self, slot):
        return (
            self.r2f.at[pl.ds(multiple(slot, 16), 16), :],
            self.r2c.at[
                pl.ds(multiple(lax.div(slot, 2), 16), 16),
                pl.ds(multiple(lax.rem(slot, 2), 128), 128),
            ],
        )

    def hop1(self, step):
        mine = my_slot(self.face, self.tile)
        other = lax.rem(mine + step, SLOTS)
        device = slot_device(other)
        src_f, src_c = self.chunk(other)
        return (
            remote(src_f, self.r1f.at[mine], self.f1s.at[other], self.f1r.at[mine], *device),
            remote(src_c, self.r1c.at[mine], self.c1s.at[other], self.c1r.at[mine], *device),
        )

    def hop1_wait(self, step):
        mine = my_slot(self.face, self.tile)
        other = lax.rem(mine + step, SLOTS)
        device = slot_device(other)
        src_f, src_c = self.chunk(other)
        for copy in (
            remote(src_f, self.r1f.at[other], self.f1s.at[other], self.f1r.at[other], *device),
            remote(src_c, self.r1c.at[other], self.c1s.at[other], self.c1r.at[other], *device),
        ):
            copy.wait_recv()
            copy.wait_send()

    def hop2(self, step):
        mine = my_slot(self.face, self.tile)
        other = lax.rem(mine + step, SLOTS)
        device = slot_device(other)
        dst_f, dst_c = self.landing(mine)
        return (
            remote(self.stf.at[other], dst_f, self.f2s.at[other], self.f2r.at[mine], *device),
            remote(self.stc.at[other], dst_c, self.c2s.at[other], self.c2r.at[mine], *device),
        )

    def hop2_wait(self, step):
        mine = my_slot(self.face, self.tile)
        other = lax.rem(mine + step, SLOTS)
        device = slot_device(other)
        dst_f, dst_c = self.landing(other)
        for copy in (
            remote(self.stf.at[other], dst_f, self.f2s.at[other], self.f2r.at[other], *device),
            remote(self.stc.at[other], dst_c, self.c2s.at[other], self.c2r.at[other], *device),
        ):
            copy.wait_recv()
            copy.wait_send()

    def start(self):
        for copy in self.rows_copies():
            copy.start()

        @pl.when(is_rim(self.tile))
        def _():
            @pl.loop(1, SLOTS)
            def _(step):
                for copy in self.hop1(step):
                    copy.start()

            mine = my_slot(self.face, self.tile)
            src_f, src_c = self.chunk(mine)
            keep = (
                pltpu.make_async_copy(src_f, self.r1f.at[mine], self.own.at[0]),
                pltpu.make_async_copy(src_c, self.r1c.at[mine], self.own.at[1]),
            )
            for copy in keep:
                copy.start()
            for copy in keep:
                copy.wait()

    def middle(self):
        for copy in self.rows_copies():
            copy.wait_recv()
            copy.wait_send()
        fine_rows = [self.hf.at[0]] + [self.fine.at[r] for r in range(RD)] + [self.hf.at[1]]
        coarse_rows = [self.hc.at[0]] + [self.coarse.at[r] for r in range(RD // 2)]
        coarse_rows += [self.hc.at[1]]
        for i, row in enumerate(fine_rows + coarse_rows):
            side = row.shape[0]
            self.rows[i : i + 1, :] = row[0:16, :].astype(F32)[0:1]
            self.rows[16 + i : 17 + i, :] = row[side - 16 : side, :].astype(F32)[15:16]
        self.srec[...] = self.rows[...].astype(BF)

        @pl.loop(1, NF)
        def _(step):
            other = lax.rem(self.face + step, NF)
            remote(
                self.srec,
                self.sall.at[self.face],
                self.ss.at[other],
                self.sr.at[self.face],
                other,
                self.tile,
            ).start()

        self.sall[self.face] = self.srec[...]

        @pl.when(is_rim(self.tile))
        def _():
            mine = my_slot(self.face, self.tile)

            @pl.loop(1, SLOTS)
            def _(step):
                self.hop1_wait(step)

            @pl.loop(0, SLOTS)
            def _(slot):
                face, edge = lax.div(slot, 2), 2 * lax.rem(slot, 2)
                source = 2 * self.nb[face, edge] + lax.div(self.ed[face, edge], 2)
                self.stf[slot] = self.r1f[source]
                self.stc[slot] = self.r1c[source]

            @pl.loop(1, SLOTS)
            def _(step):
                for copy in self.hop2(step):
                    copy.start()

            dst_f, dst_c = self.landing(mine)
            keep = (
                pltpu.make_async_copy(self.stf.at[mine], dst_f, self.own.at[2]),
                pltpu.make_async_copy(self.stc.at[mine], dst_c, self.own.at[3]),
            )
            for copy in keep:
                copy.start()
            for copy in keep:
                copy.wait()

    def finish(self, flips):
        @pl.loop(1, NF)
        def _(step):
            other = lax.rem(self.face + step, NF)
            copy = remote(
                self.srec,
                self.sall.at[other],
                self.ss.at[other],
                self.sr.at[other],
                other,
                self.tile,
            )
            copy.wait_recv()
            copy.wait_send()

        left_face, right_face = self.nb[self.face, 3], self.nb[self.face, 1]
        self.sides[0:16, :] = self.sall[left_face, 16:32, :]
        self.sides[16:32, :] = self.sall[right_face, 0:16, :]

        @pl.when(is_rim(self.tile))
        def _():
            @pl.loop(1, SLOTS)
            def _(step):
                self.hop2_wait(step)

            flip_top, flip_bottom = flips
            flip = jnp.where(self.tile == 0, flip_top, flip_bottom)
            edge = jnp.where(self.tile == 0, 0, 1)
            self.hf[edge] = dot(rim_matrix(FS, flip), self.r2f[...]).astype(BF)
            self.hc[edge] = dot(rim_matrix(CS, flip), self.r2c[...]).astype(BF)


def iota(shape, dim):
    return lax.broadcasted_iota(jnp.int32, shape, dim)


def dot(a, b):
    return jnp.dot(a, b, preferred_element_type=F32)


def sigmoid(values):
    return 0.5 * jnp.tanh(0.5 * values) + 0.5


def pool_matrix():
    row, col = iota((CS, 2 * FS), 0), iota((CS, 2 * FS), 1)
    return jnp.where(lax.div(lax.rem(col, FS), 2) == row, 1.0, 0.0).astype(BF)


def spread_matrix():
    row, col = iota((FS, 2 * CS), 0), iota((FS, 2 * CS), 1)
    return jnp.where(lax.rem(col, CS) == lax.div(row, 2), 1.0, 0.0).astype(BF)


def spread(matrix, values):
    high = values.astype(BF)
    low = (values - high.astype(F32)).astype(BF)
    return dot(matrix, jnp.concatenate([high, low], axis=0))


def rim_matrix(side, flip):
    row, col = iota((side, side), 0), iota((side, side), 1)
    source = jnp.where(flip, side - 1 - row, row)
    return jnp.where(col == source, 1.0, 0.0).astype(BF)


def store_shifted(ref, row, values, left, right):
    n = values.shape[0]
    position = iota(values.shape, 0)
    before = jnp.where(position == 0, left, pltpu.roll(values, 1, 0))
    after = jnp.where(position == n - 1, right, pltpu.roll(values, n - 1, 0))
    ref[row, :, 0:C] = before.astype(BF)
    ref[row, :, C : 2 * C] = values.astype(BF)
    ref[row, :, 2 * C : 3 * C] = after.astype(BF)


def group_sum(values):
    lane = iota(values.shape, 1)
    for width in (1, 2, 4):
        up = pltpu.roll(values, width, 1)
        down = pltpu.roll(values, C - width, 1)
        values = values + jnp.where(lax.rem(lax.div(lane, width), 2) == 0, down, up)
    return values


def norm_vectors(total):
    grouped = group_sum(total) / (CELLS * GROUP)
    mean, second = grouped[0:1], grouped[1:2]
    return mean, lax.rsqrt(second - mean * mean + 1e-05)


def edge_flags(ed_ref):
    face, tile = place()
    first, last = tile == 0, tile == NT - 1
    flip_top = first & (ed_ref[face, 0] != 2)
    flip_bottom = last & (ed_ref[face, 2] != 0)
    return first, last, flip_top, flip_bottom


def masked_sides(sides, first, last):
    row = lax.rem(iota(sides.shape, 0), 16)
    top = (row == 0) | (row == RD + 2)
    bottom = (row == RD + 1) | (row == 15)
    zero = (top & first) | (bottom & last)
    return jnp.where(zero, 0.0, sides)


def back_weights(w_ref, out_ref):
    for k in range(3):
        for m in range(3):
            tap = w_ref[8 - (3 * k + m)].astype(F32)
            out_ref[k, m * C : (m + 1) * C, :] = tap.T.astype(BF)


def halo_weights(wt_ref, flip_top, flip_bottom):
    def turned(k):
        return jnp.concatenate(
            [wt_ref[k, (2 - m) * C : (3 - m) * C, :] for m in range(3)], axis=0
        )

    top = jnp.where(flip_top, turned(2), wt_ref[0])
    bottom = jnp.where(flip_bottom, turned(0), wt_ref[2])
    return top, bottom


def rows_of(ref, start, count):
    _, side, width = ref.shape
    return ref[pl.ds(start, count)].reshape(count * side, width)


def taps_of(ref, k):
    return ref[3 * k : 3 * k + 3].reshape(3 * C, C)


SHARE = 144
NC = 16


def put_share(shares, tap, product):
    turned = product.T.reshape(NC, 2, 8, C)
    halves = [turned[..., :128], turned[..., 128:]]
    shares[:, :, 16 * tap : 16 * tap + 16, :] = jnp.concatenate(halves, axis=2).astype(BF)


def put_grads(out, total):
    total = (total * (1.0 / CELLS)).reshape(9, 2, 8, 128)
    out[:, :, 0:128] = total[:, 0]
    out[:, :, 128:256] = total[:, 1]


def tree(parts):
    parts = [part.astype(F32) for part in parts]
    while len(parts) > 1:
        parts = [sum(parts[i : i + 2]) for i in range(0, len(parts), 2)]
    return parts[0]


class Swap:
    def __init__(self, shares, scratch):
        self.shares = shares
        self.got, self.part, self.send, self.recv = scratch
        self.face, self.tile = place()
        self.core = lax.rem(self.tile, 2)

    def copy(self, q):
        return remote(
            self.shares.at[pl.ds(4 * q, 4), 1 - self.core],
            self.got.at[pl.ds(4 * q, 4)],
            self.send.at[q],
            self.recv.at[q],
            self.face,
            self.tile + 1 - 2 * self.core,
        )

    def start(self):
        for q in range(4):
            self.copy(q).start()

    def take(self, q, then):
        self.copy(q).wait_recv()

        @pl.loop(4 * q, 4 * q + 4)
        def _(j):
            both = self.shares[j, self.core].astype(F32) + self.got[j].astype(F32)
            self.part[j] = both.astype(BF)
            then(j)

    def finish(self):
        for q in range(4):
            self.copy(q).wait_send()


SWAP_SCRATCH = [
    pltpu.VMEM((NC, SHARE, 128), BF),
    pltpu.VMEM((NC, SHARE, 128), BF),
    DMA((4,)),
    DMA((4,)),
]


class ChipsFirst:
    def __init__(self, part, scratch):
        self.part = part
        self.r1, self.block, self.r2, self.s1, self.q1, self.s2, self.q2 = scratch
        self.face, self.tile = place()
        self.core, self.chip = lax.rem(self.tile, 2), lax.div(self.tile, 2)

    def scatter(self, other, slot):
        return remote(
            self.part.at[other],
            self.r1.at[slot],
            self.s1.at[other],
            self.q1.at[slot],
            self.face,
            2 * other + self.core,
        )

    def send(self, j):
        @pl.when(j != self.chip)
        def _():
            self.scatter(j, self.chip).start()

    def share(self, other, slot):
        return remote(
            self.block, self.r2.at[slot], self.s2.at[other], self.q2.at[slot], other, self.tile
        )

    def middle(self):
        self.r1[self.chip] = self.part[self.chip]

        @pl.loop(1, NC)
        def _(step):
            other = lax.rem(self.chip + step, NC)
            self.scatter(other, other).wait_recv()

        self.block[...] = tree([self.r1[j] for j in range(NC)]).astype(BF)

        @pl.loop(1, NF)
        def _(step):
            self.share(lax.rem(self.face + step, NF), self.face).start()

        self.r2[self.face] = self.block[...]

    def finish(self, out):
        @pl.loop(1, NF)
        def _(step):
            other = lax.rem(self.face + step, NF)
            self.share(other, other).wait_recv()

        put_grads(out, tree([self.r2[j] for j in range(NF)]))

        @pl.loop(1, NC)
        def _(step):
            other = lax.rem(self.chip + step, NC)
            self.scatter(other, other).wait_send()

        @pl.loop(1, NF)
        def _(step):
            other = lax.rem(self.face + step, NF)
            self.share(other, other).wait_send()


CHIPS_SCRATCH = [
    pltpu.VMEM((NC, SHARE, 128), BF),
    pltpu.VMEM((SHARE, 128), BF),
    pltpu.VMEM((NF, SHARE, 128), BF),
    DMA((NC,)),
    DMA((NC,)),
    DMA((NF,)),
    DMA((NF,)),
]


class LineFirst:
    def __init__(self, part, scratch):
        self.part = part
        (
            self.rx,
            self.px,
            self.rz,
            self.block,
            self.rb,
            self.sx,
            self.qx,
            self.sz,
            self.qz,
            self.sb,
            self.qb,
        ) = scratch
        self.face, self.tile = place()
        self.core, self.chip = lax.rem(self.tile, 2), lax.div(self.tile, 2)
        self.x, self.high = lax.div(self.face, 2), lax.rem(self.face, 2)
        self.home = lax.rem(self.chip, 4)
        self.owner = self.home == self.x

    def along(self, other, slot):
        return remote(
            self.part.at[:, other],
            self.rx.at[slot],
            self.sx.at[other],
            self.qx.at[slot],
            2 * other + self.high,
            self.tile,
        )

    def start(self):
        @pl.loop(1, 4)
        def _(step):
            self.along(lax.rem(self.x + step, 4), self.x).start()

    def scatter(self, j, slot):
        return remote(
            self.px.at[j],
            self.rz.at[slot],
            self.sz.at[j],
            self.qz.at[slot],
            self.face,
            2 * (4 * j + self.x) + self.core,
        )

    def middle(self):
        self.rx[self.x] = self.part[:, self.x]

        @pl.loop(1, 4)
        def _(step):
            other = lax.rem(self.x + step, 4)
            self.along(other, other).wait_recv()

        @pl.loop(0, 4)
        def _(j):
            self.px[j] = tree([self.rx[i, j] for i in range(4)]).astype(BF)
            mine = 4 * j + self.x == self.chip

            @pl.when(jnp.logical_not(mine))
            def _():
                self.scatter(j, self.chip).start()

            @pl.when(mine)
            def _():
                self.rz[self.chip] = self.px[j]

    def share(self, other):
        return remote(
            self.block,
            self.rb.at[self.high],
            self.sb.at[other],
            self.qb.at[self.high],
            other,
            self.tile,
        )

    def late(self):
        @pl.when(self.owner)
        def _():
            @pl.loop(1, NC)
            def _(step):
                other = lax.rem(self.chip + step, NC)
                remote(
                    self.px.at[0],
                    self.rz.at[other],
                    self.sz.at[0],
                    self.qz.at[other],
                    self.face,
                    2 * other + self.core,
                ).wait_recv()

            self.block[...] = tree([self.rz[j] for j in range(NC)]).astype(BF)

            @pl.loop(1, NF)
            def _(step):
                self.share(lax.rem(self.face + step, NF)).start()

            self.rb[self.high] = self.block[...]

    def finish(self, out):
        for high in range(2):
            source = 2 * self.home + high

            @pl.when(source != self.face)
            def _():
                remote(
                    self.block,
                    self.rb.at[high],
                    self.sb.at[0],
                    self.qb.at[high],
                    source,
                    self.tile,
                ).wait_recv()

        put_grads(out, tree([self.rb[0], self.rb[1]]))

        @pl.loop(1, 4)
        def _(step):
            other = lax.rem(self.x + step, 4)
            self.along(other, other).wait_send()

        @pl.loop(0, 4)
        def _(j):
            @pl.when(4 * j + self.x != self.chip)
            def _():
                self.scatter(j, self.chip).wait_send()

        @pl.when(self.owner)
        def _():
            @pl.loop(1, NF)
            def _(step):
                self.share(lax.rem(self.face + step, NF)).wait_send()


LINE_SCRATCH = [
    pltpu.VMEM((4, 4, SHARE, 128), BF),
    pltpu.VMEM((4, SHARE, 128), BF),
    pltpu.VMEM((NC, SHARE, 128), BF),
    pltpu.VMEM((SHARE, 128), BF),
    pltpu.VMEM((2, SHARE, 128), BF),
    DMA((4,)),
    DMA((4,)),
    DMA((4,)),
    DMA((NC,)),
    DMA((NF,)),
    DMA((2,)),
]


HALF = RD // 2
N_SUM, N_HALO = len(SUM_SCRATCH), len(HALO_SCRATCH)

WORK_SCRATCH = [
    pltpu.VMEM((HALF, CS, C), BF),
    pltpu.VMEM((3, 3 * C, C), BF),
    pltpu.VMEM((3, 3 * C, C), BF),
    pltpu.VMEM((RD + 2, FS, 3 * C), BF),
    pltpu.VMEM((RD + 2, FS, 3 * C), BF),
    pltpu.VMEM((HALF + 2, CS, 3 * C), BF),
    pltpu.VMEM((HALF + 2, CS, 3 * C), BF),
    pltpu.VMEM((RD, FS, C), BF),
    pltpu.VMEM((HALF, CS, C), BF),
    pltpu.VMEM((RD, FS, C), BF),
    pltpu.VMEM((HALF, CS, C), F32),
    pltpu.VMEM((C, RD * FS), BF),
    pltpu.VMEM((C, HALF * CS), BF),
    pltpu.VMEM((32, C), F32),
    pltpu.VMEM((32, C), F32),
    pltpu.VMEM((NC, 2, SHARE, 128), BF),
    pltpu.VMEM((NC, 2, SHARE, 128), BF),
]


def extended(ref3, field, halo, edge, first, side):
    rows = field.shape[0]

    def put(i, row):
        left, right = edge[pl.ds(first + i, 1), :], edge[pl.ds(first + i + 16, 1), :]
        store_shifted(ref3, i, side(row.astype(F32)), left, right)

    put(0, halo[0])
    put(rows + 1, halo[1])

    @pl.loop(0, rows)
    def _(r):
        put(r + 1, field[r])


def whole_kernel(
    feat, cot, wf_taps, wc_taps, gain, nb, ed,
    output, grad_features, grad_w_fine, grad_w_coarse, grad_gain, *scratch
):
    scratch = list(scratch)

    def take(n):
        got = scratch[:n]
        del scratch[:n]
        return got

    own_a, own_b, buf_a, buf_b, sa, ra, sb, rb = take(N_SUM)
    own_c, own_d, buf_c, buf_d, sc, rc, sd, rd = take(N_SUM)
    halo1_scratch, halo2_scratch = take(N_HALO), take(N_HALO)
    (
        gco, wtf, wtc, x3, u3, c3, v3, fine, coarse_in, grad_fine, gci, gt, gct,
        edge_h, edge_c, shares_f, shares_c,
    ) = take(len(WORK_SCRATCH))
    swap_f = Swap(shares_f, take(len(SWAP_SCRATCH)))
    swap_c = Swap(shares_c, take(len(SWAP_SCRATCH)))
    chips = ChipsFirst(swap_f.part, take(len(CHIPS_SCRATCH)))
    line_scratch = take(len(LINE_SCRATCH))

    halo1 = Halo(feat, gco, halo1_scratch, (nb, ed))
    halo2 = Halo(grad_fine, coarse_in, halo2_scratch, (nb, ed))
    barrier_signal()

    pool, widen = pool_matrix(), spread_matrix()
    own_a[...] = jnp.zeros_like(own_a)
    own_c[...] = jnp.zeros_like(own_c)

    @pl.loop(0, HALF)
    def _(i):
        gco[i] = dot(pool, rows_of(cot, 2 * i, 2)).astype(BF)
        values = rows_of(feat, 2 * i, 2).astype(F32)
        own_a[0:1, :] += jnp.sum(values, axis=0, keepdims=True)
        own_a[1:2, :] += jnp.sum(values * values, axis=0, keepdims=True)

    barrier_wait()
    sum_start(line_a, own_a, buf_a, sa, ra)
    halo1.start()
    back_weights(wc_taps, wtc)
    own_b[...] = sum_finish(line_a, own_a, buf_a, sa, ra)
    sum_start(line_b, own_b, buf_b, sb, rb)
    halo1.middle()
    back_weights(wf_taps, wtf)
    for r in range(HALF):
        gct[:, r * CS : (r + 1) * CS] = gco[r].astype(F32).T.astype(BF)

    first, last, flip_top, flip_bottom = edge_flags(ed)
    halo1.finish((flip_top, flip_bottom))
    edge_c[...] = masked_sides(halo1.sides[...].astype(F32), first, last)

    extended(v3, gco, halo1.hc, edge_c, RD + 2, lambda row: row)
    top, bottom = halo_weights(wtc, flip_top, flip_bottom)
    gci[...] = dot(rows_of(v3, 1, HALF), wtc[1]).reshape(HALF, CS, C)
    gci[1:HALF] += dot(rows_of(v3, 1, HALF - 1), wtc[0]).reshape(HALF - 1, CS, C)
    gci[0 : HALF - 1] += dot(rows_of(v3, 2, HALF - 1), wtc[2]).reshape(HALF - 1, CS, C)
    gci[0] += dot(v3[0], top)
    gci[HALF - 1] += dot(v3[HALF + 1], bottom)

    total = sum_finish(line_b, own_b, buf_b, sb, rb)
    mean, inverse = norm_vectors(total)
    scale = gain[...]

    def hidden(raw):
        act = (raw - mean) * inverse * scale
        return (act * sigmoid(act)).astype(BF).astype(F32)

    edge_h[...] = masked_sides(hidden(halo1.sides[...].astype(F32)), first, last)
    extended(x3, feat, halo1.hf, edge_h, 0, hidden)

    @pl.loop(0, HALF)
    def _(i):
        acc = dot(rows_of(x3, 2 * i, 2), taps_of(wf_taps, 0))
        acc += dot(rows_of(x3, 2 * i + 1, 2), taps_of(wf_taps, 1))
        acc += dot(rows_of(x3, 2 * i + 2, 2), taps_of(wf_taps, 2))
        out = acc.astype(BF)
        fine[pl.ds(2 * i, 2)] = out.reshape(2, FS, C)
        pooled = 0.25 * dot(pool, out)
        gate = sigmoid(pooled)
        coarse_in[i] = (pooled * gate).astype(BF)
        slope = gate * (1.0 + pooled * (1.0 - gate))
        wide = spread(widen, gci[i] * slope * 0.25)
        for r in range(2):
            grad_fine[2 * i + r] = (cot[2 * i + r].astype(F32) + wide).astype(BF)

    halo2.start()

    def fine_gradient(k):
        product = dot(gt[...], rows_of(x3, k, RD))
        for m in range(3):
            put_share(shares_f, 3 * k + m, product[:, m * C : (m + 1) * C])

    for r in range(RD):
        gt[:, r * FS : (r + 1) * FS] = grad_fine[r].astype(F32).T.astype(BF)
    fine_gradient(0)
    halo2.middle()
    fine_gradient(1)
    fine_gradient(2)
    swap_f.start()
    halo2.finish((flip_top, flip_bottom))
    edge_h[...] = masked_sides(halo2.sides[...].astype(F32), first, last)

    extended(c3, coarse_in, halo2.hc, edge_h, RD + 2, lambda row: row)
    for k in range(3):
        product = dot(gct[...], rows_of(c3, k, HALF))
        for m in range(3):
            put_share(shares_c, 3 * k + m, product[:, m * C : (m + 1) * C])
    swap_c.start()
    for q in range(4):
        swap_f.take(q, chips.send)

    extended(u3, grad_fine, halo2.hf, edge_h, 0, lambda row: row)
    top, bottom = halo_weights(wtf, flip_top, flip_bottom)
    ga = grad_features
    ga[1 : RD - 1] = jnp.zeros((RD - 2, FS, C), F32)
    ga[0] = dot(u3[0], top)
    ga[RD - 1] = dot(u3[RD + 1], bottom)
    u3[0] = jnp.zeros((FS, 3 * C), BF)
    u3[RD + 1] = jnp.zeros((FS, 3 * C), BF)

    def back(i):
        grad = dot(rows_of(u3, 2 * i, 2), wtf[0])
        grad += dot(rows_of(u3, 2 * i + 1, 2), wtf[1])
        grad += dot(rows_of(u3, 2 * i + 2, 2), wtf[2])
        grad += rows_of(ga, 2 * i, 2)
        normed = (rows_of(feat, 2 * i, 2).astype(F32) - mean) * inverse
        act = normed * scale
        gate = sigmoid(act)
        grad = grad * (gate * (1.0 + act * (1.0 - gate)))
        ga[pl.ds(2 * i, 2)] = grad.reshape(2, FS, C)
        own_c[0:1, :] += jnp.sum(grad * normed, axis=0, keepdims=True)
        own_c[1:2, :] += jnp.sum(grad, axis=0, keepdims=True)

    pl.loop(0, HALF // 2)(back)
    line = LineFirst(swap_c.part.reshape(4, 4, SHARE, 128), line_scratch)
    for q in range(4):
        swap_c.take(q, lambda j: None)
    line.start()
    pl.loop(HALF // 2, HALF)(back)
    sum_start(line_a, own_c, buf_c, sc, rc)

    @pl.loop(0, HALF)
    def _(i):
        out = dot(c3[i], taps_of(wc_taps, 0)) + dot(c3[i + 1], taps_of(wc_taps, 1)) + dot(c3[i + 2], taps_of(wc_taps, 2))
        wide = spread(widen, out)
        for r in range(2):
            output[2 * i + r] = (fine[2 * i + r].astype(F32) + wide).astype(BF)

    own_d[...] = sum_finish(line_a, own_c, buf_c, sc, rc)
    sum_start(line_b, own_d, buf_d, sd, rd)
    line.middle()
    chips.middle()
    sums = sum_finish(line_b, own_d, buf_d, sd, rd)

    grad_gain[...] = sums[0:1] * (1.0 / CELLS)
    grouped = group_sum(sums * scale) / (CELLS * GROUP)
    group_slope, group_shift = grouped[0:1], grouped[1:2]

    @pl.loop(0, RD)
    def _(r):
        normed = (feat[r].astype(F32) - mean) * inverse
        grad_features[r] = inverse * (scale * ga[r] - group_shift - normed * group_slope)

    line.late()
    chips.finish(grad_w_fine)
    line.finish(grad_w_coarse)
    swap_f.finish()
    swap_c.finish()


def shape(dims, dtype):
    return jax.ShapeDtypeStruct(dims, dtype)


def on_device(features, cotangent, w_fine, w_coarse, gain, neighbors, neighbor_edges):
    outs = [
        shape((RD, FS, C), BF),
        shape((RD, FS, C), F32),
        shape((9, 8, C), F32),
        shape((9, 8, C), F32),
        shape((1, C), F32),
    ]
    output, grad_features, grad_w_fine, grad_w_coarse, grad_gain = pl.pallas_call(
        whole_kernel,
        in_specs=[VM] * 5 + [SM] * 2,
        out_specs=[VM] * len(outs),
        out_shape=outs,
        scratch_shapes=SUM_SCRATCH * 2
        + HALO_SCRATCH * 2
        + WORK_SCRATCH
        + SWAP_SCRATCH * 2
        + CHIPS_SCRATCH
        + LINE_SCRATCH,
        compiler_params=pltpu.CompilerParams(
            vmem_limit_bytes=VMEM_LIMIT, collective_id=1, has_side_effects=True
        ),
    )(
        features[0],
        cotangent[0],
        w_fine,
        w_coarse,
        gain[None],
        neighbors,
        neighbor_edges,
    )
    return (output[None], grad_features[None], grad_w_fine, grad_w_coarse, grad_gain[0])


def solution(mesh):
    return jax.shard_map(
        on_device,
        mesh=mesh,
        in_specs=(
            P("face", "tile", None, None),
            P("face", "tile", None, None),
            P(),
            P(),
            P(),
            P(),
            P(),
        ),
        out_specs=(
            P("face", "tile", None, None),
            P("face", "tile", None, None),
            P(None, "tile", None),
            P(None, "tile", None),
            P(),
        ),
        check_vma=False,
    )
```

```python
import jax
import jax.numpy as jnp
from jax import lax
from jax.experimental import pallas as pl
from jax.experimental.pallas import tpu as pltpu
from jax.sharding import PartitionSpec as P

BF = jnp.bfloat16
F32 = jnp.float32
MESH = pl.DeviceIdType.MESH
NF = 8
NT = 32
NZ = 16
RD = 8
FS = 256
CS = 128
C = 256
GROUP = 8
SLOTS = 16
CELLS = NF * FS * FS
VMEM_LIMIT = 60 * 1024 * 1024

VM = pl.BlockSpec(memory_space=pltpu.VMEM)
SM = pl.BlockSpec(memory_space=pltpu.SMEM)
DMA = pltpu.SemaphoreType.DMA


def remote(src, dst, send, recv, face, tile):
    return pltpu.make_async_remote_copy(
        src_ref=src,
        dst_ref=dst,
        send_sem=send,
        recv_sem=recv,
        device_id=(face, tile),
        device_id_type=MESH,
    )


def place():
    return lax.axis_index("face"), lax.axis_index("tile")


def is_rim(tile):
    return (tile == 0) | (tile == NT - 1)


def slot_device(slot):
    return lax.div(slot, 2), (NT - 1) * lax.rem(slot, 2)


def my_slot(face, tile):
    return 2 * face + jnp.where(tile == NT - 1, 1, 0)


def multiple(value, of):
    return pl.multiple_of(value * of, of)


def signal(barrier, face, tile):
    pl.semaphore_signal(barrier, inc=1, device_id=(face, tile), device_id_type=MESH)


def line_a(face, tile, step):
    mine = lax.rem(tile, NZ)
    other = lax.rem(mine + step, NZ)
    return mine, other, (face, tile - mine + other)


def line_b(face, tile, step):
    mine = face * 2 + lax.div(tile, NZ)
    other = lax.rem(mine + step, 2 * NF)
    return mine, other, (lax.div(other, 2), lax.rem(other, 2) * NZ + lax.rem(tile, NZ))


def barrier_signal():
    face, tile = place()
    barrier = pltpu.get_barrier_semaphore()
    across = lax.rem(tile + NZ, NT)
    across = across - lax.rem(across, NZ) + lax.rem(tile, 2)

    @pl.loop(1, NZ)
    def _(step):
        for line in (line_a, line_b):
            _, _, device = line(face, tile, step)
            signal(barrier, *device)

    @pl.loop(0, NZ // 2)
    def _(z):
        signal(barrier, face, across + 2 * z)

    signal(barrier, face, lax.rem(tile + 1, NT))
    signal(barrier, face, lax.rem(tile + NT - 1, NT))

    @pl.when(is_rim(tile))
    def _():
        mine = my_slot(face, tile)

        @pl.loop(1, SLOTS)
        def _(step):
            signal(barrier, *slot_device(lax.rem(mine + step, SLOTS)))


def barrier_wait():
    _, tile = place()
    barrier = pltpu.get_barrier_semaphore()
    count = 2 * (NZ - 1) + NZ // 2 + 2

    @pl.when(is_rim(tile))
    def _():
        pl.semaphore_wait(barrier, count + SLOTS - 1)

    @pl.when(~is_rim(tile))
    def _():
        pl.semaphore_wait(barrier, count)


def sum_start(line, own, buf, send, recv):
    face, tile = place()

    @pl.loop(1, NZ)
    def _(step):
        mine, _, device = line(face, tile, step)
        remote(own, buf.at[mine], send, recv, *device).start()

    mine, _, _ = line(face, tile, 0)
    buf[mine] = own[...]


def sum_finish(line, own, buf, send, recv):
    face, tile = place()
    _, _, device = line(face, tile, 1)
    arrived = buf.at[pl.ds(0, NZ - 1)]
    copies = remote(arrived, arrived, send, recv, *device)
    copies.wait_recv()
    total = buf[0]
    for i in range(1, NZ):
        total = total + buf[i]
    copies.wait_send()
    return total


SUM_SCRATCH = [
    pltpu.VMEM((2, C), F32),
    pltpu.VMEM((2, C), F32),
    pltpu.VMEM((NZ, 2, C), F32),
    pltpu.VMEM((NZ, 2, C), F32),
    DMA,
    DMA,
    DMA,
    DMA,
]

RIM = C + 128

HALO_SCRATCH = [
    pltpu.VMEM((2, FS, C), BF),
    pltpu.VMEM((2, CS, C), BF),
    pltpu.VMEM((SLOTS, 16, RIM), BF),
    pltpu.VMEM((SLOTS, 16, RIM), BF),
    pltpu.VMEM((SLOTS, 16, RIM), BF),
    pltpu.VMEM((SLOTS, 16, RIM), BF),
    pltpu.VMEM((32, C), F32),
    pltpu.VMEM((32, C), BF),
    pltpu.VMEM((NF, 32, C), BF),
    pltpu.VMEM((32, C), BF),
] + [DMA] * 10


class Halo:
    def __init__(self, fine, coarse, scratch, tables):
        self.fine, self.coarse = fine, coarse
        (
            self.hf,
            self.hc,
            self.rim,
            self.r1,
            self.st,
            self.r2,
            self.rows,
            self.srec,
            self.sall,
            self.sides,
            self.fs,
            self.fr,
            self.cs,
            self.cr,
            self.s1,
            self.q1,
            self.s2,
            self.q2,
            self.ss,
            self.sr,
        ) = scratch
        self.nb, self.ed = tables
        self.face, self.tile = place()
        self.slot = my_slot(self.face, self.tile)

    def rows_start(self):
        up = lax.rem(self.tile + 1, NT)
        down = lax.rem(self.tile + NT - 1, NT)
        for field, halo, send, recv in (
            (self.fine, self.hf, self.fs, self.fr),
            (self.coarse, self.hc, self.cs, self.cr),
        ):
            last = field.shape[0] - 1
            remote(field.at[last], halo.at[0], send, recv, self.face, up).start()
            remote(field.at[0], halo.at[1], send, recv, self.face, down).start()

    def rows_wait(self):
        up = lax.rem(self.tile + 1, NT)
        for halo, send, recv in ((self.hf, self.fs, self.fr), (self.hc, self.cs, self.cr)):
            both = remote(halo, halo, send, recv, self.face, up)
            both.wait_recv()
            both.wait_send()

    def rim_partner(self, step):
        other = lax.rem(self.slot + step, SLOTS)
        return other, slot_device(other)

    def rim_wait(self, buf, send, recv):
        _, device = self.rim_partner(1)
        arrived = buf.at[pl.ds(0, SLOTS - 1)]
        copies = remote(arrived, arrived, send, recv, *device)
        copies.wait_recv()
        copies.wait_send()

    def start(self):
        @pl.when(is_rim(self.tile))
        def _():
            fine_row = jnp.where(self.tile == 0, 0, RD - 1)
            coarse_row = jnp.where(self.tile == 0, 0, RD // 2 - 1)
            self.rim[:, :, 0:C] = self.fine[fine_row].reshape(SLOTS, 16, C)
            cells = self.coarse[coarse_row]
            self.rim[0:8, :, C:RIM] = cells[:, 0:128].reshape(8, 16, 128)
            self.rim[8:16, :, C:RIM] = cells[:, 128:256].reshape(8, 16, 128)

            @pl.loop(1, SLOTS)
            def _(step):
                other, device = self.rim_partner(step)
                remote(self.rim.at[other], self.r1.at[self.slot], self.s1, self.q1, *device).start()

            self.r1[self.slot] = self.rim[self.slot]

        self.rows_start()

    def middle(self):
        @pl.when(is_rim(self.tile))
        def _():
            self.rim_wait(self.r1, self.s1, self.q1)

            @pl.loop(0, SLOTS)
            def _(slot):
                face, edge = lax.div(slot, 2), 2 * lax.rem(slot, 2)
                source = 2 * self.nb[face, edge] + lax.div(self.ed[face, edge], 2)
                self.st[slot] = self.r1[source]

            @pl.loop(1, SLOTS)
            def _(step):
                other, device = self.rim_partner(step)
                remote(self.st.at[other], self.r2.at[self.slot], self.s2, self.q2, *device).start()

            self.r2[self.slot] = self.st[self.slot]

        self.rows_wait()
        fine_rows = [self.hf.at[0]] + [self.fine.at[r] for r in range(RD)] + [self.hf.at[1]]
        coarse_rows = [self.hc.at[0]] + [self.coarse.at[r] for r in range(RD // 2)]
        coarse_rows += [self.hc.at[1]]
        for i, row in enumerate(fine_rows + coarse_rows):
            side = row.shape[0]
            self.rows[i : i + 1, :] = row[0:16, :].astype(F32)[0:1]
            self.rows[16 + i : 17 + i, :] = row[side - 16 : side, :].astype(F32)[15:16]
        self.srec[...] = self.rows[...].astype(BF)

        @pl.loop(1, NF)
        def _(step):
            other = lax.rem(self.face + step, NF)
            remote(
                self.srec, self.sall.at[self.face], self.ss, self.sr, other, self.tile
            ).start()

        self.sall[self.face] = self.srec[...]

    def finish(self, flips):
        @pl.when(is_rim(self.tile))
        def _():
            self.rim_wait(self.r2, self.s2, self.q2)
            flip_top, flip_bottom = flips
            flip = jnp.where(self.tile == 0, flip_top, flip_bottom)
            edge = jnp.where(self.tile == 0, 0, 1)
            fine = self.r2[:, :, 0:C].reshape(FS, C)
            coarse = jnp.concatenate(
                [
                    self.r2[0:8, :, C:RIM].reshape(CS, 128),
                    self.r2[8:16, :, C:RIM].reshape(CS, 128),
                ],
                axis=1,
            )
            self.hf[edge] = dot(rim_matrix(FS, flip), fine).astype(BF)
            self.hc[edge] = dot(rim_matrix(CS, flip), coarse).astype(BF)

        other = lax.rem(self.face + 1, NF)
        arrived = self.sall.at[pl.ds(0, NF - 1)]
        copies = remote(arrived, arrived, self.ss, self.sr, other, self.tile)
        copies.wait_recv()
        copies.wait_send()
        left_face, right_face = self.nb[self.face, 3], self.nb[self.face, 1]
        self.sides[0:16, :] = self.sall[left_face, 16:32, :]
        self.sides[16:32, :] = self.sall[right_face, 0:16, :]


def iota(shape, dim):
    return lax.broadcasted_iota(jnp.int32, shape, dim)


def dot(a, b):
    return jnp.dot(a, b, preferred_element_type=F32)


def sigmoid(values):
    return 0.5 * jnp.tanh(0.5 * values) + 0.5


def pool_matrix():
    row, col = iota((CS, 2 * FS), 0), iota((CS, 2 * FS), 1)
    return jnp.where(lax.div(lax.rem(col, FS), 2) == row, 1.0, 0.0).astype(BF)


def spread_matrix():
    row, col = iota((FS, 2 * CS), 0), iota((FS, 2 * CS), 1)
    return jnp.where(lax.rem(col, CS) == lax.div(row, 2), 1.0, 0.0).astype(BF)


def spread(matrix, values):
    high = values.astype(BF)
    low = (values - high.astype(F32)).astype(BF)
    return dot(matrix, jnp.concatenate([high, low], axis=0))


def rim_matrix(side, flip):
    row, col = iota((side, side), 0), iota((side, side), 1)
    source = jnp.where(flip, side - 1 - row, row)
    return jnp.where(col == source, 1.0, 0.0).astype(BF)


def store_shifted(ref, row, values, left, right):
    n = values.shape[0]
    position = iota(values.shape, 0)
    before = jnp.where(position == 0, left, pltpu.roll(values, 1, 0))
    after = jnp.where(position == n - 1, right, pltpu.roll(values, n - 1, 0))
    ref[row, :, 0:C] = before.astype(BF)
    ref[row, :, C : 2 * C] = values.astype(BF)
    ref[row, :, 2 * C : 3 * C] = after.astype(BF)


def group_sum(values):
    lane = iota(values.shape, 1)
    for width in (1, 2, 4):
        up = pltpu.roll(values, width, 1)
        down = pltpu.roll(values, C - width, 1)
        values = values + jnp.where(lax.rem(lax.div(lane, width), 2) == 0, down, up)
    return values


def norm_vectors(total):
    grouped = group_sum(total) / (CELLS * GROUP)
    mean, second = grouped[0:1], grouped[1:2]
    return mean, lax.rsqrt(second - mean * mean + 1e-05)


def edge_flags(ed_ref):
    face, tile = place()
    first, last = tile == 0, tile == NT - 1
    flip_top = first & (ed_ref[face, 0] != 2)
    flip_bottom = last & (ed_ref[face, 2] != 0)
    return first, last, flip_top, flip_bottom


def masked_sides(sides, first, last):
    row = lax.rem(iota(sides.shape, 0), 16)
    top = (row == 0) | (row == RD + 2)
    bottom = (row == RD + 1) | (row == 15)
    zero = (top & first) | (bottom & last)
    return jnp.where(zero, 0.0, sides)


def back_weights(w_ref, out_ref):
    for k in range(3):
        for m in range(3):
            tap = w_ref[8 - (3 * k + m)].astype(F32)
            out_ref[k, m * C : (m + 1) * C, :] = tap.T.astype(BF)


def halo_weights(wt_ref, flip_top, flip_bottom):
    def turned(k):
        return jnp.concatenate(
            [wt_ref[k, (2 - m) * C : (3 - m) * C, :] for m in range(3)], axis=0
        )

    top = jnp.where(flip_top, turned(2), wt_ref[0])
    bottom = jnp.where(flip_bottom, turned(0), wt_ref[2])
    return top, bottom


def rows_of(ref, start, count):
    _, side, width = ref.shape
    return ref[pl.ds(start, count)].reshape(count * side, width)


def taps_of(ref, k):
    return ref[3 * k : 3 * k + 3].reshape(3 * C, C)


SHARE = 144
NC = 16


def put_share(shares, tap, product):
    turned = product.T.reshape(4, 4, 2, 8, C)
    halves = [turned[..., :128], turned[..., 128:]]
    shares[:, :, :, 16 * tap : 16 * tap + 16, :] = jnp.concatenate(halves, axis=3).astype(BF)


def put_grads(out, total):
    total = (total * (1.0 / CELLS)).reshape(9, 2, 8, 128)
    out[:, :, 0:128] = total[:, 0]
    out[:, :, 128:256] = total[:, 1]


def tree(parts):
    parts = [part.astype(F32) for part in parts]
    while len(parts) > 1:
        parts = [sum(parts[i : i + 2]) for i in range(0, len(parts), 2)]
    return parts[0]


CUT = 80
LANES = ((0, CUT), (CUT, SHARE - CUT))

REDUCE_SCRATCH = [
    pltpu.VMEM((4, 4, 2, SHARE, 128), BF),
    pltpu.VMEM((4, 4, SHARE, 128), BF),
    pltpu.VMEM((4, 4, SHARE, 128), BF),
    pltpu.VMEM((2, 4, CUT, 128), BF),
    pltpu.VMEM((2, 4, SHARE - CUT, 128), BF),
    pltpu.VMEM((4, CUT, 128), BF),
    pltpu.VMEM((4, SHARE - CUT, 128), BF),
    pltpu.VMEM((4, CUT, 128), BF),
    pltpu.VMEM((4, SHARE - CUT, 128), BF),
    pltpu.VMEM((4, SHARE, 128), BF),
    pltpu.VMEM((NC, SHARE, 128), BF),
    pltpu.VMEM((SHARE, 128), BF),
    pltpu.VMEM((2, SHARE, 128), BF),
    DMA((3,)),
    DMA((3,)),
    DMA((2,)),
    DMA((2,)),
    DMA((2,)),
    DMA((2,)),
    DMA((4,)),
    DMA,
    DMA,
    DMA((2,)),
]


class Reduce:
    def __init__(self, scratch):
        (
            self.shares,
            self.got,
            self.part,
            r0,
            r1,
            t0,
            t1,
            u0,
            u1,
            self.px,
            self.rz,
            self.block,
            self.rb,
            self.s0,
            self.q0,
            self.sa,
            self.qa,
            self.sc,
            self.qc,
            self.sz,
            self.qz,
            self.sb,
            self.qb,
        ) = scratch
        self.one, self.on, self.two = (r0, r1), (t0, t1), (u0, u1)
        self.face, self.tile = place()
        self.core, self.chip = lax.rem(self.tile, 2), lax.div(self.tile, 2)
        self.x, self.high = lax.div(self.face, 2), lax.rem(self.face, 2)
        self.home = lax.rem(self.chip, 4)
        self.owner = self.home == self.x
        near = self.x + 1 - 2 * lax.rem(self.x, 2)
        self.partner = (near, 3 - self.x)

    def swap(self, k):
        rows = pl.ds(48 * k, 48)
        return remote(
            self.shares.at[:, :, 1 - self.core, rows, :],
            self.got.at[:, :, rows, :],
            self.s0.at[k],
            self.q0.at[k],
            self.face,
            self.tile + 1 - 2 * self.core,
        )

    def swap_start(self, k):
        self.swap(k).start()

    def across(self, way, src, dst, send, recv):
        return remote(src, dst, send, recv, 2 * self.partner[way] + self.high, self.tile)

    def first(self, way, i):
        other = self.partner[way]
        beyond = 3 - other if way == 0 else other + 1 - 2 * lax.rem(other, 2)
        start, rows = LANES[way]
        return self.across(
            way,
            self.part.at[:, (other, beyond)[i], pl.ds(start, rows), :],
            self.one[way].at[i],
            self.sa.at[way],
            self.qa.at[way],
        )

    def first_wait(self, way):
        return self.across(way, self.one[way], self.one[way], self.sa.at[way], self.qa.at[way])

    def second(self, way):
        return self.across(1 - way, self.on[way], self.two[way], self.sc.at[way], self.qc.at[way])

    def swap_take(self):
        for k in range(3):
            self.swap(k).wait_recv()

        @pl.loop(0, 4)
        def _(j):
            for h in range(4):
                both = self.shares[j, h, self.core].astype(F32) + self.got[j, h].astype(F32)
                self.part[j, h] = both.astype(BF)

        for way in range(2):
            for i in range(2):
                self.first(way, i).start()

    def first_take(self):
        for way in range(2):
            self.first_wait(way).wait_recv()
            start, rows = LANES[way]
            span = pl.ds(start, rows)
            mine = self.part[:, self.partner[1 - way], span, :].astype(F32)
            self.on[way][...] = (mine + self.one[way][1].astype(F32)).astype(BF)
            self.second(way).start()

    def second_take(self):
        for way in range(2):
            self.second(way).wait_recv()
            start, rows = LANES[way]
            mine = self.part[:, self.x, pl.ds(start, rows), :].astype(F32)
            total = mine + self.one[way][0].astype(F32) + self.two[way][...].astype(F32)
            self.px[:, start : start + rows, :] = total.astype(BF)

        @pl.loop(0, 4)
        def _(j):
            mine = 4 * j + self.x == self.chip

            @pl.when(jnp.logical_not(mine))
            def _():
                self.scatter(j).start()

            @pl.when(mine)
            def _():
                self.rz[self.chip] = self.px[j]

    def scatter(self, j):
        return remote(
            self.px.at[j],
            self.rz.at[self.chip],
            self.sz.at[j],
            self.qz,
            self.face,
            2 * (4 * j + self.x) + self.core,
        )

    def share(self, other):
        return remote(
            self.block, self.rb.at[self.high], self.sb, self.qb.at[self.high], other, self.tile
        )

    def chips_take(self):
        @pl.when(self.owner)
        def _():
            arrived = self.rz.at[pl.ds(0, NC - 1)]
            other = lax.rem(self.chip + 1, NC)
            remote(
                arrived, arrived, self.sb, self.qz, self.face, 2 * other + self.core
            ).wait_recv()
            self.block[...] = tree([self.rz[j] for j in range(NC)]).astype(BF)

            @pl.loop(1, NF)
            def _(step):
                self.share(lax.rem(self.face + step, NF)).start()

            self.rb[self.high] = self.block[...]

    def finish(self, out):
        for high in range(2):
            source = 2 * self.home + high

            @pl.when(source != self.face)
            def _():
                remote(
                    self.block, self.rb.at[high], self.sb, self.qb.at[high], source, self.tile
                ).wait_recv()

        put_grads(out, tree([self.rb[0], self.rb[1]]))

        for k in range(3):
            self.swap(k).wait_send()
        for way in range(2):
            self.first_wait(way).wait_send()
            self.second(way).wait_send()

        @pl.loop(0, 4)
        def _(j):
            @pl.when(4 * j + self.x != self.chip)
            def _():
                self.scatter(j).wait_send()

        @pl.when(self.owner)
        def _():
            sent = self.rz.at[pl.ds(0, NF - 1)]
            remote(
                sent, sent, self.sb, self.qz, lax.rem(self.face + 1, NF), self.tile
            ).wait_send()


HALF = RD // 2
N_SUM, N_HALO = len(SUM_SCRATCH), len(HALO_SCRATCH)

ANY = pl.BlockSpec(memory_space=pl.ANY)

WORK_SCRATCH = [
    pltpu.SMEM((NF, 4), jnp.int32),
    pltpu.SMEM((NF, 4), jnp.int32),
    pltpu.VMEM((9, C, C), BF),
    pltpu.VMEM((9, C, C), BF),
    pltpu.VMEM((HALF, CS, C), BF),
    pltpu.VMEM((3, 3 * C, C), BF),
    pltpu.VMEM((3, 3 * C, C), BF),
    pltpu.VMEM((RD + 2, FS, 3 * C), BF),
    pltpu.VMEM((RD + 2, FS, 3 * C), BF),
    pltpu.VMEM((HALF + 2, CS, 3 * C), BF),
    pltpu.VMEM((HALF + 2, CS, 3 * C), BF),
    pltpu.VMEM((RD, FS, C), BF),
    pltpu.VMEM((HALF, CS, C), BF),
    pltpu.VMEM((RD, FS, C), BF),
    pltpu.VMEM((RD, FS, C), F32),
    pltpu.VMEM((HALF, CS, C), F32),
    pltpu.VMEM((C, RD * FS), BF),
    pltpu.VMEM((C, HALF * CS), BF),
    pltpu.VMEM((32, C), F32),
    pltpu.VMEM((32, C), F32),
    DMA((6,)),
]


def extended(ref3, field, halo, edge, first, side):
    rows = field.shape[0]

    def put(i, row):
        left, right = edge[pl.ds(first + i, 1), :], edge[pl.ds(first + i + 16, 1), :]
        store_shifted(ref3, i, side(row.astype(F32)), left, right)

    put(0, halo[0])
    put(rows + 1, halo[1])

    @pl.loop(0, rows)
    def _(r):
        put(r + 1, field[r])


def whole_kernel(
    feat, cot, wf_any, wc_any, gain, nb_any, ed_any,
    output, grad_act, grad_w_fine, grad_w_coarse, grad_gain, vectors, *scratch
):
    scratch = list(scratch)

    def take(n):
        got = scratch[:n]
        del scratch[:n]
        return got

    own_a, own_b, buf_a, buf_b, sa, ra, sb, rb = take(N_SUM)
    own_c, own_d, buf_c, buf_d, sc, rc, sd, rd = take(N_SUM)
    halo1_scratch, halo2_scratch = take(N_HALO), take(N_HALO)
    (
        nb, ed, wf_taps, wc_taps, gco, wtf, wtc, x3, u3, c3, v3, fine, coarse_in, grad_fine,
        ga, gci, gt, gct, edge_h, edge_c, local,
    ) = take(len(WORK_SCRATCH))
    reduce_f = Reduce(take(len(REDUCE_SCRATCH)))
    reduce_c = Reduce(take(len(REDUCE_SCRATCH)))

    barrier_signal()
    loads = [
        pltpu.make_async_copy(src, dst, local.at[i])
        for i, (src, dst) in enumerate(
            ((nb_any, nb), (ed_any, ed), (wf_any, wf_taps), (wc_any, wc_taps))
        )
    ]
    for load in loads:
        load.start()
    halo1 = Halo(feat, gco, halo1_scratch, (nb, ed))
    halo2 = Halo(grad_fine, coarse_in, halo2_scratch, (nb, ed))

    pool, widen = pool_matrix(), spread_matrix()
    own_a[...] = jnp.zeros_like(own_a)
    own_c[...] = jnp.zeros_like(own_c)

    @pl.loop(0, HALF)
    def _(i):
        gco[i] = dot(pool, rows_of(cot, 2 * i, 2)).astype(BF)
        values = rows_of(feat, 2 * i, 2).astype(F32)
        own_a[0:1, :] += jnp.sum(values, axis=0, keepdims=True)
        own_a[1:2, :] += jnp.sum(values * values, axis=0, keepdims=True)

    barrier_wait()
    sum_start(line_a, own_a, buf_a, sa, ra)
    halo1.start()
    for load in loads:
        load.wait()
    back_weights(wc_taps, wtc)
    own_b[...] = sum_finish(line_a, own_a, buf_a, sa, ra)
    sum_start(line_b, own_b, buf_b, sb, rb)
    halo1.middle()
    back_weights(wf_taps, wtf)
    for r in range(HALF):
        gct[:, r * CS : (r + 1) * CS] = gco[r].astype(F32).T.astype(BF)

    first, last, flip_top, flip_bottom = edge_flags(ed)
    halo1.finish((flip_top, flip_bottom))
    edge_c[...] = masked_sides(halo1.sides[...].astype(F32), first, last)

    extended(v3, gco, halo1.hc, edge_c, RD + 2, lambda row: row)
    top, bottom = halo_weights(wtc, flip_top, flip_bottom)
    gci[...] = dot(rows_of(v3, 1, HALF), wtc[1]).reshape(HALF, CS, C)
    gci[1:HALF] += dot(rows_of(v3, 1, HALF - 1), wtc[0]).reshape(HALF - 1, CS, C)
    gci[0 : HALF - 1] += dot(rows_of(v3, 2, HALF - 1), wtc[2]).reshape(HALF - 1, CS, C)
    gci[0] += dot(v3[0], top)
    gci[HALF - 1] += dot(v3[HALF + 1], bottom)

    total = sum_finish(line_b, own_b, buf_b, sb, rb)
    mean, inverse = norm_vectors(total)
    scale = gain[...]

    def hidden(raw):
        act = (raw - mean) * inverse * scale
        return (act * sigmoid(act)).astype(BF).astype(F32)

    edge_h[...] = masked_sides(hidden(halo1.sides[...].astype(F32)), first, last)
    extended(x3, feat, halo1.hf, edge_h, 0, hidden)

    def forward(i):
        acc = dot(rows_of(x3, 2 * i, 2), taps_of(wf_taps, 0))
        acc += dot(rows_of(x3, 2 * i + 1, 2), taps_of(wf_taps, 1))
        acc += dot(rows_of(x3, 2 * i + 2, 2), taps_of(wf_taps, 2))
        out = acc.astype(BF)
        fine[pl.ds(2 * i, 2)] = out.reshape(2, FS, C)
        pooled = 0.25 * dot(pool, out)
        gate = sigmoid(pooled)
        coarse_in[i] = (pooled * gate).astype(BF)
        slope = gate * (1.0 + pooled * (1.0 - gate))
        wide = spread(widen, gci[i] * slope * 0.25)
        for r in range(2):
            grad_fine[2 * i + r] = (cot[2 * i + r].astype(F32) + wide).astype(BF)

    @pl.loop(0, 2)
    def _(i):
        forward((HALF - 1) * i)

    halo2.start()
    pl.loop(1, HALF - 1)(forward)

    def fine_gradient(k):
        product = dot(gt[...], rows_of(x3, k, RD))
        for m in range(3):
            put_share(reduce_f.shares, 3 * k + m, product[:, m * C : (m + 1) * C])
        reduce_f.swap_start(k)

    for r in range(RD):
        gt[:, r * FS : (r + 1) * FS] = grad_fine[r].astype(F32).T.astype(BF)
    halo2.middle()
    for k in range(3):
        fine_gradient(k)
    halo2.finish((flip_top, flip_bottom))
    edge_h[...] = masked_sides(halo2.sides[...].astype(F32), first, last)
    reduce_f.swap_take()

    extended(c3, coarse_in, halo2.hc, edge_h, RD + 2, lambda row: row)
    for k in range(3):
        product = dot(gct[...], rows_of(c3, k, HALF))
        for m in range(3):
            put_share(reduce_c.shares, 3 * k + m, product[:, m * C : (m + 1) * C])
        reduce_c.swap_start(k)
    reduce_f.first_take()

    extended(u3, grad_fine, halo2.hf, edge_h, 0, lambda row: row)
    top, bottom = halo_weights(wtf, flip_top, flip_bottom)
    reduce_c.swap_take()
    ga[1 : RD - 1] = jnp.zeros((RD - 2, FS, C), F32)
    ga[0] = dot(u3[0], top)
    ga[RD - 1] = dot(u3[RD + 1], bottom)
    u3[0] = jnp.zeros((FS, 3 * C), BF)
    u3[RD + 1] = jnp.zeros((FS, 3 * C), BF)

    def back(i):
        grad = dot(rows_of(u3, 2 * i, 2), wtf[0])
        grad += dot(rows_of(u3, 2 * i + 1, 2), wtf[1])
        grad += dot(rows_of(u3, 2 * i + 2, 2), wtf[2])
        grad += rows_of(ga, 2 * i, 2)
        normed = (rows_of(feat, 2 * i, 2).astype(F32) - mean) * inverse
        act = normed * scale
        gate = sigmoid(act)
        grad = grad * (gate * (1.0 + act * (1.0 - gate)))
        ga[pl.ds(2 * i, 2)] = grad.reshape(2, FS, C)
        own_c[0:1, :] += jnp.sum(grad * normed, axis=0, keepdims=True)
        own_c[1:2, :] += jnp.sum(grad, axis=0, keepdims=True)

    pl.loop(0, HALF // 2)(back)
    reduce_f.second_take()
    reduce_c.first_take()
    pl.loop(HALF // 2, HALF)(back)
    sum_start(line_a, own_c, buf_c, sc, rc)
    store_act = pltpu.make_async_copy(ga, grad_act, local.at[4])
    store_act.start()
    reduce_c.second_take()

    @pl.loop(0, HALF)
    def _(i):
        out = dot(c3[i], taps_of(wc_taps, 0))
        out += dot(c3[i + 1], taps_of(wc_taps, 1))
        out += dot(c3[i + 2], taps_of(wc_taps, 2))
        wide = spread(widen, out)
        for r in range(2):
            fine[2 * i + r] = (fine[2 * i + r].astype(F32) + wide).astype(BF)

    store_output = pltpu.make_async_copy(fine, output, local.at[5])
    store_output.start()
    own_d[...] = sum_finish(line_a, own_c, buf_c, sc, rc)
    sum_start(line_b, own_d, buf_d, sd, rd)
    reduce_f.chips_take()
    reduce_c.chips_take()
    sums = sum_finish(line_b, own_d, buf_d, sd, rd)

    grad_gain[...] = sums[0:1] * (1.0 / CELLS)
    grouped = group_sum(sums * scale) / (CELLS * GROUP)
    group_slope, group_shift = grouped[0:1], grouped[1:2]
    for i, vector in enumerate((mean, inverse, scale, group_shift, group_slope)):
        vectors[i : i + 1, :] = vector
    reduce_f.finish(grad_w_fine)
    reduce_c.finish(grad_w_coarse)
    store_act.wait()
    store_output.wait()


def last_kernel(
    feat, ga, vectors, output_in, wf_in, wc_in, gain_in,
    output, grad_features, wf_out, wc_out, gain_out, feat_v, ga_v, out_v, sems
):
    passed = [
        pltpu.make_async_copy(src, dst, sems.at[i])
        for i, (src, dst) in enumerate(
            ((output_in, output), (wf_in, wf_out), (wc_in, wc_out), (gain_in, gain_out))
        )
    ]

    def rows(q):
        return pl.ds(2 * q, 2)

    loads = [
        (
            pltpu.make_async_copy(feat.at[rows(q)], feat_v.at[rows(q)], sems.at[4 + 3 * q]),
            pltpu.make_async_copy(ga.at[rows(q)], ga_v.at[rows(q)], sems.at[5 + 3 * q]),
        )
        for q in range(HALF)
    ]
    stores = [
        pltpu.make_async_copy(out_v.at[rows(q)], grad_features.at[rows(q)], sems.at[6 + 3 * q])
        for q in range(HALF)
    ]
    for load in loads:
        for copy in load:
            copy.start()
    for copy in passed:
        copy.start()
    mean, inverse, scale = vectors[0:1], vectors[1:2], vectors[2:3]
    group_shift, group_slope = vectors[3:4], vectors[4:5]
    for q in range(HALF):
        for copy in loads[q]:
            copy.wait()
        for r in (2 * q, 2 * q + 1):
            normed = (feat_v[r].astype(F32) - mean) * inverse
            out_v[r] = inverse * (scale * ga_v[r] - group_shift - normed * group_slope)
        stores[q].start()
    for copy in stores + passed:
        copy.wait()


def shape(dims, dtype):
    return jax.ShapeDtypeStruct(dims, dtype)


def on_device(features, cotangent, w_fine, w_coarse, gain, neighbors, neighbor_edges):
    outs = [
        shape((RD, FS, C), BF),
        shape((RD, FS, C), F32),
        shape((9, 8, C), F32),
        shape((9, 8, C), F32),
        shape((1, C), F32),
    ]
    output, grad_act, grad_w_fine, grad_w_coarse, grad_gain, vectors = pl.pallas_call(
        whole_kernel,
        in_specs=[VM, VM, ANY, ANY, VM, ANY, ANY],
        out_specs=[ANY, ANY, VM, VM, VM, VM],
        out_shape=outs + [shape((8, C), F32)],
        scratch_shapes=SUM_SCRATCH * 2
        + HALO_SCRATCH * 2
        + WORK_SCRATCH
        + REDUCE_SCRATCH * 2,
        compiler_params=pltpu.CompilerParams(
            vmem_limit_bytes=VMEM_LIMIT, collective_id=1, has_side_effects=True
        ),
    )(features[0], cotangent[0], w_fine, w_coarse, gain[None], neighbors, neighbor_edges)
    output, grad_features, grad_w_fine, grad_w_coarse, grad_gain = pl.pallas_call(
        last_kernel,
        in_specs=[ANY, ANY, VM] + [ANY] * 4,
        out_specs=[ANY] * 5,
        out_shape=outs,
        scratch_shapes=[
            pltpu.VMEM((RD, FS, C), BF),
            pltpu.VMEM((RD, FS, C), F32),
            pltpu.VMEM((RD, FS, C), F32),
            DMA((4 + 3 * HALF,)),
        ],
        compiler_params=pltpu.CompilerParams(vmem_limit_bytes=VMEM_LIMIT),
    )(features[0], grad_act, vectors, output, grad_w_fine, grad_w_coarse, grad_gain)
    return (output[None], grad_features[None], grad_w_fine, grad_w_coarse, grad_gain[0])


def solution(mesh):
    return jax.shard_map(
        on_device,
        mesh=mesh,
        in_specs=(
            P("face", "tile", None, None),
            P("face", "tile", None, None),
            P(),
            P(),
            P(),
            P(),
            P(),
        ),
        out_specs=(
            P("face", "tile", None, None),
            P("face", "tile", None, None),
            P(None, "tile", None),
            P(None, "tile", None),
            P(),
        ),
        check_vma=False,
    )
```

```python
import jax
import jax.numpy as jnp
from jax import lax
from jax.experimental import pallas as pl
from jax.experimental.pallas import tpu as pltpu
from jax.sharding import PartitionSpec as P

BF = jnp.bfloat16
F32 = jnp.float32
MESH = pl.DeviceIdType.MESH
NF = 8
NT = 32
NZ = 16
RD = 8
FS = 256
CS = 128
C = 256
GROUP = 8
SLOTS = 16
CELLS = NF * FS * FS
VMEM_LIMIT = 60 * 1024 * 1024

VM = pl.BlockSpec(memory_space=pltpu.VMEM)
SM = pl.BlockSpec(memory_space=pltpu.SMEM)
DMA = pltpu.SemaphoreType.DMA


def remote(src, dst, send, recv, face, tile):
    return pltpu.make_async_remote_copy(
        src_ref=src,
        dst_ref=dst,
        send_sem=send,
        recv_sem=recv,
        device_id=(face, tile),
        device_id_type=MESH,
    )


def place():
    return lax.axis_index("face"), lax.axis_index("tile")


def is_rim(tile):
    return (tile == 0) | (tile == NT - 1)


def slot_device(slot):
    return lax.div(slot, 2), (NT - 1) * lax.rem(slot, 2)


def my_slot(face, tile):
    return 2 * face + jnp.where(tile == NT - 1, 1, 0)


def multiple(value, of):
    return pl.multiple_of(value * of, of)


def signal(barrier, face, tile):
    pl.semaphore_signal(barrier, inc=1, device_id=(face, tile), device_id_type=MESH)


def line_a(face, tile, step):
    mine = lax.rem(tile, NZ)
    other = lax.rem(mine + step, NZ)
    return mine, other, (face, tile - mine + other)


def line_b(face, tile, step):
    mine = face * 2 + lax.div(tile, NZ)
    other = lax.rem(mine + step, 2 * NF)
    return mine, other, (lax.div(other, 2), lax.rem(other, 2) * NZ + lax.rem(tile, NZ))


def barrier_signal():
    face, tile = place()
    barrier = pltpu.get_barrier_semaphore()
    across = lax.rem(tile + NZ, NT)
    across = across - lax.rem(across, NZ) + lax.rem(tile, 2)

    @pl.loop(1, NZ)
    def _(step):
        for line in (line_a, line_b):
            _, _, device = line(face, tile, step)
            signal(barrier, *device)

    @pl.loop(0, NZ // 2)
    def _(z):
        signal(barrier, face, across + 2 * z)

    signal(barrier, face, lax.rem(tile + 1, NT))
    signal(barrier, face, lax.rem(tile + NT - 1, NT))

    @pl.when(is_rim(tile))
    def _():
        mine = my_slot(face, tile)

        @pl.loop(1, SLOTS)
        def _(step):
            signal(barrier, *slot_device(lax.rem(mine + step, SLOTS)))


def barrier_wait():
    _, tile = place()
    barrier = pltpu.get_barrier_semaphore()
    count = 2 * (NZ - 1) + NZ // 2 + 2

    @pl.when(is_rim(tile))
    def _():
        pl.semaphore_wait(barrier, count + SLOTS - 1)

    @pl.when(~is_rim(tile))
    def _():
        pl.semaphore_wait(barrier, count)


def sum_start(line, own, buf, send, recv):
    face, tile = place()

    @pl.loop(1, NZ)
    def _(step):
        mine, _, device = line(face, tile, step)
        remote(own, buf.at[mine], send, recv, *device).start()

    mine, _, _ = line(face, tile, 0)
    buf[mine] = own[...]


def sum_finish(line, own, buf, send, recv):
    face, tile = place()
    _, _, device = line(face, tile, 1)
    arrived = buf.at[pl.ds(0, NZ - 1)]
    copies = remote(arrived, arrived, send, recv, *device)
    copies.wait_recv()
    total = buf[0]
    for i in range(1, NZ):
        total = total + buf[i]
    copies.wait_send()
    return total


SUM_SCRATCH = [
    pltpu.VMEM((2, C), F32),
    pltpu.VMEM((2, C), F32),
    pltpu.VMEM((NZ, 2, C), F32),
    pltpu.VMEM((NZ, 2, C), F32),
    DMA,
    DMA,
    DMA,
    DMA,
]

RIM = C + 128

HALO_SCRATCH = [
    pltpu.VMEM((2, FS, C), BF),
    pltpu.VMEM((2, CS, C), BF),
    pltpu.VMEM((SLOTS, 16, RIM), BF),
    pltpu.VMEM((SLOTS, 16, RIM), BF),
    pltpu.VMEM((SLOTS, 16, RIM), BF),
    pltpu.VMEM((SLOTS, 16, RIM), BF),
    pltpu.VMEM((32, C), F32),
    pltpu.VMEM((32, C), BF),
    pltpu.VMEM((NF, 32, C), BF),
    pltpu.VMEM((32, C), BF),
] + [DMA] * 10


class Halo:
    def __init__(self, fine, coarse, scratch, tables):
        self.fine, self.coarse = fine, coarse
        (
            self.hf,
            self.hc,
            self.rim,
            self.r1,
            self.st,
            self.r2,
            self.rows,
            self.srec,
            self.sall,
            self.sides,
            self.fs,
            self.fr,
            self.cs,
            self.cr,
            self.s1,
            self.q1,
            self.s2,
            self.q2,
            self.ss,
            self.sr,
        ) = scratch
        self.nb, self.ed = tables
        self.face, self.tile = place()
        self.slot = my_slot(self.face, self.tile)

    def rows_start(self):
        up = lax.rem(self.tile + 1, NT)
        down = lax.rem(self.tile + NT - 1, NT)
        for field, halo, send, recv in (
            (self.fine, self.hf, self.fs, self.fr),
            (self.coarse, self.hc, self.cs, self.cr),
        ):
            last = field.shape[0] - 1
            remote(field.at[last], halo.at[0], send, recv, self.face, up).start()
            remote(field.at[0], halo.at[1], send, recv, self.face, down).start()

    def rows_wait(self):
        up = lax.rem(self.tile + 1, NT)
        for halo, send, recv in ((self.hf, self.fs, self.fr), (self.hc, self.cs, self.cr)):
            both = remote(halo, halo, send, recv, self.face, up)
            both.wait_recv()
            both.wait_send()

    def rim_partner(self, step):
        other = lax.rem(self.slot + step, SLOTS)
        return other, slot_device(other)

    def rim_wait(self, buf, send, recv):
        _, device = self.rim_partner(1)
        arrived = buf.at[pl.ds(0, SLOTS - 1)]
        copies = remote(arrived, arrived, send, recv, *device)
        copies.wait_recv()
        copies.wait_send()

    def start(self):
        @pl.when(is_rim(self.tile))
        def _():
            fine_row = jnp.where(self.tile == 0, 0, RD - 1)
            coarse_row = jnp.where(self.tile == 0, 0, RD // 2 - 1)
            self.rim[:, :, 0:C] = self.fine[fine_row].reshape(SLOTS, 16, C)
            cells = self.coarse[coarse_row]
            self.rim[0:8, :, C:RIM] = cells[:, 0:128].reshape(8, 16, 128)
            self.rim[8:16, :, C:RIM] = cells[:, 128:256].reshape(8, 16, 128)

            @pl.loop(1, SLOTS)
            def _(step):
                other, device = self.rim_partner(step)
                remote(self.rim.at[other], self.r1.at[self.slot], self.s1, self.q1, *device).start()

            self.r1[self.slot] = self.rim[self.slot]

        self.rows_start()

    def middle(self):
        @pl.when(is_rim(self.tile))
        def _():
            self.rim_wait(self.r1, self.s1, self.q1)

            @pl.loop(0, SLOTS)
            def _(slot):
                face, edge = lax.div(slot, 2), 2 * lax.rem(slot, 2)
                source = 2 * self.nb[edge, face] + lax.div(self.ed[edge, face], 2)
                self.st[slot] = self.r1[source]

            @pl.loop(1, SLOTS)
            def _(step):
                other, device = self.rim_partner(step)
                remote(self.st.at[other], self.r2.at[self.slot], self.s2, self.q2, *device).start()

            self.r2[self.slot] = self.st[self.slot]

        self.rows_wait()
        fine_rows = [self.hf.at[0]] + [self.fine.at[r] for r in range(RD)] + [self.hf.at[1]]
        coarse_rows = [self.hc.at[0]] + [self.coarse.at[r] for r in range(RD // 2)]
        coarse_rows += [self.hc.at[1]]
        for i, row in enumerate(fine_rows + coarse_rows):
            side = row.shape[0]
            self.rows[i : i + 1, :] = row[0:16, :].astype(F32)[0:1]
            self.rows[16 + i : 17 + i, :] = row[side - 16 : side, :].astype(F32)[15:16]
        self.srec[...] = self.rows[...].astype(BF)

        @pl.loop(1, NF)
        def _(step):
            other = lax.rem(self.face + step, NF)
            remote(
                self.srec, self.sall.at[self.face], self.ss, self.sr, other, self.tile
            ).start()

        self.sall[self.face] = self.srec[...]

    def finish(self, flips):
        @pl.when(is_rim(self.tile))
        def _():
            self.rim_wait(self.r2, self.s2, self.q2)
            flip_top, flip_bottom = flips
            flip = jnp.where(self.tile == 0, flip_top, flip_bottom)
            edge = jnp.where(self.tile == 0, 0, 1)
            fine = self.r2[:, :, 0:C].reshape(FS, C)
            coarse = jnp.concatenate(
                [
                    self.r2[0:8, :, C:RIM].reshape(CS, 128),
                    self.r2[8:16, :, C:RIM].reshape(CS, 128),
                ],
                axis=1,
            )
            self.hf[edge] = dot(rim_matrix(FS, flip), fine).astype(BF)
            self.hc[edge] = dot(rim_matrix(CS, flip), coarse).astype(BF)

        other = lax.rem(self.face + 1, NF)
        arrived = self.sall.at[pl.ds(0, NF - 1)]
        copies = remote(arrived, arrived, self.ss, self.sr, other, self.tile)
        copies.wait_recv()
        copies.wait_send()
        left_face, right_face = self.nb[3, self.face], self.nb[1, self.face]
        self.sides[0:16, :] = self.sall[left_face, 16:32, :]
        self.sides[16:32, :] = self.sall[right_face, 0:16, :]


def iota(shape, dim):
    return lax.broadcasted_iota(jnp.int32, shape, dim)


def dot(a, b):
    return jnp.dot(a, b, preferred_element_type=F32)


def sigmoid(values):
    return 0.5 * jnp.tanh(0.5 * values) + 0.5


def pool_matrix():
    row, col = iota((CS, 2 * FS), 0), iota((CS, 2 * FS), 1)
    return jnp.where(lax.div(lax.rem(col, FS), 2) == row, 1.0, 0.0).astype(BF)


def spread_matrix():
    row, col = iota((FS, 2 * CS), 0), iota((FS, 2 * CS), 1)
    return jnp.where(lax.rem(col, CS) == lax.div(row, 2), 1.0, 0.0).astype(BF)


def spread(matrix, values):
    high = values.astype(BF)
    low = (values - high.astype(F32)).astype(BF)
    return dot(matrix, jnp.concatenate([high, low], axis=0))


def rim_matrix(side, flip):
    row, col = iota((side, side), 0), iota((side, side), 1)
    source = jnp.where(flip, side - 1 - row, row)
    return jnp.where(col == source, 1.0, 0.0).astype(BF)


def store_shifted(ref, row, values, left, right):
    n = values.shape[0]
    position = iota(values.shape, 0)
    before = jnp.where(position == 0, left, pltpu.roll(values, 1, 0))
    after = jnp.where(position == n - 1, right, pltpu.roll(values, n - 1, 0))
    ref[row, :, 0:C] = before.astype(BF)
    ref[row, :, C : 2 * C] = values.astype(BF)
    ref[row, :, 2 * C : 3 * C] = after.astype(BF)


def group_sum(values):
    lane = iota(values.shape, 1)
    for width in (1, 2, 4):
        up = pltpu.roll(values, width, 1)
        down = pltpu.roll(values, C - width, 1)
        values = values + jnp.where(lax.rem(lax.div(lane, width), 2) == 0, down, up)
    return values


def norm_vectors(total):
    grouped = group_sum(total) / (CELLS * GROUP)
    mean, second = grouped[0:1], grouped[1:2]
    return mean, lax.rsqrt(second - mean * mean + 1e-05)


def edge_flags(ed_ref):
    face, tile = place()
    first, last = tile == 0, tile == NT - 1
    flip_top = first & (ed_ref[0, face] != 2)
    flip_bottom = last & (ed_ref[2, face] != 0)
    return first, last, flip_top, flip_bottom


def masked_sides(sides, first, last):
    row = lax.rem(iota(sides.shape, 0), 16)
    top = (row == 0) | (row == RD + 2)
    bottom = (row == RD + 1) | (row == 15)
    zero = (top & first) | (bottom & last)
    return jnp.where(zero, 0.0, sides)


def back_weights(w_ref, out_ref):
    for k in range(3):
        for m in range(3):
            tap = w_ref[8 - (3 * k + m)].astype(F32)
            out_ref[k, m * C : (m + 1) * C, :] = tap.T.astype(BF)


def halo_weights(wt_ref, flip_top, flip_bottom):
    def turned(k):
        return jnp.concatenate(
            [wt_ref[k, (2 - m) * C : (3 - m) * C, :] for m in range(3)], axis=0
        )

    top = jnp.where(flip_top, turned(2), wt_ref[0])
    bottom = jnp.where(flip_bottom, turned(0), wt_ref[2])
    return top, bottom


def rows_of(ref, start, count):
    _, side, width = ref.shape
    return ref[pl.ds(start, count)].reshape(count * side, width)


def taps_of(ref, k):
    return ref[3 * k : 3 * k + 3].reshape(3 * C, C)


SHARE = 144
NC = 16


def put_share(shares, tap, product):
    turned = product.T.reshape(4, 4, 2, 8, C)
    halves = [turned[..., :128], turned[..., 128:]]
    shares[:, :, :, 16 * tap : 16 * tap + 16, :] = jnp.concatenate(halves, axis=3).astype(BF)


def put_grads(out, total):
    total = (total * (1.0 / CELLS)).reshape(9, 2, 8, 128)
    out[:, :, 0:128] = total[:, 0]
    out[:, :, 128:256] = total[:, 1]


def tree(parts):
    parts = [part.astype(F32) for part in parts]
    while len(parts) > 1:
        parts = [sum(parts[i : i + 2]) for i in range(0, len(parts), 2)]
    return parts[0]


CUT = 80
LANES = ((0, CUT), (CUT, SHARE - CUT))

REDUCE_SCRATCH = [
    pltpu.VMEM((4, 4, 2, SHARE, 128), BF),
    pltpu.VMEM((4, 4, SHARE, 128), BF),
    pltpu.VMEM((4, 4, SHARE, 128), BF),
    pltpu.VMEM((2, 4, CUT, 128), BF),
    pltpu.VMEM((2, 4, SHARE - CUT, 128), BF),
    pltpu.VMEM((4, CUT, 128), BF),
    pltpu.VMEM((4, SHARE - CUT, 128), BF),
    pltpu.VMEM((4, CUT, 128), BF),
    pltpu.VMEM((4, SHARE - CUT, 128), BF),
    pltpu.VMEM((4, SHARE, 128), BF),
    pltpu.VMEM((NC, SHARE, 128), BF),
    pltpu.VMEM((SHARE, 128), BF),
    pltpu.VMEM((2, SHARE, 128), BF),
    DMA((3,)),
    DMA((3,)),
    DMA((2,)),
    DMA((2,)),
    DMA((2,)),
    DMA((2,)),
    DMA((4,)),
    DMA,
    DMA,
    DMA((2,)),
]


class Reduce:
    def __init__(self, scratch):
        (
            self.shares,
            self.got,
            self.part,
            r0,
            r1,
            t0,
            t1,
            u0,
            u1,
            self.px,
            self.rz,
            self.block,
            self.rb,
            self.s0,
            self.q0,
            self.sa,
            self.qa,
            self.sc,
            self.qc,
            self.sz,
            self.qz,
            self.sb,
            self.qb,
        ) = scratch
        self.one, self.on, self.two = (r0, r1), (t0, t1), (u0, u1)
        self.face, self.tile = place()
        self.core, self.chip = lax.rem(self.tile, 2), lax.div(self.tile, 2)
        self.x, self.high = lax.div(self.face, 2), lax.rem(self.face, 2)
        self.home = lax.rem(self.chip, 4)
        self.owner = self.home == self.x
        near = self.x + 1 - 2 * lax.rem(self.x, 2)
        self.partner = (near, 3 - self.x)

    def swap(self, k):
        rows = pl.ds(48 * k, 48)
        return remote(
            self.shares.at[:, :, 1 - self.core, rows, :],
            self.got.at[:, :, rows, :],
            self.s0.at[k],
            self.q0.at[k],
            self.face,
            self.tile + 1 - 2 * self.core,
        )

    def swap_start(self, k):
        self.swap(k).start()

    def across(self, way, src, dst, send, recv):
        return remote(src, dst, send, recv, 2 * self.partner[way] + self.high, self.tile)

    def first(self, way, i):
        other = self.partner[way]
        beyond = 3 - other if way == 0 else other + 1 - 2 * lax.rem(other, 2)
        start, rows = LANES[way]
        return self.across(
            way,
            self.part.at[:, (other, beyond)[i], pl.ds(start, rows), :],
            self.one[way].at[i],
            self.sa.at[way],
            self.qa.at[way],
        )

    def first_wait(self, way):
        return self.across(way, self.one[way], self.one[way], self.sa.at[way], self.qa.at[way])

    def second(self, way):
        return self.across(1 - way, self.on[way], self.two[way], self.sc.at[way], self.qc.at[way])

    def swap_take(self):
        for k in range(3):
            self.swap(k).wait_recv()

        @pl.loop(0, 4)
        def _(j):
            for h in range(4):
                both = self.shares[j, h, self.core].astype(F32) + self.got[j, h].astype(F32)
                self.part[j, h] = both.astype(BF)

        for way in range(2):
            for i in range(2):
                self.first(way, i).start()

    def first_take(self):
        for way in range(2):
            self.first_wait(way).wait_recv()
            start, rows = LANES[way]
            span = pl.ds(start, rows)
            mine = self.part[:, self.partner[1 - way], span, :].astype(F32)
            self.on[way][...] = (mine + self.one[way][1].astype(F32)).astype(BF)
            self.second(way).start()

    def second_take(self):
        for way in range(2):
            self.second(way).wait_recv()
            start, rows = LANES[way]
            mine = self.part[:, self.x, pl.ds(start, rows), :].astype(F32)
            total = mine + self.one[way][0].astype(F32) + self.two[way][...].astype(F32)
            self.px[:, start : start + rows, :] = total.astype(BF)

        @pl.loop(0, 4)
        def _(j):
            mine = 4 * j + self.x == self.chip

            @pl.when(jnp.logical_not(mine))
            def _():
                self.scatter(j).start()

            @pl.when(mine)
            def _():
                self.rz[self.chip] = self.px[j]

    def scatter(self, j):
        return remote(
            self.px.at[j],
            self.rz.at[self.chip],
            self.sz.at[j],
            self.qz,
            self.face,
            2 * (4 * j + self.x) + self.core,
        )

    def share(self, other):
        return remote(
            self.block, self.rb.at[self.high], self.sb, self.qb.at[self.high], other, self.tile
        )

    def chips_take(self):
        @pl.when(self.owner)
        def _():
            arrived = self.rz.at[pl.ds(0, NC - 1)]
            other = lax.rem(self.chip + 1, NC)
            remote(
                arrived, arrived, self.sb, self.qz, self.face, 2 * other + self.core
            ).wait_recv()
            self.block[...] = tree([self.rz[j] for j in range(NC)]).astype(BF)

            @pl.loop(1, NF)
            def _(step):
                self.share(lax.rem(self.face + step, NF)).start()

            self.rb[self.high] = self.block[...]

    def finish(self, out):
        for high in range(2):
            source = 2 * self.home + high

            @pl.when(source != self.face)
            def _():
                remote(
                    self.block, self.rb.at[high], self.sb, self.qb.at[high], source, self.tile
                ).wait_recv()

        put_grads(out, tree([self.rb[0], self.rb[1]]))

        for k in range(3):
            self.swap(k).wait_send()
        for way in range(2):
            self.first_wait(way).wait_send()
            self.second(way).wait_send()

        @pl.loop(0, 4)
        def _(j):
            @pl.when(4 * j + self.x != self.chip)
            def _():
                self.scatter(j).wait_send()

        @pl.when(self.owner)
        def _():
            sent = self.rz.at[pl.ds(0, NF - 1)]
            remote(
                sent, sent, self.sb, self.qz, lax.rem(self.face + 1, NF), self.tile
            ).wait_send()


HALF = RD // 2
N_SUM, N_HALO = len(SUM_SCRATCH), len(HALO_SCRATCH)

ANY = pl.BlockSpec(memory_space=pl.ANY)

WORK_SCRATCH = [
    pltpu.SMEM((4, NF), jnp.int32),
    pltpu.SMEM((4, NF), jnp.int32),
    pltpu.VMEM((9, C, C), BF),
    pltpu.VMEM((9, C, C), BF),
    pltpu.VMEM((HALF, CS, C), BF),
    pltpu.VMEM((3, 3 * C, C), BF),
    pltpu.VMEM((3, 3 * C, C), BF),
    pltpu.VMEM((RD + 2, FS, 3 * C), BF),
    pltpu.VMEM((RD + 2, FS, 3 * C), BF),
    pltpu.VMEM((HALF + 2, CS, 3 * C), BF),
    pltpu.VMEM((HALF + 2, CS, 3 * C), BF),
    pltpu.VMEM((RD, FS, C), BF),
    pltpu.VMEM((HALF, CS, C), BF),
    pltpu.VMEM((RD, FS, C), BF),
    pltpu.VMEM((RD, FS, C), F32),
    pltpu.VMEM((HALF, CS, C), F32),
    pltpu.VMEM((C, RD * FS), BF),
    pltpu.VMEM((C, HALF * CS), BF),
    pltpu.VMEM((32, C), F32),
    pltpu.VMEM((32, C), F32),
    DMA((6,)),
]


def extended(ref3, field, halo, edge, first, side):
    rows = field.shape[0]

    def put(i, row):
        left, right = edge[pl.ds(first + i, 1), :], edge[pl.ds(first + i + 16, 1), :]
        store_shifted(ref3, i, side(row.astype(F32)), left, right)

    put(0, halo[0])
    put(rows + 1, halo[1])

    @pl.loop(0, rows)
    def _(r):
        put(r + 1, field[r])


def whole_kernel(
    feat, cot, wf_any, wc_any, gain, nb_any, ed_any,
    output, grad_act, grad_w_fine, grad_w_coarse, grad_gain, vectors, *scratch
):
    scratch = list(scratch)

    def take(n):
        got = scratch[:n]
        del scratch[:n]
        return got

    own_a, own_b, buf_a, buf_b, sa, ra, sb, rb = take(N_SUM)
    own_c, own_d, buf_c, buf_d, sc, rc, sd, rd = take(N_SUM)
    halo1_scratch, halo2_scratch = take(N_HALO), take(N_HALO)
    (
        nb, ed, wf_taps, wc_taps, gco, wtf, wtc, x3, u3, c3, v3, fine, coarse_in, grad_fine,
        ga, gci, gt, gct, edge_h, edge_c, local,
    ) = take(len(WORK_SCRATCH))
    reduce_f = Reduce(take(len(REDUCE_SCRATCH)))
    reduce_c = Reduce(take(len(REDUCE_SCRATCH)))

    barrier_signal()
    loads = [
        pltpu.make_async_copy(src, dst, local.at[i])
        for i, (src, dst) in enumerate(
            ((nb_any, nb), (ed_any, ed), (wf_any, wf_taps), (wc_any, wc_taps))
        )
    ]
    for load in loads:
        load.start()
    halo1 = Halo(feat, gco, halo1_scratch, (nb, ed))
    halo2 = Halo(grad_fine, coarse_in, halo2_scratch, (nb, ed))

    pool, widen = pool_matrix(), spread_matrix()
    own_a[...] = jnp.zeros_like(own_a)
    own_c[...] = jnp.zeros_like(own_c)

    @pl.loop(0, HALF)
    def _(i):
        gco[i] = dot(pool, rows_of(cot, 2 * i, 2)).astype(BF)
        values = rows_of(feat, 2 * i, 2).astype(F32)
        own_a[0:1, :] += jnp.sum(values, axis=0, keepdims=True)
        own_a[1:2, :] += jnp.sum(values * values, axis=0, keepdims=True)

    barrier_wait()
    sum_start(line_a, own_a, buf_a, sa, ra)
    halo1.start()
    for load in loads:
        load.wait()
    back_weights(wc_taps, wtc)
    own_b[...] = sum_finish(line_a, own_a, buf_a, sa, ra)
    sum_start(line_b, own_b, buf_b, sb, rb)
    halo1.middle()
    back_weights(wf_taps, wtf)
    for r in range(HALF):
        gct[:, r * CS : (r + 1) * CS] = gco[r].astype(F32).T.astype(BF)

    first, last, flip_top, flip_bottom = edge_flags(ed)
    halo1.finish((flip_top, flip_bottom))
    edge_c[...] = masked_sides(halo1.sides[...].astype(F32), first, last)

    extended(v3, gco, halo1.hc, edge_c, RD + 2, lambda row: row)
    top, bottom = halo_weights(wtc, flip_top, flip_bottom)
    gci[...] = dot(rows_of(v3, 1, HALF), wtc[1]).reshape(HALF, CS, C)
    gci[1:HALF] += dot(rows_of(v3, 1, HALF - 1), wtc[0]).reshape(HALF - 1, CS, C)
    gci[0 : HALF - 1] += dot(rows_of(v3, 2, HALF - 1), wtc[2]).reshape(HALF - 1, CS, C)
    gci[0] += dot(v3[0], top)
    gci[HALF - 1] += dot(v3[HALF + 1], bottom)

    total = sum_finish(line_b, own_b, buf_b, sb, rb)
    mean, inverse = norm_vectors(total)
    scale = gain[...]

    def hidden(raw):
        act = (raw - mean) * inverse * scale
        return (act * sigmoid(act)).astype(BF).astype(F32)

    edge_h[...] = masked_sides(hidden(halo1.sides[...].astype(F32)), first, last)
    extended(x3, feat, halo1.hf, edge_h, 0, hidden)

    def forward(i):
        acc = dot(rows_of(x3, 2 * i, 2), taps_of(wf_taps, 0))
        acc += dot(rows_of(x3, 2 * i + 1, 2), taps_of(wf_taps, 1))
        acc += dot(rows_of(x3, 2 * i + 2, 2), taps_of(wf_taps, 2))
        out = acc.astype(BF)
        fine[pl.ds(2 * i, 2)] = out.reshape(2, FS, C)
        pooled = 0.25 * dot(pool, out)
        gate = sigmoid(pooled)
        coarse_in[i] = (pooled * gate).astype(BF)
        slope = gate * (1.0 + pooled * (1.0 - gate))
        wide = spread(widen, gci[i] * slope * 0.25)
        for r in range(2):
            grad_fine[2 * i + r] = (cot[2 * i + r].astype(F32) + wide).astype(BF)

    @pl.loop(0, 2)
    def _(i):
        forward((HALF - 1) * i)

    halo2.start()
    pl.loop(1, HALF - 1)(forward)

    def fine_gradient(k):
        product = dot(gt[...], rows_of(x3, k, RD))
        for m in range(3):
            put_share(reduce_f.shares, 3 * k + m, product[:, m * C : (m + 1) * C])
        reduce_f.swap_start(k)

    for r in range(RD):
        gt[:, r * FS : (r + 1) * FS] = grad_fine[r].astype(F32).T.astype(BF)
    halo2.middle()
    for k in range(3):
        fine_gradient(k)
    halo2.finish((flip_top, flip_bottom))
    edge_h[...] = masked_sides(halo2.sides[...].astype(F32), first, last)
    reduce_f.swap_take()

    extended(c3, coarse_in, halo2.hc, edge_h, RD + 2, lambda row: row)
    for k in range(3):
        product = dot(gct[...], rows_of(c3, k, HALF))
        for m in range(3):
            put_share(reduce_c.shares, 3 * k + m, product[:, m * C : (m + 1) * C])
        reduce_c.swap_start(k)
    reduce_f.first_take()

    extended(u3, grad_fine, halo2.hf, edge_h, 0, lambda row: row)
    top, bottom = halo_weights(wtf, flip_top, flip_bottom)
    reduce_c.swap_take()
    ga[1 : RD - 1] = jnp.zeros((RD - 2, FS, C), F32)
    ga[0] = dot(u3[0], top)
    ga[RD - 1] = dot(u3[RD + 1], bottom)
    u3[0] = jnp.zeros((FS, 3 * C), BF)
    u3[RD + 1] = jnp.zeros((FS, 3 * C), BF)

    def back(i):
        grad = dot(rows_of(u3, 2 * i, 2), wtf[0])
        grad += dot(rows_of(u3, 2 * i + 1, 2), wtf[1])
        grad += dot(rows_of(u3, 2 * i + 2, 2), wtf[2])
        grad += rows_of(ga, 2 * i, 2)
        normed = (rows_of(feat, 2 * i, 2).astype(F32) - mean) * inverse
        act = normed * scale
        gate = sigmoid(act)
        grad = grad * (gate * (1.0 + act * (1.0 - gate)))
        ga[pl.ds(2 * i, 2)] = grad.reshape(2, FS, C)
        own_c[0:1, :] += jnp.sum(grad * normed, axis=0, keepdims=True)
        own_c[1:2, :] += jnp.sum(grad, axis=0, keepdims=True)

    pl.loop(0, HALF // 2)(back)
    reduce_f.second_take()
    reduce_c.first_take()
    pl.loop(HALF // 2, HALF)(back)
    sum_start(line_a, own_c, buf_c, sc, rc)
    store_act = pltpu.make_async_copy(ga, grad_act, local.at[4])
    store_act.start()
    reduce_c.second_take()

    @pl.loop(0, HALF)
    def _(i):
        out = dot(c3[i], taps_of(wc_taps, 0))
        out += dot(c3[i + 1], taps_of(wc_taps, 1))
        out += dot(c3[i + 2], taps_of(wc_taps, 2))
        wide = spread(widen, out)
        for r in range(2):
            fine[2 * i + r] = (fine[2 * i + r].astype(F32) + wide).astype(BF)

    store_output = pltpu.make_async_copy(fine, output, local.at[5])
    store_output.start()
    own_d[...] = sum_finish(line_a, own_c, buf_c, sc, rc)
    sum_start(line_b, own_d, buf_d, sd, rd)
    reduce_f.chips_take()
    reduce_c.chips_take()
    sums = sum_finish(line_b, own_d, buf_d, sd, rd)

    grad_gain[...] = sums[0:1] * (1.0 / CELLS)
    grouped = group_sum(sums * scale) / (CELLS * GROUP)
    group_slope, group_shift = grouped[0:1], grouped[1:2]
    for i, vector in enumerate((mean, inverse, scale, group_shift, group_slope)):
        vectors[i : i + 1, :] = vector
    reduce_f.finish(grad_w_fine)
    reduce_c.finish(grad_w_coarse)
    store_act.wait()
    store_output.wait()


def last_kernel(
    feat, ga, vectors, wf_in, wc_in, gain_in, output_in,
    output, grad_features, wf_out, wc_out, gain_out, feat_v, ga_v, sum_v, out_v, sems
):
    def rows(ref, q):
        return ref.at[pl.ds(2 * q, 2)]

    def moves(pairs, first):
        return [
            [
                pltpu.make_async_copy(rows(src, q), rows(dst, q), sems.at[first + i, q])
                for i, (src, dst) in enumerate(pairs)
            ]
            for q in range(HALF)
        ]

    loads = moves(((feat, feat_v), (ga, ga_v), (output_in, sum_v)), 0)
    stores = moves(((out_v, grad_features), (sum_v, output)), 3)
    for chunk in loads:
        for copy in chunk:
            copy.start()
    wf_out[...] = wf_in[...]
    wc_out[...] = wc_in[...]
    gain_out[...] = gain_in[...]
    mean, inverse, scale = vectors[0:1], vectors[1:2], vectors[2:3]
    group_shift, group_slope = vectors[3:4], vectors[4:5]
    for q in range(HALF):
        for copy in loads[q]:
            copy.wait()
        for r in (2 * q, 2 * q + 1):
            normed = (feat_v[r].astype(F32) - mean) * inverse
            out_v[r] = inverse * (scale * ga_v[r] - group_shift - normed * group_slope)
        for copy in stores[q]:
            copy.start()
    for chunk in stores:
        for copy in chunk:
            copy.wait()


def shape(dims, dtype):
    return jax.ShapeDtypeStruct(dims, dtype)


def on_device(features, cotangent, w_fine, w_coarse, gain, neighbors, neighbor_edges):
    outs = [
        shape((RD, FS, C), BF),
        shape((RD, FS, C), F32),
        shape((9, 8, C), F32),
        shape((9, 8, C), F32),
        shape((1, C), F32),
    ]
    output, grad_act, grad_w_fine, grad_w_coarse, grad_gain, vectors = pl.pallas_call(
        whole_kernel,
        in_specs=[VM, VM, ANY, ANY, VM, ANY, ANY],
        out_specs=[ANY, ANY, VM, VM, VM, VM],
        out_shape=outs + [shape((8, C), F32)],
        scratch_shapes=SUM_SCRATCH * 2
        + HALO_SCRATCH * 2
        + WORK_SCRATCH
        + REDUCE_SCRATCH * 2,
        compiler_params=pltpu.CompilerParams(
            vmem_limit_bytes=VMEM_LIMIT, collective_id=1, has_side_effects=True
        ),
    )(features[0], cotangent[0], w_fine, w_coarse, gain[None], neighbors.T, neighbor_edges.T)
    output, grad_features, grad_w_fine, grad_w_coarse, grad_gain = pl.pallas_call(
        last_kernel,
        in_specs=[ANY, ANY] + [VM] * 4 + [ANY],
        out_specs=[ANY, ANY] + [VM] * 3,
        out_shape=outs,
        scratch_shapes=[
            pltpu.VMEM((RD, FS, C), BF),
            pltpu.VMEM((RD, FS, C), F32),
            pltpu.VMEM((RD, FS, C), BF),
            pltpu.VMEM((RD, FS, C), F32),
            DMA((5, HALF)),
        ],
        compiler_params=pltpu.CompilerParams(vmem_limit_bytes=VMEM_LIMIT),
    )(features[0], grad_act, vectors, grad_w_fine, grad_w_coarse, grad_gain, output)
    return (output[None], grad_features[None], grad_w_fine, grad_w_coarse, grad_gain[0])


def solution(mesh):
    return jax.shard_map(
        on_device,
        mesh=mesh,
        in_specs=(
            P("face", "tile", None, None),
            P("face", "tile", None, None),
            P(),
            P(),
            P(),
            P(),
            P(),
        ),
        out_specs=(
            P("face", "tile", None, None),
            P("face", "tile", None, None),
            P(None, "tile", None),
            P(None, "tile", None),
            P(),
        ),
        check_vma=False,
    )
```

```python
import jax
import jax.numpy as jnp
from jax import lax
from jax.experimental import pallas as pl
from jax.experimental.pallas import tpu as pltpu
from jax.sharding import PartitionSpec as P

BF = jnp.bfloat16
F32 = jnp.float32
MESH = pl.DeviceIdType.MESH
NF = 8
NT = 32
NZ = 16
RD = 8
FS = 256
CS = 128
C = 256
GROUP = 8
SLOTS = 16
CELLS = NF * FS * FS
VMEM_LIMIT = 60 * 1024 * 1024

VM = pl.BlockSpec(memory_space=pltpu.VMEM)
SM = pl.BlockSpec(memory_space=pltpu.SMEM)
DMA = pltpu.SemaphoreType.DMA


def remote(src, dst, send, recv, face, tile):
    return pltpu.make_async_remote_copy(
        src_ref=src,
        dst_ref=dst,
        send_sem=send,
        recv_sem=recv,
        device_id=(face, tile),
        device_id_type=MESH,
    )


def place():
    return lax.axis_index("face"), lax.axis_index("tile")


def is_rim(tile):
    return (tile == 0) | (tile == NT - 1)


def slot_device(slot):
    return lax.div(slot, 2), (NT - 1) * lax.rem(slot, 2)


def my_slot(face, tile):
    return 2 * face + jnp.where(tile == NT - 1, 1, 0)


def multiple(value, of):
    return pl.multiple_of(value * of, of)


def signal(barrier, face, tile):
    pl.semaphore_signal(barrier, inc=1, device_id=(face, tile), device_id_type=MESH)


def line_a(face, tile, step):
    mine = lax.rem(tile, NZ)
    other = lax.rem(mine + step, NZ)
    return mine, other, (face, tile - mine + other)


def line_b(face, tile, step):
    mine = face * 2 + lax.div(tile, NZ)
    other = lax.rem(mine + step, 2 * NF)
    return mine, other, (lax.div(other, 2), lax.rem(other, 2) * NZ + lax.rem(tile, NZ))


def barrier_signal():
    face, tile = place()
    barrier = pltpu.get_barrier_semaphore()
    across = lax.rem(tile + NZ, NT)
    across = across - lax.rem(across, NZ) + lax.rem(tile, 2)

    @pl.loop(1, NZ)
    def _(step):
        for line in (line_a, line_b):
            _, _, device = line(face, tile, step)
            signal(barrier, *device)

    @pl.loop(0, NZ // 2)
    def _(z):
        signal(barrier, face, across + 2 * z)

    signal(barrier, face, lax.rem(tile + 1, NT))
    signal(barrier, face, lax.rem(tile + NT - 1, NT))

    @pl.when(is_rim(tile))
    def _():
        mine = my_slot(face, tile)

        @pl.loop(1, SLOTS)
        def _(step):
            signal(barrier, *slot_device(lax.rem(mine + step, SLOTS)))


def barrier_wait():
    _, tile = place()
    barrier = pltpu.get_barrier_semaphore()
    count = 2 * (NZ - 1) + NZ // 2 + 2

    @pl.when(is_rim(tile))
    def _():
        pl.semaphore_wait(barrier, count + SLOTS - 1)

    @pl.when(~is_rim(tile))
    def _():
        pl.semaphore_wait(barrier, count)


def sum_start(line, own, buf, send, recv):
    face, tile = place()

    @pl.loop(1, NZ)
    def _(step):
        mine, _, device = line(face, tile, step)
        remote(own, buf.at[mine], send, recv, *device).start()

    mine, _, _ = line(face, tile, 0)
    buf[mine] = own[...]


def sum_finish(line, own, buf, send, recv):
    face, tile = place()
    _, _, device = line(face, tile, 1)
    arrived = buf.at[pl.ds(0, NZ - 1)]
    copies = remote(arrived, arrived, send, recv, *device)
    copies.wait_recv()
    total = buf[0]
    for i in range(1, NZ):
        total = total + buf[i]
    copies.wait_send()
    return total


SUM_SCRATCH = [
    pltpu.VMEM((2, C), F32),
    pltpu.VMEM((2, C), F32),
    pltpu.VMEM((NZ, 2, C), F32),
    pltpu.VMEM((NZ, 2, C), F32),
    DMA,
    DMA,
    DMA,
    DMA,
]

RIM = C + 128

HALO_SCRATCH = [
    pltpu.VMEM((2, FS, C), BF),
    pltpu.VMEM((2, CS, C), BF),
    pltpu.VMEM((SLOTS, 16, RIM), BF),
    pltpu.VMEM((SLOTS, 16, RIM), BF),
    pltpu.VMEM((SLOTS, 16, RIM), BF),
    pltpu.VMEM((SLOTS, 16, RIM), BF),
    pltpu.VMEM((32, C), F32),
    pltpu.VMEM((32, C), BF),
    pltpu.VMEM((NF, 32, C), BF),
    pltpu.VMEM((32, C), BF),
] + [DMA] * 10


class Halo:
    def __init__(self, fine, coarse, scratch, tables):
        self.fine, self.coarse = fine, coarse
        (
            self.hf,
            self.hc,
            self.rim,
            self.r1,
            self.st,
            self.r2,
            self.rows,
            self.srec,
            self.sall,
            self.sides,
            self.fs,
            self.fr,
            self.cs,
            self.cr,
            self.s1,
            self.q1,
            self.s2,
            self.q2,
            self.ss,
            self.sr,
        ) = scratch
        self.nb, self.ed = tables
        self.face, self.tile = place()
        self.slot = my_slot(self.face, self.tile)

    def rows_start(self):
        up = lax.rem(self.tile + 1, NT)
        down = lax.rem(self.tile + NT - 1, NT)
        for field, halo, send, recv in (
            (self.fine, self.hf, self.fs, self.fr),
            (self.coarse, self.hc, self.cs, self.cr),
        ):
            last = field.shape[0] - 1
            remote(field.at[last], halo.at[0], send, recv, self.face, up).start()
            remote(field.at[0], halo.at[1], send, recv, self.face, down).start()

    def rows_wait(self):
        up = lax.rem(self.tile + 1, NT)
        for halo, send, recv in ((self.hf, self.fs, self.fr), (self.hc, self.cs, self.cr)):
            both = remote(halo, halo, send, recv, self.face, up)
            both.wait_recv()
            both.wait_send()

    def rim_partner(self, step):
        other = lax.rem(self.slot + step, SLOTS)
        return other, slot_device(other)

    def rim_wait(self, buf, send, recv):
        _, device = self.rim_partner(1)
        arrived = buf.at[pl.ds(0, SLOTS - 1)]
        copies = remote(arrived, arrived, send, recv, *device)
        copies.wait_recv()
        copies.wait_send()

    def start(self):
        @pl.when(is_rim(self.tile))
        def _():
            fine_row = jnp.where(self.tile == 0, 0, RD - 1)
            coarse_row = jnp.where(self.tile == 0, 0, RD // 2 - 1)
            self.rim[:, :, 0:C] = self.fine[fine_row].reshape(SLOTS, 16, C)
            cells = self.coarse[coarse_row]
            self.rim[0:8, :, C:RIM] = cells[:, 0:128].reshape(8, 16, 128)
            self.rim[8:16, :, C:RIM] = cells[:, 128:256].reshape(8, 16, 128)

            @pl.loop(1, SLOTS)
            def _(step):
                other, device = self.rim_partner(step)
                remote(self.rim.at[other], self.r1.at[self.slot], self.s1, self.q1, *device).start()

            self.r1[self.slot] = self.rim[self.slot]

        self.rows_start()

    def middle(self):
        @pl.when(is_rim(self.tile))
        def _():
            self.rim_wait(self.r1, self.s1, self.q1)

            @pl.loop(0, SLOTS)
            def _(slot):
                face, edge = lax.div(slot, 2), 2 * lax.rem(slot, 2)
                source = 2 * self.nb[edge, face] + lax.div(self.ed[edge, face], 2)
                self.st[slot] = self.r1[source]

            @pl.loop(1, SLOTS)
            def _(step):
                other, device = self.rim_partner(step)
                remote(self.st.at[other], self.r2.at[self.slot], self.s2, self.q2, *device).start()

            self.r2[self.slot] = self.st[self.slot]

        self.rows_wait()
        fine_rows = [self.hf.at[0]] + [self.fine.at[r] for r in range(RD)] + [self.hf.at[1]]
        coarse_rows = [self.hc.at[0]] + [self.coarse.at[r] for r in range(RD // 2)]
        coarse_rows += [self.hc.at[1]]
        for i, row in enumerate(fine_rows + coarse_rows):
            side = row.shape[0]
            self.rows[i : i + 1, :] = row[0:16, :].astype(F32)[0:1]
            self.rows[16 + i : 17 + i, :] = row[side - 16 : side, :].astype(F32)[15:16]
        self.srec[...] = self.rows[...].astype(BF)

        @pl.loop(1, NF)
        def _(step):
            other = lax.rem(self.face + step, NF)
            remote(
                self.srec, self.sall.at[self.face], self.ss, self.sr, other, self.tile
            ).start()

        self.sall[self.face] = self.srec[...]

    def finish(self, flips):
        @pl.when(is_rim(self.tile))
        def _():
            self.rim_wait(self.r2, self.s2, self.q2)
            flip_top, flip_bottom = flips
            flip = jnp.where(self.tile == 0, flip_top, flip_bottom)
            edge = jnp.where(self.tile == 0, 0, 1)
            fine = self.r2[:, :, 0:C].reshape(FS, C)
            coarse = jnp.concatenate(
                [
                    self.r2[0:8, :, C:RIM].reshape(CS, 128),
                    self.r2[8:16, :, C:RIM].reshape(CS, 128),
                ],
                axis=1,
            )
            self.hf[edge] = dot(rim_matrix(FS, flip), fine).astype(BF)
            self.hc[edge] = dot(rim_matrix(CS, flip), coarse).astype(BF)

        other = lax.rem(self.face + 1, NF)
        arrived = self.sall.at[pl.ds(0, NF - 1)]
        copies = remote(arrived, arrived, self.ss, self.sr, other, self.tile)
        copies.wait_recv()
        copies.wait_send()
        left_face, right_face = self.nb[3, self.face], self.nb[1, self.face]
        self.sides[0:16, :] = self.sall[left_face, 16:32, :]
        self.sides[16:32, :] = self.sall[right_face, 0:16, :]


def iota(shape, dim):
    return lax.broadcasted_iota(jnp.int32, shape, dim)


def dot(a, b):
    return jnp.dot(a, b, preferred_element_type=F32)


def sigmoid(values):
    return 0.5 * jnp.tanh(0.5 * values) + 0.5


def pool_matrix():
    row, col = iota((CS, 2 * FS), 0), iota((CS, 2 * FS), 1)
    return jnp.where(lax.div(lax.rem(col, FS), 2) == row, 1.0, 0.0).astype(BF)


def spread_matrix():
    row, col = iota((FS, 2 * CS), 0), iota((FS, 2 * CS), 1)
    return jnp.where(lax.rem(col, CS) == lax.div(row, 2), 1.0, 0.0).astype(BF)


def spread(matrix, values):
    high = values.astype(BF)
    low = (values - high.astype(F32)).astype(BF)
    return dot(matrix, jnp.concatenate([high, low], axis=0))


def rim_matrix(side, flip):
    row, col = iota((side, side), 0), iota((side, side), 1)
    source = jnp.where(flip, side - 1 - row, row)
    return jnp.where(col == source, 1.0, 0.0).astype(BF)


def store_shifted(ref, row, values, left, right):
    n = values.shape[0]
    position = iota(values.shape, 0)
    before = jnp.where(position == 0, left, pltpu.roll(values, 1, 0))
    after = jnp.where(position == n - 1, right, pltpu.roll(values, n - 1, 0))
    ref[row, :, 0:C] = before.astype(BF)
    ref[row, :, C : 2 * C] = values.astype(BF)
    ref[row, :, 2 * C : 3 * C] = after.astype(BF)


def group_sum(values):
    lane = iota(values.shape, 1)
    for width in (1, 2, 4):
        up = pltpu.roll(values, width, 1)
        down = pltpu.roll(values, C - width, 1)
        values = values + jnp.where(lax.rem(lax.div(lane, width), 2) == 0, down, up)
    return values


def norm_vectors(total):
    grouped = group_sum(total) / (CELLS * GROUP)
    mean, second = grouped[0:1], grouped[1:2]
    return mean, lax.rsqrt(second - mean * mean + 1e-05)


def edge_flags(ed_ref):
    face, tile = place()
    first, last = tile == 0, tile == NT - 1
    flip_top = first & (ed_ref[0, face] != 2)
    flip_bottom = last & (ed_ref[2, face] != 0)
    return first, last, flip_top, flip_bottom


def masked_sides(sides, first, last):
    row = lax.rem(iota(sides.shape, 0), 16)
    top = (row == 0) | (row == RD + 2)
    bottom = (row == RD + 1) | (row == 15)
    zero = (top & first) | (bottom & last)
    return jnp.where(zero, 0.0, sides)


def back_weights(w_ref, out_ref):
    for k in range(3):
        for m in range(3):
            tap = w_ref[8 - (3 * k + m)].astype(F32)
            out_ref[k, m * C : (m + 1) * C, :] = tap.T.astype(BF)


def halo_weights(wt_ref, flip_top, flip_bottom):
    def turned(k):
        return jnp.concatenate(
            [wt_ref[k, (2 - m) * C : (3 - m) * C, :] for m in range(3)], axis=0
        )

    top = jnp.where(flip_top, turned(2), wt_ref[0])
    bottom = jnp.where(flip_bottom, turned(0), wt_ref[2])
    return top, bottom


def rows_of(ref, start, count):
    _, side, width = ref.shape
    return ref[pl.ds(start, count)].reshape(count * side, width)


def taps_of(ref, k):
    return ref[3 * k : 3 * k + 3].reshape(3 * C, C)


SHARE = 144
NC = 16


def put_share(shares, tap, product):
    cut = product.reshape(4, 4, 2, 8, C)
    halves = [cut[..., :128], cut[..., 128:]]
    shares[:, :, :, 16 * tap : 16 * tap + 16, :] = jnp.concatenate(halves, axis=3).astype(BF)


def put_grads(out, total):
    total = (total * (1.0 / CELLS)).reshape(9, 2, 8, 128)
    out[:, :, 0:128] = total[:, 0]
    out[:, :, 128:256] = total[:, 1]


def tree(parts):
    parts = [part.astype(F32) for part in parts]
    while len(parts) > 1:
        parts = [sum(parts[i : i + 2]) for i in range(0, len(parts), 2)]
    return parts[0]


CUT = 80
LANES = ((0, CUT), (CUT, SHARE - CUT))

REDUCE_SCRATCH = [
    pltpu.VMEM((4, 4, 2, SHARE, 128), BF),
    pltpu.VMEM((4, 4, SHARE, 128), BF),
    pltpu.VMEM((4, 4, SHARE, 128), BF),
    pltpu.VMEM((2, 4, CUT, 128), BF),
    pltpu.VMEM((2, 4, SHARE - CUT, 128), BF),
    pltpu.VMEM((4, CUT, 128), BF),
    pltpu.VMEM((4, SHARE - CUT, 128), BF),
    pltpu.VMEM((4, CUT, 128), BF),
    pltpu.VMEM((4, SHARE - CUT, 128), BF),
    pltpu.VMEM((4, SHARE, 128), BF),
    pltpu.VMEM((NC, SHARE, 128), BF),
    pltpu.VMEM((SHARE, 128), BF),
    pltpu.VMEM((2, SHARE, 128), BF),
    DMA((3,)),
    DMA((3,)),
    DMA((2,)),
    DMA((2,)),
    DMA((2,)),
    DMA((2,)),
    DMA((4,)),
    DMA,
    DMA,
    DMA((2,)),
]


class Reduce:
    def __init__(self, scratch):
        (
            self.shares,
            self.got,
            self.part,
            r0,
            r1,
            t0,
            t1,
            u0,
            u1,
            self.px,
            self.rz,
            self.block,
            self.rb,
            self.s0,
            self.q0,
            self.sa,
            self.qa,
            self.sc,
            self.qc,
            self.sz,
            self.qz,
            self.sb,
            self.qb,
        ) = scratch
        self.one, self.on, self.two = (r0, r1), (t0, t1), (u0, u1)
        self.face, self.tile = place()
        self.core, self.chip = lax.rem(self.tile, 2), lax.div(self.tile, 2)
        self.x, self.high = lax.div(self.face, 2), lax.rem(self.face, 2)
        self.home = lax.rem(self.chip, 4)
        self.owner = self.home == self.x
        near = self.x + 1 - 2 * lax.rem(self.x, 2)
        self.partner = (near, 3 - self.x)

    def swap(self, k):
        rows = pl.ds(48 * k, 48)
        return remote(
            self.shares.at[:, :, 1 - self.core, rows, :],
            self.got.at[:, :, rows, :],
            self.s0.at[k],
            self.q0.at[k],
            self.face,
            self.tile + 1 - 2 * self.core,
        )

    def swap_start(self, k):
        self.swap(k).start()

    def across(self, way, src, dst, send, recv):
        return remote(src, dst, send, recv, 2 * self.partner[way] + self.high, self.tile)

    def first(self, way, i):
        other = self.partner[way]
        beyond = 3 - other if way == 0 else other + 1 - 2 * lax.rem(other, 2)
        start, rows = LANES[way]
        return self.across(
            way,
            self.part.at[:, (other, beyond)[i], pl.ds(start, rows), :],
            self.one[way].at[i],
            self.sa.at[way],
            self.qa.at[way],
        )

    def first_wait(self, way):
        return self.across(way, self.one[way], self.one[way], self.sa.at[way], self.qa.at[way])

    def second(self, way):
        return self.across(1 - way, self.on[way], self.two[way], self.sc.at[way], self.qc.at[way])

    def swap_take(self):
        for k in range(3):
            self.swap(k).wait_recv()

        @pl.loop(0, 4)
        def _(j):
            for h in range(4):
                both = self.shares[j, h, self.core].astype(F32) + self.got[j, h].astype(F32)
                self.part[j, h] = both.astype(BF)

        for way in range(2):
            for i in range(2):
                self.first(way, i).start()

    def first_take(self):
        for way in range(2):
            self.first_wait(way).wait_recv()
            start, rows = LANES[way]
            span = pl.ds(start, rows)
            mine = self.part[:, self.partner[1 - way], span, :].astype(F32)
            self.on[way][...] = (mine + self.one[way][1].astype(F32)).astype(BF)
            self.second(way).start()

    def second_take(self):
        for way in range(2):
            self.second(way).wait_recv()
            start, rows = LANES[way]
            mine = self.part[:, self.x, pl.ds(start, rows), :].astype(F32)
            total = mine + self.one[way][0].astype(F32) + self.two[way][...].astype(F32)
            self.px[:, start : start + rows, :] = total.astype(BF)

        @pl.loop(0, 4)
        def _(j):
            mine = 4 * j + self.x == self.chip

            @pl.when(jnp.logical_not(mine))
            def _():
                self.scatter(j).start()

            @pl.when(mine)
            def _():
                self.rz[self.chip] = self.px[j]

    def scatter(self, j):
        return remote(
            self.px.at[j],
            self.rz.at[self.chip],
            self.sz.at[j],
            self.qz,
            self.face,
            2 * (4 * j + self.x) + self.core,
        )

    def share(self, other):
        return remote(
            self.block, self.rb.at[self.high], self.sb, self.qb.at[self.high], other, self.tile
        )

    def chips_take(self):
        @pl.when(self.owner)
        def _():
            arrived = self.rz.at[pl.ds(0, NC - 1)]
            other = lax.rem(self.chip + 1, NC)
            remote(
                arrived, arrived, self.sb, self.qz, self.face, 2 * other + self.core
            ).wait_recv()
            self.block[...] = tree([self.rz[j] for j in range(NC)]).astype(BF)

            @pl.loop(1, NF)
            def _(step):
                self.share(lax.rem(self.face + step, NF)).start()

            self.rb[self.high] = self.block[...]

    def finish(self, out):
        for high in range(2):
            source = 2 * self.home + high

            @pl.when(source != self.face)
            def _():
                remote(
                    self.block, self.rb.at[high], self.sb, self.qb.at[high], source, self.tile
                ).wait_recv()

        put_grads(out, tree([self.rb[0], self.rb[1]]))

        for k in range(3):
            self.swap(k).wait_send()
        for way in range(2):
            self.first_wait(way).wait_send()
            self.second(way).wait_send()

        @pl.loop(0, 4)
        def _(j):
            @pl.when(4 * j + self.x != self.chip)
            def _():
                self.scatter(j).wait_send()

        @pl.when(self.owner)
        def _():
            sent = self.rz.at[pl.ds(0, NF - 1)]
            remote(
                sent, sent, self.sb, self.qz, lax.rem(self.face + 1, NF), self.tile
            ).wait_send()


HALF = RD // 2
N_SUM, N_HALO = len(SUM_SCRATCH), len(HALO_SCRATCH)

ANY = pl.BlockSpec(memory_space=pl.ANY)

WORK_SCRATCH = [
    pltpu.SMEM((4, NF), jnp.int32),
    pltpu.SMEM((4, NF), jnp.int32),
    pltpu.VMEM((9, C, C), BF),
    pltpu.VMEM((9, C, C), BF),
    pltpu.VMEM((HALF, CS, C), BF),
    pltpu.VMEM((3, 3 * C, C), BF),
    pltpu.VMEM((3, 3 * C, C), BF),
    pltpu.VMEM((RD + 2, FS, 3 * C), BF),
    pltpu.VMEM((RD + 2, FS, 3 * C), BF),
    pltpu.VMEM((HALF + 2, CS, 3 * C), BF),
    pltpu.VMEM((HALF + 2, CS, 3 * C), BF),
    pltpu.VMEM((RD, FS, C), BF),
    pltpu.VMEM((HALF, CS, C), BF),
    pltpu.VMEM((RD, FS, C), BF),
    pltpu.VMEM((RD, FS, C), F32),
    pltpu.VMEM((HALF, CS, C), F32),
    pltpu.VMEM((C, RD * FS), BF),
    pltpu.VMEM((C, HALF * CS), BF),
    pltpu.VMEM((32, C), F32),
    pltpu.VMEM((32, C), F32),
    DMA((6,)),
]


def extended(ref3, field, halo, edge, first, side):
    rows = field.shape[0]

    def put(i, row):
        left, right = edge[pl.ds(first + i, 1), :], edge[pl.ds(first + i + 16, 1), :]
        store_shifted(ref3, i, side(row.astype(F32)), left, right)

    put(0, halo[0])
    put(rows + 1, halo[1])

    @pl.loop(0, rows)
    def _(r):
        put(r + 1, field[r])


def whole_kernel(
    feat, cot, wf_any, wc_any, gain, nb_any, ed_any,
    output, grad_act, grad_w_fine, grad_w_coarse, grad_gain, vectors, *scratch
):
    scratch = list(scratch)

    def take(n):
        got = scratch[:n]
        del scratch[:n]
        return got

    own_a, own_b, buf_a, buf_b, sa, ra, sb, rb = take(N_SUM)
    own_c, own_d, buf_c, buf_d, sc, rc, sd, rd = take(N_SUM)
    halo1_scratch, halo2_scratch = take(N_HALO), take(N_HALO)
    (
        nb, ed, wf_taps, wc_taps, gco, wtf, wtc, x3, u3, c3, v3, fine, coarse_in, grad_fine,
        ga, gci, gt, ct, edge_h, edge_c, local,
    ) = take(len(WORK_SCRATCH))
    reduce_f = Reduce(take(len(REDUCE_SCRATCH)))
    reduce_c = Reduce(take(len(REDUCE_SCRATCH)))

    barrier_signal()
    loads = [
        pltpu.make_async_copy(src, dst, local.at[i])
        for i, (src, dst) in enumerate(
            ((nb_any, nb), (ed_any, ed), (wf_any, wf_taps), (wc_any, wc_taps))
        )
    ]
    for load in loads:
        load.start()
    halo1 = Halo(feat, gco, halo1_scratch, (nb, ed))
    halo2 = Halo(grad_fine, coarse_in, halo2_scratch, (nb, ed))

    pool, widen = pool_matrix(), spread_matrix()
    own_a[...] = jnp.zeros_like(own_a)
    own_c[...] = jnp.zeros_like(own_c)

    @pl.loop(0, HALF)
    def _(i):
        gco[i] = dot(pool, rows_of(cot, 2 * i, 2)).astype(BF)
        values = rows_of(feat, 2 * i, 2).astype(F32)
        own_a[0:1, :] += jnp.sum(values, axis=0, keepdims=True)
        own_a[1:2, :] += jnp.sum(values * values, axis=0, keepdims=True)

    barrier_wait()
    sum_start(line_a, own_a, buf_a, sa, ra)
    halo1.start()
    for load in loads:
        load.wait()
    back_weights(wc_taps, wtc)
    own_b[...] = sum_finish(line_a, own_a, buf_a, sa, ra)
    sum_start(line_b, own_b, buf_b, sb, rb)
    halo1.middle()
    back_weights(wf_taps, wtf)

    first, last, flip_top, flip_bottom = edge_flags(ed)
    halo1.finish((flip_top, flip_bottom))
    edge_c[...] = masked_sides(halo1.sides[...].astype(F32), first, last)

    extended(v3, gco, halo1.hc, edge_c, RD + 2, lambda row: row)
    top, bottom = halo_weights(wtc, flip_top, flip_bottom)
    gci[...] = dot(rows_of(v3, 1, HALF), wtc[1]).reshape(HALF, CS, C)
    gci[1:HALF] += dot(rows_of(v3, 1, HALF - 1), wtc[0]).reshape(HALF - 1, CS, C)
    gci[0 : HALF - 1] += dot(rows_of(v3, 2, HALF - 1), wtc[2]).reshape(HALF - 1, CS, C)
    gci[0] += dot(v3[0], top)
    gci[HALF - 1] += dot(v3[HALF + 1], bottom)

    total = sum_finish(line_b, own_b, buf_b, sb, rb)
    mean, inverse = norm_vectors(total)
    scale = gain[...]

    def hidden(raw):
        act = (raw - mean) * inverse * scale
        return (act * sigmoid(act)).astype(BF).astype(F32)

    edge_h[...] = masked_sides(hidden(halo1.sides[...].astype(F32)), first, last)
    extended(x3, feat, halo1.hf, edge_h, 0, hidden)

    def forward(i):
        acc = dot(rows_of(x3, 2 * i, 2), taps_of(wf_taps, 0))
        acc += dot(rows_of(x3, 2 * i + 1, 2), taps_of(wf_taps, 1))
        acc += dot(rows_of(x3, 2 * i + 2, 2), taps_of(wf_taps, 2))
        out = acc.astype(BF)
        fine[pl.ds(2 * i, 2)] = out.reshape(2, FS, C)
        pooled = 0.25 * dot(pool, out)
        gate = sigmoid(pooled)
        coarse_in[i] = (pooled * gate).astype(BF)
        slope = gate * (1.0 + pooled * (1.0 - gate))
        wide = spread(widen, gci[i] * slope * 0.25)
        for r in range(2):
            grad_fine[2 * i + r] = (cot[2 * i + r].astype(F32) + wide).astype(BF)

    @pl.loop(0, 2)
    def _(i):
        forward((HALF - 1) * i)

    halo2.start()
    pl.loop(1, HALF - 1)(forward)

    for r in range(HALF):
        ct[:, r * CS : (r + 1) * CS] = coarse_in[r].astype(F32).T.astype(BF)
    inner = (HALF - 1) * CS
    over_top = dot(ct[:, 0:CS], v3[0])
    over_bottom = dot(ct[:, inner:], v3[HALF + 1])

    def block(product, m):
        return product[:, m * C : (m + 1) * C]

    for k in (2, 1, 0):
        if k == 0:
            product = dot(ct[:, CS:], rows_of(v3, 1, HALF - 1))
        elif k == 1:
            product = dot(ct[...], rows_of(v3, 1, HALF))
        else:
            product = dot(ct[:, 0:inner], rows_of(v3, 2, HALF - 1))
        for m in range(3):
            term = block(product, m)
            if k == 0:
                term += jnp.where(flip_top, 0.0, block(over_top, m))
                term += jnp.where(flip_bottom, block(over_bottom, 2 - m), 0.0)
            elif k == 2:
                term += jnp.where(flip_bottom, 0.0, block(over_bottom, m))
                term += jnp.where(flip_top, block(over_top, 2 - m), 0.0)
            put_share(reduce_c.shares, 8 - (3 * k + m), term)
        reduce_c.swap_start(2 - k)

    def fine_gradient(k):
        product = dot(gt[...], rows_of(x3, k, RD))
        for m in range(3):
            put_share(reduce_f.shares, 3 * k + m, block(product, m).T)
        reduce_f.swap_start(k)

    for r in range(RD):
        gt[:, r * FS : (r + 1) * FS] = grad_fine[r].astype(F32).T.astype(BF)
    fine_gradient(0)
    halo2.middle()
    fine_gradient(1)
    reduce_c.swap_take()
    fine_gradient(2)
    halo2.finish((flip_top, flip_bottom))
    edge_h[...] = masked_sides(halo2.sides[...].astype(F32), first, last)
    reduce_f.swap_take()

    extended(u3, grad_fine, halo2.hf, edge_h, 0, lambda row: row)
    top, bottom = halo_weights(wtf, flip_top, flip_bottom)
    reduce_c.first_take()
    ga[1 : RD - 1] = jnp.zeros((RD - 2, FS, C), F32)
    ga[0] = dot(u3[0], top)
    ga[RD - 1] = dot(u3[RD + 1], bottom)
    u3[0] = jnp.zeros((FS, 3 * C), BF)
    u3[RD + 1] = jnp.zeros((FS, 3 * C), BF)

    def back(i):
        grad = dot(rows_of(u3, 2 * i, 2), wtf[0])
        grad += dot(rows_of(u3, 2 * i + 1, 2), wtf[1])
        grad += dot(rows_of(u3, 2 * i + 2, 2), wtf[2])
        grad += rows_of(ga, 2 * i, 2)
        normed = (rows_of(feat, 2 * i, 2).astype(F32) - mean) * inverse
        act = normed * scale
        gate = sigmoid(act)
        grad = grad * (gate * (1.0 + act * (1.0 - gate)))
        ga[pl.ds(2 * i, 2)] = grad.reshape(2, FS, C)
        own_c[0:1, :] += jnp.sum(grad * normed, axis=0, keepdims=True)
        own_c[1:2, :] += jnp.sum(grad, axis=0, keepdims=True)

    pl.loop(0, HALF // 2)(back)
    reduce_f.first_take()
    reduce_c.second_take()
    pl.loop(HALF // 2, HALF)(back)
    sum_start(line_a, own_c, buf_c, sc, rc)
    store_act = pltpu.make_async_copy(ga, grad_act, local.at[4])
    store_act.start()
    reduce_f.second_take()

    extended(c3, coarse_in, halo2.hc, edge_h, RD + 2, lambda row: row)
    own_d[...] = sum_finish(line_a, own_c, buf_c, sc, rc)
    sum_start(line_b, own_d, buf_d, sd, rd)
    reduce_c.chips_take()

    @pl.loop(0, HALF)
    def _(i):
        out = dot(c3[i], taps_of(wc_taps, 0))
        out += dot(c3[i + 1], taps_of(wc_taps, 1))
        out += dot(c3[i + 2], taps_of(wc_taps, 2))
        wide = spread(widen, out)
        for r in range(2):
            fine[2 * i + r] = (fine[2 * i + r].astype(F32) + wide).astype(BF)

    store_output = pltpu.make_async_copy(fine, output, local.at[5])
    store_output.start()
    reduce_f.chips_take()
    sums = sum_finish(line_b, own_d, buf_d, sd, rd)

    grad_gain[...] = sums[0:1] * (1.0 / CELLS)
    grouped = group_sum(sums * scale) / (CELLS * GROUP)
    group_slope, group_shift = grouped[0:1], grouped[1:2]
    for i, vector in enumerate((mean, inverse, scale, group_shift, group_slope)):
        vectors[i : i + 1, :] = vector
    reduce_c.finish(grad_w_coarse)
    reduce_f.finish(grad_w_fine)
    store_act.wait()
    store_output.wait()


def last_kernel(
    feat, ga, vectors, wf_in, wc_in, gain_in, output_in,
    output, grad_features, wf_out, wc_out, gain_out, feat_v, ga_v, sum_v, out_v, sems
):
    def rows(ref, q):
        return ref.at[pl.ds(2 * q, 2)]

    def moves(pairs, first):
        return [
            [
                pltpu.make_async_copy(rows(src, q), rows(dst, q), sems.at[first + i, q])
                for i, (src, dst) in enumerate(pairs)
            ]
            for q in range(HALF)
        ]

    loads = moves(((feat, feat_v), (ga, ga_v), (output_in, sum_v)), 0)
    stores = moves(((out_v, grad_features), (sum_v, output)), 3)
    for chunk in loads:
        for copy in chunk:
            copy.start()
    wf_out[...] = wf_in[...]
    wc_out[...] = wc_in[...]
    gain_out[...] = gain_in[...]
    mean, inverse, scale = vectors[0:1], vectors[1:2], vectors[2:3]
    group_shift, group_slope = vectors[3:4], vectors[4:5]
    for q in range(HALF):
        for copy in loads[q]:
            copy.wait()
        for r in (2 * q, 2 * q + 1):
            normed = (feat_v[r].astype(F32) - mean) * inverse
            out_v[r] = inverse * (scale * ga_v[r] - group_shift - normed * group_slope)
        for copy in stores[q]:
            copy.start()
    for chunk in stores:
        for copy in chunk:
            copy.wait()


def shape(dims, dtype):
    return jax.ShapeDtypeStruct(dims, dtype)


def on_device(features, cotangent, w_fine, w_coarse, gain, neighbors, neighbor_edges):
    outs = [
        shape((RD, FS, C), BF),
        shape((RD, FS, C), F32),
        shape((9, 8, C), F32),
        shape((9, 8, C), F32),
        shape((1, C), F32),
    ]
    output, grad_act, grad_w_fine, grad_w_coarse, grad_gain, vectors = pl.pallas_call(
        whole_kernel,
        in_specs=[VM, VM, ANY, ANY, VM, ANY, ANY],
        out_specs=[ANY, ANY, VM, VM, VM, VM],
        out_shape=outs + [shape((8, C), F32)],
        scratch_shapes=SUM_SCRATCH * 2
        + HALO_SCRATCH * 2
        + WORK_SCRATCH
        + REDUCE_SCRATCH * 2,
        compiler_params=pltpu.CompilerParams(
            vmem_limit_bytes=VMEM_LIMIT, collective_id=1, has_side_effects=True
        ),
    )(features[0], cotangent[0], w_fine, w_coarse, gain[None], neighbors.T, neighbor_edges.T)
    output, grad_features, grad_w_fine, grad_w_coarse, grad_gain = pl.pallas_call(
        last_kernel,
        in_specs=[ANY, ANY] + [VM] * 4 + [ANY],
        out_specs=[ANY, ANY] + [VM] * 3,
        out_shape=outs,
        scratch_shapes=[
            pltpu.VMEM((RD, FS, C), BF),
            pltpu.VMEM((RD, FS, C), F32),
            pltpu.VMEM((RD, FS, C), BF),
            pltpu.VMEM((RD, FS, C), F32),
            DMA((5, HALF)),
        ],
        compiler_params=pltpu.CompilerParams(vmem_limit_bytes=VMEM_LIMIT),
    )(features[0], grad_act, vectors, grad_w_fine, grad_w_coarse, grad_gain, output)
    return (output[None], grad_features[None], grad_w_fine, grad_w_coarse, grad_gain[0])


def solution(mesh):
    return jax.shard_map(
        on_device,
        mesh=mesh,
        in_specs=(
            P("face", "tile", None, None),
            P("face", "tile", None, None),
            P(),
            P(),
            P(),
            P(),
            P(),
        ),
        out_specs=(
            P("face", "tile", None, None),
            P("face", "tile", None, None),
            P(None, "tile", None),
            P(None, "tile", None),
            P(),
        ),
        check_vma=False,
    )
```

```python
import jax
import jax.numpy as jnp
from jax import lax
from jax.experimental import pallas as pl
from jax.experimental.pallas import tpu as pltpu
from jax.sharding import PartitionSpec as P

BF = jnp.bfloat16
F32 = jnp.float32
MESH = pl.DeviceIdType.MESH
NF = 8
NT = 32
NZ = 16
RD = 8
FS = 256
CS = 128
C = 256
GROUP = 8
SLOTS = 16
CELLS = NF * FS * FS
VMEM_LIMIT = 60 * 1024 * 1024

VM = pl.BlockSpec(memory_space=pltpu.VMEM)
SM = pl.BlockSpec(memory_space=pltpu.SMEM)
DMA = pltpu.SemaphoreType.DMA


def remote(src, dst, send, recv, face, tile):
    return pltpu.make_async_remote_copy(
        src_ref=src,
        dst_ref=dst,
        send_sem=send,
        recv_sem=recv,
        device_id=(face, tile),
        device_id_type=MESH,
    )


def place():
    return lax.axis_index("face"), lax.axis_index("tile")


def is_rim(tile):
    return (tile == 0) | (tile == NT - 1)


def slot_device(slot):
    return lax.div(slot, 2), (NT - 1) * lax.rem(slot, 2)


def my_slot(face, tile):
    return 2 * face + jnp.where(tile == NT - 1, 1, 0)


def multiple(value, of):
    return pl.multiple_of(value * of, of)


def signal(barrier, face, tile):
    pl.semaphore_signal(barrier, inc=1, device_id=(face, tile), device_id_type=MESH)


def line_a(face, tile, step):
    mine = lax.rem(tile, NZ)
    other = lax.rem(mine + step, NZ)
    return mine, other, (face, tile - mine + other)


def line_b(face, tile, step):
    mine = face * 2 + lax.div(tile, NZ)
    other = lax.rem(mine + step, 2 * NF)
    return mine, other, (lax.div(other, 2), lax.rem(other, 2) * NZ + lax.rem(tile, NZ))


def barrier_signal():
    face, tile = place()
    barrier = pltpu.get_barrier_semaphore()
    across = lax.rem(tile + NZ, NT)
    across = across - lax.rem(across, NZ) + lax.rem(tile, 2)

    @pl.loop(1, NZ)
    def _(step):
        for line in (line_a, line_b):
            _, _, device = line(face, tile, step)
            signal(barrier, *device)

    @pl.loop(0, NZ // 2)
    def _(z):
        signal(barrier, face, across + 2 * z)

    signal(barrier, face, lax.rem(tile + 1, NT))
    signal(barrier, face, lax.rem(tile + NT - 1, NT))

    @pl.when(is_rim(tile))
    def _():
        mine = my_slot(face, tile)

        @pl.loop(1, SLOTS)
        def _(step):
            signal(barrier, *slot_device(lax.rem(mine + step, SLOTS)))


def barrier_wait():
    _, tile = place()
    barrier = pltpu.get_barrier_semaphore()
    count = 2 * (NZ - 1) + NZ // 2 + 2

    @pl.when(is_rim(tile))
    def _():
        pl.semaphore_wait(barrier, count + SLOTS - 1)

    @pl.when(~is_rim(tile))
    def _():
        pl.semaphore_wait(barrier, count)


def sum_start(line, own, buf, send, recv):
    face, tile = place()

    @pl.loop(1, NZ)
    def _(step):
        mine, _, device = line(face, tile, step)
        remote(own, buf.at[mine], send, recv, *device).start()

    mine, _, _ = line(face, tile, 0)
    buf[mine] = own[...]


def sum_finish(line, own, buf, send, recv):
    face, tile = place()
    _, _, device = line(face, tile, 1)
    arrived = buf.at[pl.ds(0, NZ - 1)]
    copies = remote(arrived, arrived, send, recv, *device)
    copies.wait_recv()
    total = buf[0]
    for i in range(1, NZ):
        total = total + buf[i]
    copies.wait_send()
    return total


SUM_SCRATCH = [
    pltpu.VMEM((2, C), F32),
    pltpu.VMEM((2, C), F32),
    pltpu.VMEM((NZ, 2, C), F32),
    pltpu.VMEM((NZ, 2, C), F32),
    DMA,
    DMA,
    DMA,
    DMA,
]

RIM = C + 128

HALO_SCRATCH = [
    pltpu.VMEM((2, FS, C), BF),
    pltpu.VMEM((2, CS, C), BF),
    pltpu.VMEM((SLOTS, 16, RIM), BF),
    pltpu.VMEM((SLOTS, 16, RIM), BF),
    pltpu.VMEM((SLOTS, 16, RIM), BF),
    pltpu.VMEM((SLOTS, 16, RIM), BF),
    pltpu.VMEM((32, C), F32),
    pltpu.VMEM((32, C), BF),
    pltpu.VMEM((NF, 32, C), BF),
    pltpu.VMEM((32, C), BF),
] + [DMA] * 10


class Halo:
    def __init__(self, fine, coarse, scratch, tables):
        self.fine, self.coarse = fine, coarse
        (
            self.hf,
            self.hc,
            self.rim,
            self.r1,
            self.st,
            self.r2,
            self.rows,
            self.srec,
            self.sall,
            self.sides,
            self.fs,
            self.fr,
            self.cs,
            self.cr,
            self.s1,
            self.q1,
            self.s2,
            self.q2,
            self.ss,
            self.sr,
        ) = scratch
        self.nb, self.ed = tables
        self.face, self.tile = place()
        self.slot = my_slot(self.face, self.tile)

    def rows_start(self):
        up = lax.rem(self.tile + 1, NT)
        down = lax.rem(self.tile + NT - 1, NT)
        for field, halo, send, recv in (
            (self.fine, self.hf, self.fs, self.fr),
            (self.coarse, self.hc, self.cs, self.cr),
        ):
            last = field.shape[0] - 1
            remote(field.at[last], halo.at[0], send, recv, self.face, up).start()
            remote(field.at[0], halo.at[1], send, recv, self.face, down).start()

    def rows_wait(self):
        up = lax.rem(self.tile + 1, NT)
        for halo, send, recv in ((self.hf, self.fs, self.fr), (self.hc, self.cs, self.cr)):
            both = remote(halo, halo, send, recv, self.face, up)
            both.wait_recv()
            both.wait_send()

    def rim_partner(self, step):
        other = lax.rem(self.slot + step, SLOTS)
        return other, slot_device(other)

    def rim_wait(self, buf, send, recv):
        _, device = self.rim_partner(1)
        arrived = buf.at[pl.ds(0, SLOTS - 1)]
        copies = remote(arrived, arrived, send, recv, *device)
        copies.wait_recv()
        copies.wait_send()

    def start(self):
        @pl.when(is_rim(self.tile))
        def _():
            fine_row = jnp.where(self.tile == 0, 0, RD - 1)
            coarse_row = jnp.where(self.tile == 0, 0, RD // 2 - 1)
            self.rim[:, :, 0:C] = self.fine[fine_row].reshape(SLOTS, 16, C)
            cells = self.coarse[coarse_row]
            self.rim[0:8, :, C:RIM] = cells[:, 0:128].reshape(8, 16, 128)
            self.rim[8:16, :, C:RIM] = cells[:, 128:256].reshape(8, 16, 128)

            @pl.loop(1, SLOTS)
            def _(step):
                other, device = self.rim_partner(step)
                remote(self.rim.at[other], self.r1.at[self.slot], self.s1, self.q1, *device).start()

            self.r1[self.slot] = self.rim[self.slot]

        self.rows_start()

    def middle(self):
        @pl.when(is_rim(self.tile))
        def _():
            self.rim_wait(self.r1, self.s1, self.q1)

            @pl.loop(0, SLOTS)
            def _(slot):
                face, edge = lax.div(slot, 2), 2 * lax.rem(slot, 2)
                source = 2 * self.nb[edge, face] + lax.div(self.ed[edge, face], 2)
                self.st[slot] = self.r1[source]

            @pl.loop(1, SLOTS)
            def _(step):
                other, device = self.rim_partner(step)
                remote(self.st.at[other], self.r2.at[self.slot], self.s2, self.q2, *device).start()

            self.r2[self.slot] = self.st[self.slot]

        self.rows_wait()
        fine_rows = [self.hf.at[0]] + [self.fine.at[r] for r in range(RD)] + [self.hf.at[1]]
        coarse_rows = [self.hc.at[0]] + [self.coarse.at[r] for r in range(RD // 2)]
        coarse_rows += [self.hc.at[1]]
        for i, row in enumerate(fine_rows + coarse_rows):
            side = row.shape[0]
            self.rows[i : i + 1, :] = row[0:16, :].astype(F32)[0:1]
            self.rows[16 + i : 17 + i, :] = row[side - 16 : side, :].astype(F32)[15:16]
        self.srec[...] = self.rows[...].astype(BF)

        @pl.loop(1, NF)
        def _(step):
            other = lax.rem(self.face + step, NF)
            remote(
                self.srec, self.sall.at[self.face], self.ss, self.sr, other, self.tile
            ).start()

        self.sall[self.face] = self.srec[...]

    def finish(self, flips):
        @pl.when(is_rim(self.tile))
        def _():
            self.rim_wait(self.r2, self.s2, self.q2)
            flip_top, flip_bottom = flips
            flip = jnp.where(self.tile == 0, flip_top, flip_bottom)
            edge = jnp.where(self.tile == 0, 0, 1)
            fine = self.r2[:, :, 0:C].reshape(FS, C)
            coarse = jnp.concatenate(
                [
                    self.r2[0:8, :, C:RIM].reshape(CS, 128),
                    self.r2[8:16, :, C:RIM].reshape(CS, 128),
                ],
                axis=1,
            )
            self.hf[edge] = dot(rim_matrix(FS, flip), fine).astype(BF)
            self.hc[edge] = dot(rim_matrix(CS, flip), coarse).astype(BF)

        other = lax.rem(self.face + 1, NF)
        arrived = self.sall.at[pl.ds(0, NF - 1)]
        copies = remote(arrived, arrived, self.ss, self.sr, other, self.tile)
        copies.wait_recv()
        copies.wait_send()
        left_face, right_face = self.nb[3, self.face], self.nb[1, self.face]
        self.sides[0:16, :] = self.sall[left_face, 16:32, :]
        self.sides[16:32, :] = self.sall[right_face, 0:16, :]


def iota(shape, dim):
    return lax.broadcasted_iota(jnp.int32, shape, dim)


def dot(a, b):
    return jnp.dot(a, b, preferred_element_type=F32)


def sigmoid(values):
    return 0.5 * jnp.tanh(0.5 * values) + 0.5


def pool_matrix():
    row, col = iota((CS, 2 * FS), 0), iota((CS, 2 * FS), 1)
    return jnp.where(lax.div(lax.rem(col, FS), 2) == row, 1.0, 0.0).astype(BF)


def spread_matrix():
    row, col = iota((FS, 2 * CS), 0), iota((FS, 2 * CS), 1)
    return jnp.where(lax.rem(col, CS) == lax.div(row, 2), 1.0, 0.0).astype(BF)


def spread(matrix, values):
    high = values.astype(BF)
    low = (values - high.astype(F32)).astype(BF)
    return dot(matrix, jnp.concatenate([high, low], axis=0))


def rim_matrix(side, flip):
    row, col = iota((side, side), 0), iota((side, side), 1)
    source = jnp.where(flip, side - 1 - row, row)
    return jnp.where(col == source, 1.0, 0.0).astype(BF)


def store_shifted(ref, row, values, left, right):
    n = values.shape[0]
    position = iota(values.shape, 0)
    before = jnp.where(position == 0, left, pltpu.roll(values, 1, 0))
    after = jnp.where(position == n - 1, right, pltpu.roll(values, n - 1, 0))
    ref[row, :, 0:C] = before.astype(BF)
    ref[row, :, C : 2 * C] = values.astype(BF)
    ref[row, :, 2 * C : 3 * C] = after.astype(BF)


def group_sum(values):
    lane = iota(values.shape, 1)
    for width in (1, 2, 4):
        up = pltpu.roll(values, width, 1)
        down = pltpu.roll(values, C - width, 1)
        values = values + jnp.where(lax.rem(lax.div(lane, width), 2) == 0, down, up)
    return values


def norm_vectors(total):
    grouped = group_sum(total) / (CELLS * GROUP)
    mean, second = grouped[0:1], grouped[1:2]
    return mean, lax.rsqrt(second - mean * mean + 1e-05)


def edge_flags(ed_ref):
    face, tile = place()
    first, last = tile == 0, tile == NT - 1
    flip_top = first & (ed_ref[0, face] != 2)
    flip_bottom = last & (ed_ref[2, face] != 0)
    return first, last, flip_top, flip_bottom


def masked_sides(sides, first, last):
    row = lax.rem(iota(sides.shape, 0), 16)
    top = (row == 0) | (row == RD + 2)
    bottom = (row == RD + 1) | (row == 15)
    zero = (top & first) | (bottom & last)
    return jnp.where(zero, 0.0, sides)


def back_weights(w_ref, out_ref):
    for k in range(3):
        for m in range(3):
            tap = w_ref[8 - (3 * k + m)].astype(F32)
            out_ref[k, m * C : (m + 1) * C, :] = tap.T.astype(BF)


def halo_weights(wt_ref, flip_top, flip_bottom):
    def turned(k):
        return jnp.concatenate(
            [wt_ref[k, (2 - m) * C : (3 - m) * C, :] for m in range(3)], axis=0
        )

    top = jnp.where(flip_top, turned(2), wt_ref[0])
    bottom = jnp.where(flip_bottom, turned(0), wt_ref[2])
    return top, bottom


def rows_of(ref, start, count):
    _, side, width = ref.shape
    return ref[pl.ds(start, count)].reshape(count * side, width)


def taps_of(ref, k):
    return ref[3 * k : 3 * k + 3].reshape(3 * C, C)


SHARE = 144
NC = 16


def put_share(shares, tap, product):
    cut = product.reshape(4, 4, 2, 8, C)
    halves = [cut[..., :128], cut[..., 128:]]
    shares[:, :, :, 16 * tap : 16 * tap + 16, :] = jnp.concatenate(halves, axis=3).astype(BF)


def put_grads(out, total):
    total = (total * (1.0 / CELLS)).reshape(9, 2, 8, 128)
    out[:, :, 0:128] = total[:, 0]
    out[:, :, 128:256] = total[:, 1]


def tree(parts):
    parts = [part.astype(F32) for part in parts]
    while len(parts) > 1:
        parts = [sum(parts[i : i + 2]) for i in range(0, len(parts), 2)]
    return parts[0]


CUT = 80
LANES = ((0, CUT), (CUT, SHARE - CUT))

REDUCE_SCRATCH = [
    pltpu.VMEM((4, 4, 2, SHARE, 128), BF),
    pltpu.VMEM((4, 4, SHARE, 128), BF),
    pltpu.VMEM((4, 4, SHARE, 128), BF),
    pltpu.VMEM((2, 4, CUT, 128), BF),
    pltpu.VMEM((2, 4, SHARE - CUT, 128), BF),
    pltpu.VMEM((4, CUT, 128), BF),
    pltpu.VMEM((4, SHARE - CUT, 128), BF),
    pltpu.VMEM((4, CUT, 128), BF),
    pltpu.VMEM((4, SHARE - CUT, 128), BF),
    pltpu.VMEM((4, SHARE, 128), BF),
    pltpu.VMEM((NC, SHARE, 128), BF),
    pltpu.VMEM((SHARE, 128), BF),
    pltpu.VMEM((2, SHARE, 128), BF),
    DMA((3,)),
    DMA((3,)),
    DMA((2,)),
    DMA((2,)),
    DMA((2,)),
    DMA((2,)),
    DMA((4,)),
    DMA,
    DMA,
    DMA((2,)),
]


class Reduce:
    def __init__(self, scratch):
        (
            self.shares,
            self.got,
            self.part,
            r0,
            r1,
            t0,
            t1,
            u0,
            u1,
            self.px,
            self.rz,
            self.block,
            self.rb,
            self.s0,
            self.q0,
            self.sa,
            self.qa,
            self.sc,
            self.qc,
            self.sz,
            self.qz,
            self.sb,
            self.qb,
        ) = scratch
        self.one, self.on, self.two = (r0, r1), (t0, t1), (u0, u1)
        self.face, self.tile = place()
        self.core, self.chip = lax.rem(self.tile, 2), lax.div(self.tile, 2)
        self.x, self.high = lax.div(self.face, 2), lax.rem(self.face, 2)
        self.home = lax.rem(self.chip, 4)
        self.owner = self.home == self.x
        near = self.x + 1 - 2 * lax.rem(self.x, 2)
        self.partner = (near, 3 - self.x)

    def swap(self, k):
        rows = pl.ds(48 * k, 48)
        return remote(
            self.shares.at[:, :, 1 - self.core, rows, :],
            self.got.at[:, :, rows, :],
            self.s0.at[k],
            self.q0.at[k],
            self.face,
            self.tile + 1 - 2 * self.core,
        )

    def swap_start(self, k):
        self.swap(k).start()

    def across(self, way, src, dst, send, recv):
        return remote(src, dst, send, recv, 2 * self.partner[way] + self.high, self.tile)

    def first(self, way, i):
        other = self.partner[way]
        beyond = 3 - other if way == 0 else other + 1 - 2 * lax.rem(other, 2)
        start, rows = LANES[way]
        return self.across(
            way,
            self.part.at[:, (other, beyond)[i], pl.ds(start, rows), :],
            self.one[way].at[i],
            self.sa.at[way],
            self.qa.at[way],
        )

    def first_wait(self, way):
        return self.across(way, self.one[way], self.one[way], self.sa.at[way], self.qa.at[way])

    def second(self, way):
        return self.across(1 - way, self.on[way], self.two[way], self.sc.at[way], self.qc.at[way])

    def swap_take(self):
        for k in range(3):
            self.swap(k).wait_recv()

        @pl.loop(0, 4)
        def _(j):
            for h in range(4):
                both = self.shares[j, h, self.core].astype(F32) + self.got[j, h].astype(F32)
                self.part[j, h] = both.astype(BF)

        for way in range(2):
            for i in range(2):
                self.first(way, i).start()

    def first_take(self):
        for way in range(2):
            self.first_wait(way).wait_recv()
            start, rows = LANES[way]
            span = pl.ds(start, rows)
            mine = self.part[:, self.partner[1 - way], span, :].astype(F32)
            self.on[way][...] = (mine + self.one[way][1].astype(F32)).astype(BF)
            self.second(way).start()

    def second_take(self):
        for way in range(2):
            self.second(way).wait_recv()
            start, rows = LANES[way]
            mine = self.part[:, self.x, pl.ds(start, rows), :].astype(F32)
            total = mine + self.one[way][0].astype(F32) + self.two[way][...].astype(F32)
            self.px[:, start : start + rows, :] = total.astype(BF)

        @pl.loop(0, 4)
        def _(j):
            mine = 4 * j + self.x == self.chip

            @pl.when(jnp.logical_not(mine))
            def _():
                self.scatter(j).start()

            @pl.when(mine)
            def _():
                self.rz[self.chip] = self.px[j]

    def scatter(self, j):
        return remote(
            self.px.at[j],
            self.rz.at[self.chip],
            self.sz.at[j],
            self.qz,
            self.face,
            2 * (4 * j + self.x) + self.core,
        )

    def share(self, other):
        return remote(
            self.block, self.rb.at[self.high], self.sb, self.qb.at[self.high], other, self.tile
        )

    def chips_take(self):
        @pl.when(self.owner)
        def _():
            arrived = self.rz.at[pl.ds(0, NC - 1)]
            other = lax.rem(self.chip + 1, NC)
            remote(
                arrived, arrived, self.sb, self.qz, self.face, 2 * other + self.core
            ).wait_recv()
            self.block[...] = tree([self.rz[j] for j in range(NC)]).astype(BF)

            @pl.loop(1, NF)
            def _(step):
                self.share(lax.rem(self.face + step, NF)).start()

            self.rb[self.high] = self.block[...]

    def finish(self, out):
        for high in range(2):
            source = 2 * self.home + high

            @pl.when(source != self.face)
            def _():
                remote(
                    self.block, self.rb.at[high], self.sb, self.qb.at[high], source, self.tile
                ).wait_recv()

        put_grads(out, tree([self.rb[0], self.rb[1]]))

        for k in range(3):
            self.swap(k).wait_send()
        for way in range(2):
            self.first_wait(way).wait_send()
            self.second(way).wait_send()

        @pl.loop(0, 4)
        def _(j):
            @pl.when(4 * j + self.x != self.chip)
            def _():
                self.scatter(j).wait_send()

        @pl.when(self.owner)
        def _():
            sent = self.rz.at[pl.ds(0, NF - 1)]
            remote(
                sent, sent, self.sb, self.qz, lax.rem(self.face + 1, NF), self.tile
            ).wait_send()


HALF = RD // 2
N_SUM, N_HALO = len(SUM_SCRATCH), len(HALO_SCRATCH)

ANY = pl.BlockSpec(memory_space=pl.ANY)

WORK_SCRATCH = [
    pltpu.SMEM((4, NF), jnp.int32),
    pltpu.SMEM((4, NF), jnp.int32),
    pltpu.VMEM((9, C, C), BF),
    pltpu.VMEM((9, C, C), BF),
    pltpu.VMEM((HALF, CS, C), BF),
    pltpu.VMEM((3, 3 * C, C), BF),
    pltpu.VMEM((3, 3 * C, C), BF),
    pltpu.VMEM((RD + 2, FS, 3 * C), BF),
    pltpu.VMEM((RD + 2, FS, 3 * C), BF),
    pltpu.VMEM((HALF + 2, CS, 3 * C), BF),
    pltpu.VMEM((HALF + 2, CS, 3 * C), BF),
    pltpu.VMEM((RD, FS, C), BF),
    pltpu.VMEM((HALF, CS, C), BF),
    pltpu.VMEM((RD, FS, C), BF),
    pltpu.VMEM((RD, FS, C), F32),
    pltpu.VMEM((HALF, CS, C), F32),
    pltpu.VMEM((C, RD * FS), BF),
    pltpu.VMEM((C, HALF * CS), BF),
    pltpu.VMEM((32, C), F32),
    pltpu.VMEM((32, C), F32),
    DMA((6,)),
]


def extended(ref3, field, halo, edge, first, side):
    rows = field.shape[0]

    def put(i, row):
        left, right = edge[pl.ds(first + i, 1), :], edge[pl.ds(first + i + 16, 1), :]
        store_shifted(ref3, i, side(row.astype(F32)), left, right)

    put(0, halo[0])
    put(rows + 1, halo[1])

    @pl.loop(0, rows)
    def _(r):
        put(r + 1, field[r])


def whole_kernel(
    feat, cot, wf_any, wc_any, gain, nb_any, ed_any,
    output, grad_features, grad_w_fine, grad_w_coarse, grad_gain, *scratch
):
    scratch = list(scratch)

    def take(n):
        got = scratch[:n]
        del scratch[:n]
        return got

    own_a, own_b, buf_a, buf_b, sa, ra, sb, rb = take(N_SUM)
    own_c, own_d, buf_c, buf_d, sc, rc, sd, rd = take(N_SUM)
    halo1_scratch, halo2_scratch = take(N_HALO), take(N_HALO)
    (
        nb, ed, wf_taps, wc_taps, gco, wtf, wtc, x3, u3, c3, v3, fine, coarse_in, grad_fine,
        ga, gci, gt, ct, edge_h, edge_c, local,
    ) = take(len(WORK_SCRATCH))
    reduce_f = Reduce(take(len(REDUCE_SCRATCH)))
    reduce_c = Reduce(take(len(REDUCE_SCRATCH)))

    barrier_signal()
    loads = [
        pltpu.make_async_copy(src, dst, local.at[i])
        for i, (src, dst) in enumerate(
            ((nb_any, nb), (ed_any, ed), (wf_any, wf_taps), (wc_any, wc_taps))
        )
    ]
    for load in loads:
        load.start()
    halo1 = Halo(feat, gco, halo1_scratch, (nb, ed))
    halo2 = Halo(grad_fine, coarse_in, halo2_scratch, (nb, ed))

    pool, widen = pool_matrix(), spread_matrix()
    own_a[...] = jnp.zeros_like(own_a)
    own_c[...] = jnp.zeros_like(own_c)

    @pl.loop(0, HALF)
    def _(i):
        gco[i] = dot(pool, rows_of(cot, 2 * i, 2)).astype(BF)
        values = rows_of(feat, 2 * i, 2).astype(F32)
        own_a[0:1, :] += jnp.sum(values, axis=0, keepdims=True)
        own_a[1:2, :] += jnp.sum(values * values, axis=0, keepdims=True)

    barrier_wait()
    sum_start(line_a, own_a, buf_a, sa, ra)
    halo1.start()
    for load in loads:
        load.wait()
    back_weights(wc_taps, wtc)
    own_b[...] = sum_finish(line_a, own_a, buf_a, sa, ra)
    sum_start(line_b, own_b, buf_b, sb, rb)
    halo1.middle()
    back_weights(wf_taps, wtf)

    first, last, flip_top, flip_bottom = edge_flags(ed)
    halo1.finish((flip_top, flip_bottom))
    edge_c[...] = masked_sides(halo1.sides[...].astype(F32), first, last)

    extended(v3, gco, halo1.hc, edge_c, RD + 2, lambda row: row)
    top, bottom = halo_weights(wtc, flip_top, flip_bottom)
    gci[...] = dot(rows_of(v3, 1, HALF), wtc[1]).reshape(HALF, CS, C)
    gci[1:HALF] += dot(rows_of(v3, 1, HALF - 1), wtc[0]).reshape(HALF - 1, CS, C)
    gci[0 : HALF - 1] += dot(rows_of(v3, 2, HALF - 1), wtc[2]).reshape(HALF - 1, CS, C)
    gci[0] += dot(v3[0], top)
    gci[HALF - 1] += dot(v3[HALF + 1], bottom)

    total = sum_finish(line_b, own_b, buf_b, sb, rb)
    mean, inverse = norm_vectors(total)
    scale = gain[...]

    def hidden(raw):
        act = (raw - mean) * inverse * scale
        return (act * sigmoid(act)).astype(BF).astype(F32)

    edge_h[...] = masked_sides(hidden(halo1.sides[...].astype(F32)), first, last)
    extended(x3, feat, halo1.hf, edge_h, 0, hidden)

    def forward(i):
        acc = dot(rows_of(x3, 2 * i, 2), taps_of(wf_taps, 0))
        acc += dot(rows_of(x3, 2 * i + 1, 2), taps_of(wf_taps, 1))
        acc += dot(rows_of(x3, 2 * i + 2, 2), taps_of(wf_taps, 2))
        out = acc.astype(BF)
        fine[pl.ds(2 * i, 2)] = out.reshape(2, FS, C)
        pooled = 0.25 * dot(pool, out)
        gate = sigmoid(pooled)
        coarse_in[i] = (pooled * gate).astype(BF)
        slope = gate * (1.0 + pooled * (1.0 - gate))
        wide = spread(widen, gci[i] * slope * 0.25)
        for r in range(2):
            grad_fine[2 * i + r] = (cot[2 * i + r].astype(F32) + wide).astype(BF)

    @pl.loop(0, 2)
    def _(i):
        forward((HALF - 1) * i)

    halo2.start()
    pl.loop(1, HALF - 1)(forward)

    for r in range(HALF):
        ct[:, r * CS : (r + 1) * CS] = coarse_in[r].astype(F32).T.astype(BF)
    inner = (HALF - 1) * CS
    over_top = dot(ct[:, 0:CS], v3[0])
    over_bottom = dot(ct[:, inner:], v3[HALF + 1])

    def block(product, m):
        return product[:, m * C : (m + 1) * C]

    for k in (2, 1, 0):
        if k == 0:
            product = dot(ct[:, CS:], rows_of(v3, 1, HALF - 1))
        elif k == 1:
            product = dot(ct[...], rows_of(v3, 1, HALF))
        else:
            product = dot(ct[:, 0:inner], rows_of(v3, 2, HALF - 1))
        for m in range(3):
            term = block(product, m)
            if k == 0:
                term += jnp.where(flip_top, 0.0, block(over_top, m))
                term += jnp.where(flip_bottom, block(over_bottom, 2 - m), 0.0)
            elif k == 2:
                term += jnp.where(flip_bottom, 0.0, block(over_bottom, m))
                term += jnp.where(flip_top, block(over_top, 2 - m), 0.0)
            put_share(reduce_c.shares, 8 - (3 * k + m), term)
        reduce_c.swap_start(2 - k)

    def fine_gradient(k):
        product = dot(gt[...], rows_of(x3, k, RD))
        for m in range(3):
            put_share(reduce_f.shares, 3 * k + m, block(product, m).T)
        reduce_f.swap_start(k)

    for r in range(RD):
        gt[:, r * FS : (r + 1) * FS] = grad_fine[r].astype(F32).T.astype(BF)
    fine_gradient(0)
    halo2.middle()
    fine_gradient(1)
    reduce_c.swap_take()
    fine_gradient(2)
    halo2.finish((flip_top, flip_bottom))
    edge_h[...] = masked_sides(halo2.sides[...].astype(F32), first, last)
    reduce_f.swap_take()

    extended(u3, grad_fine, halo2.hf, edge_h, 0, lambda row: row)
    top, bottom = halo_weights(wtf, flip_top, flip_bottom)
    reduce_c.first_take()
    ga[1 : RD - 1] = jnp.zeros((RD - 2, FS, C), F32)
    ga[0] = dot(u3[0], top)
    ga[RD - 1] = dot(u3[RD + 1], bottom)
    u3[0] = jnp.zeros((FS, 3 * C), BF)
    u3[RD + 1] = jnp.zeros((FS, 3 * C), BF)

    def back(i):
        grad = dot(rows_of(u3, 2 * i, 2), wtf[0])
        grad += dot(rows_of(u3, 2 * i + 1, 2), wtf[1])
        grad += dot(rows_of(u3, 2 * i + 2, 2), wtf[2])
        grad += rows_of(ga, 2 * i, 2)
        normed = (rows_of(feat, 2 * i, 2).astype(F32) - mean) * inverse
        act = normed * scale
        gate = sigmoid(act)
        grad = grad * (gate * (1.0 + act * (1.0 - gate)))
        ga[pl.ds(2 * i, 2)] = grad.reshape(2, FS, C)
        own_c[0:1, :] += jnp.sum(grad * normed, axis=0, keepdims=True)
        own_c[1:2, :] += jnp.sum(grad, axis=0, keepdims=True)

    pl.loop(0, HALF // 2)(back)
    reduce_f.first_take()
    reduce_c.second_take()
    pl.loop(HALF // 2, HALF)(back)
    sum_start(line_a, own_c, buf_c, sc, rc)
    reduce_f.second_take()

    extended(c3, coarse_in, halo2.hc, edge_h, RD + 2, lambda row: row)
    own_d[...] = sum_finish(line_a, own_c, buf_c, sc, rc)
    sum_start(line_b, own_d, buf_d, sd, rd)
    reduce_c.chips_take()

    @pl.loop(0, HALF)
    def _(i):
        out = dot(c3[i], taps_of(wc_taps, 0))
        out += dot(c3[i + 1], taps_of(wc_taps, 1))
        out += dot(c3[i + 2], taps_of(wc_taps, 2))
        wide = spread(widen, out)
        for r in range(2):
            fine[2 * i + r] = (fine[2 * i + r].astype(F32) + wide).astype(BF)

    store_output = pltpu.make_async_copy(fine, output, local.at[5])
    store_output.start()
    sums = sum_finish(line_b, own_d, buf_d, sd, rd)

    grad_gain[...] = sums[0:1] * (1.0 / CELLS)
    grouped = group_sum(sums * scale) / (CELLS * GROUP)
    group_slope, group_shift = grouped[0:1], grouped[1:2]

    @pl.loop(0, RD)
    def _(r):
        normed = (feat[r].astype(F32) - mean) * inverse
        grad = inverse * (scale * ga[r] - group_shift - normed * group_slope)
        grad_fine[r] = grad.astype(BF)

    store_features = pltpu.make_async_copy(grad_fine, grad_features, local.at[4])
    store_features.start()
    reduce_f.chips_take()
    reduce_c.finish(grad_w_coarse)
    reduce_f.finish(grad_w_fine)
    store_features.wait()
    store_output.wait()


def last_kernel(
    features_in, output_in, wf_in, wc_in, gain_in,
    output, grad_features, wf_out, wc_out, gain_out, narrow, sum_v, wide, sems
):
    def rows(ref, q):
        return ref.at[pl.ds(2 * q, 2)]

    def moves(pairs, first):
        return [
            [
                pltpu.make_async_copy(rows(src, q), rows(dst, q), sems.at[first + i, q])
                for i, (src, dst) in enumerate(pairs)
            ]
            for q in range(HALF)
        ]

    loads = moves(((features_in, narrow), (output_in, sum_v)), 0)
    stores = moves(((wide, grad_features), (sum_v, output)), 2)
    for chunk in loads:
        for copy in chunk:
            copy.start()
    wf_out[...] = wf_in[...]
    wc_out[...] = wc_in[...]
    gain_out[...] = gain_in[...]
    for q in range(HALF):
        for load, store in zip(loads[q], stores[q]):
            load.wait()
            if store is stores[q][0]:
                wide[2 * q : 2 * q + 2] = narrow[2 * q : 2 * q + 2].astype(F32)
            store.start()
    for chunk in stores:
        for copy in chunk:
            copy.wait()


def shape(dims, dtype):
    return jax.ShapeDtypeStruct(dims, dtype)


def on_device(features, cotangent, w_fine, w_coarse, gain, neighbors, neighbor_edges):
    outs = [
        shape((RD, FS, C), BF),
        shape((RD, FS, C), F32),
        shape((9, 8, C), F32),
        shape((9, 8, C), F32),
        shape((1, C), F32),
    ]
    narrow = [outs[0], shape((RD, FS, C), BF)] + outs[2:]
    output, grad_features, grad_w_fine, grad_w_coarse, grad_gain = pl.pallas_call(
        whole_kernel,
        in_specs=[VM, VM, ANY, ANY, VM, ANY, ANY],
        out_specs=[ANY, ANY, VM, VM, VM],
        out_shape=narrow,
        scratch_shapes=SUM_SCRATCH * 2
        + HALO_SCRATCH * 2
        + WORK_SCRATCH
        + REDUCE_SCRATCH * 2,
        compiler_params=pltpu.CompilerParams(
            vmem_limit_bytes=VMEM_LIMIT, collective_id=1, has_side_effects=True
        ),
    )(features[0], cotangent[0], w_fine, w_coarse, gain[None], neighbors.T, neighbor_edges.T)
    output, grad_features, grad_w_fine, grad_w_coarse, grad_gain = pl.pallas_call(
        last_kernel,
        in_specs=[ANY, ANY] + [VM] * 3,
        out_specs=[ANY, ANY] + [VM] * 3,
        out_shape=outs,
        scratch_shapes=[
            pltpu.VMEM((RD, FS, C), BF),
            pltpu.VMEM((RD, FS, C), BF),
            pltpu.VMEM((RD, FS, C), F32),
            DMA((4, HALF)),
        ],
        compiler_params=pltpu.CompilerParams(vmem_limit_bytes=VMEM_LIMIT),
    )(grad_features, output, grad_w_fine, grad_w_coarse, grad_gain)
    return (output[None], grad_features[None], grad_w_fine, grad_w_coarse, grad_gain[0])


def solution(mesh):
    return jax.shard_map(
        on_device,
        mesh=mesh,
        in_specs=(
            P("face", "tile", None, None),
            P("face", "tile", None, None),
            P(),
            P(),
            P(),
            P(),
            P(),
        ),
        out_specs=(
            P("face", "tile", None, None),
            P("face", "tile", None, None),
            P(None, "tile", None),
            P(None, "tile", None),
            P(),
        ),
        check_vma=False,
    )
```

```python
import jax
import jax.numpy as jnp
from jax import lax
from jax.experimental import pallas as pl
from jax.experimental.pallas import tpu as pltpu
from jax.sharding import PartitionSpec as P

BF = jnp.bfloat16
F32 = jnp.float32
MESH = pl.DeviceIdType.MESH
NF = 8
NT = 32
NZ = 16
RD = 8
FS = 256
CS = 128
C = 256
GROUP = 8
SLOTS = 16
CELLS = NF * FS * FS
VMEM_LIMIT = 60 * 1024 * 1024

VM = pl.BlockSpec(memory_space=pltpu.VMEM)
SM = pl.BlockSpec(memory_space=pltpu.SMEM)
DMA = pltpu.SemaphoreType.DMA


def remote(src, dst, send, recv, face, tile):
    return pltpu.make_async_remote_copy(
        src_ref=src,
        dst_ref=dst,
        send_sem=send,
        recv_sem=recv,
        device_id=(face, tile),
        device_id_type=MESH,
    )


def place():
    return lax.axis_index("face"), lax.axis_index("tile")


def is_rim(tile):
    return (tile == 0) | (tile == NT - 1)


def slot_device(slot):
    return lax.div(slot, 2), (NT - 1) * lax.rem(slot, 2)


def my_slot(face, tile):
    return 2 * face + jnp.where(tile == NT - 1, 1, 0)


def multiple(value, of):
    return pl.multiple_of(value * of, of)


def signal(barrier, face, tile):
    pl.semaphore_signal(barrier, inc=1, device_id=(face, tile), device_id_type=MESH)


def line_a(face, tile, step):
    mine = lax.rem(tile, NZ)
    other = lax.rem(mine + step, NZ)
    return mine, other, (face, tile - mine + other)


def line_b(face, tile, step):
    mine = face * 2 + lax.div(tile, NZ)
    other = lax.rem(mine + step, 2 * NF)
    return mine, other, (lax.div(other, 2), lax.rem(other, 2) * NZ + lax.rem(tile, NZ))


def barrier_signal():
    face, tile = place()
    barrier = pltpu.get_barrier_semaphore()
    across = lax.rem(tile + NZ, NT)
    across = across - lax.rem(across, NZ) + lax.rem(tile, 2)

    @pl.loop(1, NZ)
    def _(step):
        for line in (line_a, line_b):
            _, _, device = line(face, tile, step)
            signal(barrier, *device)

    @pl.loop(0, NZ // 2)
    def _(z):
        signal(barrier, face, across + 2 * z)

    signal(barrier, face, lax.rem(tile + 1, NT))
    signal(barrier, face, lax.rem(tile + NT - 1, NT))

    @pl.when(is_rim(tile))
    def _():
        mine = my_slot(face, tile)

        @pl.loop(1, SLOTS)
        def _(step):
            signal(barrier, *slot_device(lax.rem(mine + step, SLOTS)))


def barrier_wait():
    _, tile = place()
    barrier = pltpu.get_barrier_semaphore()
    count = 2 * (NZ - 1) + NZ // 2 + 2

    @pl.when(is_rim(tile))
    def _():
        pl.semaphore_wait(barrier, count + SLOTS - 1)

    @pl.when(~is_rim(tile))
    def _():
        pl.semaphore_wait(barrier, count)


def sum_start(line, own, buf, send, recv):
    face, tile = place()

    @pl.loop(1, NZ)
    def _(step):
        mine, _, device = line(face, tile, step)
        remote(own, buf.at[mine], send, recv, *device).start()

    mine, _, _ = line(face, tile, 0)
    buf[mine] = own[...]


def sum_finish(line, own, buf, send, recv):
    face, tile = place()
    _, _, device = line(face, tile, 1)
    arrived = buf.at[pl.ds(0, NZ - 1)]
    copies = remote(arrived, arrived, send, recv, *device)
    copies.wait_recv()
    total = buf[0]
    for i in range(1, NZ):
        total = total + buf[i]
    copies.wait_send()
    return total


SUM_SCRATCH = [
    pltpu.VMEM((2, C), F32),
    pltpu.VMEM((2, C), F32),
    pltpu.VMEM((NZ, 2, C), F32),
    pltpu.VMEM((NZ, 2, C), F32),
    DMA,
    DMA,
    DMA,
    DMA,
]

RIM = C + 128

HALO_SCRATCH = [
    pltpu.VMEM((2, FS, C), BF),
    pltpu.VMEM((2, CS, C), BF),
    pltpu.VMEM((SLOTS, 16, RIM), BF),
    pltpu.VMEM((SLOTS, 16, RIM), BF),
    pltpu.VMEM((SLOTS, 16, RIM), BF),
    pltpu.VMEM((SLOTS, 16, RIM), BF),
    pltpu.VMEM((32, C), F32),
    pltpu.VMEM((32, C), BF),
    pltpu.VMEM((NF, 32, C), BF),
    pltpu.VMEM((32, C), BF),
] + [DMA] * 10


class Halo:
    def __init__(self, fine, coarse, scratch, tables):
        self.fine, self.coarse = fine, coarse
        (
            self.hf,
            self.hc,
            self.rim,
            self.r1,
            self.st,
            self.r2,
            self.rows,
            self.srec,
            self.sall,
            self.sides,
            self.fs,
            self.fr,
            self.cs,
            self.cr,
            self.s1,
            self.q1,
            self.s2,
            self.q2,
            self.ss,
            self.sr,
        ) = scratch
        self.nb, self.ed = tables
        self.face, self.tile = place()
        self.slot = my_slot(self.face, self.tile)

    def rows_start(self):
        up = lax.rem(self.tile + 1, NT)
        down = lax.rem(self.tile + NT - 1, NT)
        for field, halo, send, recv in (
            (self.fine, self.hf, self.fs, self.fr),
            (self.coarse, self.hc, self.cs, self.cr),
        ):
            last = field.shape[0] - 1
            remote(field.at[last], halo.at[0], send, recv, self.face, up).start()
            remote(field.at[0], halo.at[1], send, recv, self.face, down).start()

    def rows_wait(self):
        up = lax.rem(self.tile + 1, NT)
        for halo, send, recv in ((self.hf, self.fs, self.fr), (self.hc, self.cs, self.cr)):
            both = remote(halo, halo, send, recv, self.face, up)
            both.wait_recv()
            both.wait_send()

    def rim_partner(self, step):
        other = lax.rem(self.slot + step, SLOTS)
        return other, slot_device(other)

    def rim_wait(self, buf, send, recv):
        _, device = self.rim_partner(1)
        arrived = buf.at[pl.ds(0, SLOTS - 1)]
        copies = remote(arrived, arrived, send, recv, *device)
        copies.wait_recv()
        copies.wait_send()

    def start(self):
        @pl.when(is_rim(self.tile))
        def _():
            fine_row = jnp.where(self.tile == 0, 0, RD - 1)
            coarse_row = jnp.where(self.tile == 0, 0, RD // 2 - 1)
            self.rim[:, :, 0:C] = self.fine[fine_row].reshape(SLOTS, 16, C)
            cells = self.coarse[coarse_row]
            self.rim[0:8, :, C:RIM] = cells[:, 0:128].reshape(8, 16, 128)
            self.rim[8:16, :, C:RIM] = cells[:, 128:256].reshape(8, 16, 128)

            @pl.loop(1, SLOTS)
            def _(step):
                other, device = self.rim_partner(step)
                remote(self.rim.at[other], self.r1.at[self.slot], self.s1, self.q1, *device).start()

            self.r1[self.slot] = self.rim[self.slot]

        self.rows_start()

    def middle(self):
        @pl.when(is_rim(self.tile))
        def _():
            self.rim_wait(self.r1, self.s1, self.q1)

            @pl.loop(0, SLOTS)
            def _(slot):
                face, edge = lax.div(slot, 2), 2 * lax.rem(slot, 2)
                source = 2 * self.nb[edge, face] + lax.div(self.ed[edge, face], 2)
                self.st[slot] = self.r1[source]

            @pl.loop(1, SLOTS)
            def _(step):
                other, device = self.rim_partner(step)
                remote(self.st.at[other], self.r2.at[self.slot], self.s2, self.q2, *device).start()

            self.r2[self.slot] = self.st[self.slot]

        self.rows_wait()
        fine_rows = [self.hf.at[0]] + [self.fine.at[r] for r in range(RD)] + [self.hf.at[1]]
        coarse_rows = [self.hc.at[0]] + [self.coarse.at[r] for r in range(RD // 2)]
        coarse_rows += [self.hc.at[1]]
        for i, row in enumerate(fine_rows + coarse_rows):
            side = row.shape[0]
            self.rows[i : i + 1, :] = row[0:16, :].astype(F32)[0:1]
            self.rows[16 + i : 17 + i, :] = row[side - 16 : side, :].astype(F32)[15:16]
        self.srec[...] = self.rows[...].astype(BF)

        @pl.loop(1, NF)
        def _(step):
            other = lax.rem(self.face + step, NF)
            remote(
                self.srec, self.sall.at[self.face], self.ss, self.sr, other, self.tile
            ).start()

        self.sall[self.face] = self.srec[...]

    def finish(self, flips):
        @pl.when(is_rim(self.tile))
        def _():
            self.rim_wait(self.r2, self.s2, self.q2)
            flip_top, flip_bottom = flips
            flip = jnp.where(self.tile == 0, flip_top, flip_bottom)
            edge = jnp.where(self.tile == 0, 0, 1)
            fine = self.r2[:, :, 0:C].reshape(FS, C)
            coarse = jnp.concatenate(
                [
                    self.r2[0:8, :, C:RIM].reshape(CS, 128),
                    self.r2[8:16, :, C:RIM].reshape(CS, 128),
                ],
                axis=1,
            )
            self.hf[edge] = dot(rim_matrix(FS, flip), fine).astype(BF)
            self.hc[edge] = dot(rim_matrix(CS, flip), coarse).astype(BF)

        other = lax.rem(self.face + 1, NF)
        arrived = self.sall.at[pl.ds(0, NF - 1)]
        copies = remote(arrived, arrived, self.ss, self.sr, other, self.tile)
        copies.wait_recv()
        copies.wait_send()
        left_face, right_face = self.nb[3, self.face], self.nb[1, self.face]
        self.sides[0:16, :] = self.sall[left_face, 16:32, :]
        self.sides[16:32, :] = self.sall[right_face, 0:16, :]


def iota(shape, dim):
    return lax.broadcasted_iota(jnp.int32, shape, dim)


def dot(a, b):
    return jnp.dot(a, b, preferred_element_type=F32)


def sigmoid(values):
    return 0.5 * jnp.tanh(0.5 * values) + 0.5


def pool_matrix():
    row, col = iota((CS, 2 * FS), 0), iota((CS, 2 * FS), 1)
    return jnp.where(lax.div(lax.rem(col, FS), 2) == row, 1.0, 0.0).astype(BF)


def spread_matrix():
    row, col = iota((FS, 2 * CS), 0), iota((FS, 2 * CS), 1)
    return jnp.where(lax.rem(col, CS) == lax.div(row, 2), 1.0, 0.0).astype(BF)


def spread(matrix, values):
    high = values.astype(BF)
    low = (values - high.astype(F32)).astype(BF)
    return dot(matrix, jnp.concatenate([high, low], axis=0))


def rim_matrix(side, flip):
    row, col = iota((side, side), 0), iota((side, side), 1)
    source = jnp.where(flip, side - 1 - row, row)
    return jnp.where(col == source, 1.0, 0.0).astype(BF)


def store_shifted(ref, row, values, left, right):
    n = values.shape[0]
    position = iota(values.shape, 0)
    before = jnp.where(position == 0, left, pltpu.roll(values, 1, 0))
    after = jnp.where(position == n - 1, right, pltpu.roll(values, n - 1, 0))
    ref[row, :, 0:C] = before.astype(BF)
    ref[row, :, C : 2 * C] = values.astype(BF)
    ref[row, :, 2 * C : 3 * C] = after.astype(BF)


def group_sum(values):
    lane = iota(values.shape, 1)
    for width in (1, 2, 4):
        up = pltpu.roll(values, width, 1)
        down = pltpu.roll(values, C - width, 1)
        values = values + jnp.where(lax.rem(lax.div(lane, width), 2) == 0, down, up)
    return values


def norm_vectors(total):
    grouped = group_sum(total) / (CELLS * GROUP)
    mean, second = grouped[0:1], grouped[1:2]
    return mean, lax.rsqrt(second - mean * mean + 1e-05)


def edge_flags(ed_ref):
    face, tile = place()
    first, last = tile == 0, tile == NT - 1
    flip_top = first & (ed_ref[0, face] != 2)
    flip_bottom = last & (ed_ref[2, face] != 0)
    return first, last, flip_top, flip_bottom


def masked_sides(sides, first, last):
    row = lax.rem(iota(sides.shape, 0), 16)
    top = (row == 0) | (row == RD + 2)
    bottom = (row == RD + 1) | (row == 15)
    zero = (top & first) | (bottom & last)
    return jnp.where(zero, 0.0, sides)


def back_weights(w_ref, out_ref):
    for k in range(3):
        for m in range(3):
            tap = w_ref[8 - (3 * k + m)].astype(F32)
            out_ref[k, m * C : (m + 1) * C, :] = tap.T.astype(BF)


def halo_weights(wt_ref, flip_top, flip_bottom):
    def turned(k):
        return jnp.concatenate(
            [wt_ref[k, (2 - m) * C : (3 - m) * C, :] for m in range(3)], axis=0
        )

    top = jnp.where(flip_top, turned(2), wt_ref[0])
    bottom = jnp.where(flip_bottom, turned(0), wt_ref[2])
    return top, bottom


def rows_of(ref, start, count):
    _, side, width = ref.shape
    return ref[pl.ds(start, count)].reshape(count * side, width)


def taps_of(ref, k):
    return ref[3 * k : 3 * k + 3].reshape(3 * C, C)


SHARE = 144
NC = 16


def put_share(shares, tap, product):
    cut = product.reshape(4, 4, 2, 8, C)
    halves = [cut[..., :128], cut[..., 128:]]
    shares[:, :, :, 16 * tap : 16 * tap + 16, :] = jnp.concatenate(halves, axis=3).astype(BF)


def put_grads(out, total):
    total = (total * (1.0 / CELLS)).reshape(9, 2, 8, 128)
    out[:, :, 0:128] = total[:, 0]
    out[:, :, 128:256] = total[:, 1]


def tree(parts):
    parts = [part.astype(F32) for part in parts]
    while len(parts) > 1:
        parts = [sum(parts[i : i + 2]) for i in range(0, len(parts), 2)]
    return parts[0]


CUT = 80
LANES = ((0, CUT), (CUT, SHARE - CUT))

REDUCE_SCRATCH = [
    pltpu.VMEM((4, 4, 2, SHARE, 128), BF),
    pltpu.VMEM((4, 4, SHARE, 128), BF),
    pltpu.VMEM((4, 4, SHARE, 128), BF),
    pltpu.VMEM((2, 4, CUT, 128), BF),
    pltpu.VMEM((2, 4, SHARE - CUT, 128), BF),
    pltpu.VMEM((4, CUT, 128), BF),
    pltpu.VMEM((4, SHARE - CUT, 128), BF),
    pltpu.VMEM((4, CUT, 128), BF),
    pltpu.VMEM((4, SHARE - CUT, 128), BF),
    pltpu.VMEM((4, SHARE, 128), BF),
    pltpu.VMEM((NC, SHARE, 128), BF),
    pltpu.VMEM((SHARE, 128), BF),
    pltpu.VMEM((2, SHARE, 128), BF),
    DMA((3,)),
    DMA((3,)),
    DMA((2,)),
    DMA((2,)),
    DMA((2,)),
    DMA((2,)),
    DMA((4,)),
    DMA,
    DMA,
    DMA((2,)),
]


class Reduce:
    def __init__(self, scratch):
        (
            self.shares,
            self.got,
            self.part,
            r0,
            r1,
            t0,
            t1,
            u0,
            u1,
            self.px,
            self.rz,
            self.block,
            self.rb,
            self.s0,
            self.q0,
            self.sa,
            self.qa,
            self.sc,
            self.qc,
            self.sz,
            self.qz,
            self.sb,
            self.qb,
        ) = scratch
        self.one, self.on, self.two = (r0, r1), (t0, t1), (u0, u1)
        self.face, self.tile = place()
        self.core, self.chip = lax.rem(self.tile, 2), lax.div(self.tile, 2)
        self.x, self.high = lax.div(self.face, 2), lax.rem(self.face, 2)
        self.home = lax.rem(self.chip, 4)
        self.owner = self.home == self.x
        near = self.x + 1 - 2 * lax.rem(self.x, 2)
        self.partner = (near, 3 - self.x)

    def swap(self, k):
        rows = pl.ds(48 * k, 48)
        return remote(
            self.shares.at[:, :, 1 - self.core, rows, :],
            self.got.at[:, :, rows, :],
            self.s0.at[k],
            self.q0.at[k],
            self.face,
            self.tile + 1 - 2 * self.core,
        )

    def swap_start(self, k):
        self.swap(k).start()

    def across(self, way, src, dst, send, recv):
        return remote(src, dst, send, recv, 2 * self.partner[way] + self.high, self.tile)

    def first(self, way, i):
        other = self.partner[way]
        beyond = 3 - other if way == 0 else other + 1 - 2 * lax.rem(other, 2)
        start, rows = LANES[way]
        return self.across(
            way,
            self.part.at[:, (other, beyond)[i], pl.ds(start, rows), :],
            self.one[way].at[i],
            self.sa.at[way],
            self.qa.at[way],
        )

    def first_wait(self, way):
        return self.across(way, self.one[way], self.one[way], self.sa.at[way], self.qa.at[way])

    def second(self, way):
        return self.across(1 - way, self.on[way], self.two[way], self.sc.at[way], self.qc.at[way])

    def swap_take(self):
        for k in range(3):
            self.swap(k).wait_recv()

        @pl.loop(0, 4)
        def _(j):
            for h in range(4):
                both = self.shares[j, h, self.core].astype(F32) + self.got[j, h].astype(F32)
                self.part[j, h] = both.astype(BF)

        for way in range(2):
            for i in range(2):
                self.first(way, i).start()

    def first_take(self):
        for way in range(2):
            self.first_wait(way).wait_recv()
            start, rows = LANES[way]
            span = pl.ds(start, rows)
            mine = self.part[:, self.partner[1 - way], span, :].astype(F32)
            self.on[way][...] = (mine + self.one[way][1].astype(F32)).astype(BF)
            self.second(way).start()

    def second_take(self):
        for way in range(2):
            self.second(way).wait_recv()
            start, rows = LANES[way]
            mine = self.part[:, self.x, pl.ds(start, rows), :].astype(F32)
            total = mine + self.one[way][0].astype(F32) + self.two[way][...].astype(F32)
            self.px[:, start : start + rows, :] = total.astype(BF)

        @pl.loop(0, 4)
        def _(j):
            mine = 4 * j + self.x == self.chip

            @pl.when(jnp.logical_not(mine))
            def _():
                self.scatter(j).start()

            @pl.when(mine)
            def _():
                self.rz[self.chip] = self.px[j]

    def scatter(self, j):
        return remote(
            self.px.at[j],
            self.rz.at[self.chip],
            self.sz.at[j],
            self.qz,
            self.face,
            2 * (4 * j + self.x) + self.core,
        )

    def share(self, other):
        return remote(
            self.block, self.rb.at[self.high], self.sb, self.qb.at[self.high], other, self.tile
        )

    def chips_take(self):
        @pl.when(self.owner)
        def _():
            arrived = self.rz.at[pl.ds(0, NC - 1)]
            other = lax.rem(self.chip + 1, NC)
            remote(
                arrived, arrived, self.sb, self.qz, self.face, 2 * other + self.core
            ).wait_recv()
            self.block[...] = tree([self.rz[j] for j in range(NC)]).astype(BF)

            @pl.loop(1, NF)
            def _(step):
                self.share(lax.rem(self.face + step, NF)).start()

            self.rb[self.high] = self.block[...]

    def finish(self, out):
        for high in range(2):
            source = 2 * self.home + high

            @pl.when(source != self.face)
            def _():
                remote(
                    self.block, self.rb.at[high], self.sb, self.qb.at[high], source, self.tile
                ).wait_recv()

        put_grads(out, tree([self.rb[0], self.rb[1]]))

        for k in range(3):
            self.swap(k).wait_send()
        for way in range(2):
            self.first_wait(way).wait_send()
            self.second(way).wait_send()

        @pl.loop(0, 4)
        def _(j):
            @pl.when(4 * j + self.x != self.chip)
            def _():
                self.scatter(j).wait_send()

        @pl.when(self.owner)
        def _():
            sent = self.rz.at[pl.ds(0, NF - 1)]
            remote(
                sent, sent, self.sb, self.qz, lax.rem(self.face + 1, NF), self.tile
            ).wait_send()


HALF = RD // 2
N_SUM, N_HALO = len(SUM_SCRATCH), len(HALO_SCRATCH)

ANY = pl.BlockSpec(memory_space=pl.ANY)

WORK_SCRATCH = [
    pltpu.SMEM((4, NF), jnp.int32),
    pltpu.SMEM((4, NF), jnp.int32),
    pltpu.VMEM((RD, FS, C), BF),
    pltpu.VMEM((RD, FS, C), BF),
    pltpu.VMEM((9, C, C), BF),
    pltpu.VMEM((9, C, C), BF),
    pltpu.VMEM((HALF, CS, C), BF),
    pltpu.VMEM((3, 3 * C, C), BF),
    pltpu.VMEM((3, 3 * C, C), BF),
    pltpu.VMEM((RD + 2, FS, 3 * C), BF),
    pltpu.VMEM((RD + 2, FS, 3 * C), BF),
    pltpu.VMEM((HALF + 2, CS, 3 * C), BF),
    pltpu.VMEM((HALF + 2, CS, 3 * C), BF),
    pltpu.VMEM((RD, FS, C), BF),
    pltpu.VMEM((HALF, CS, C), BF),
    pltpu.VMEM((RD, FS, C), BF),
    pltpu.VMEM((RD, FS, C), F32),
    pltpu.VMEM((HALF, CS, C), F32),
    pltpu.VMEM((C, RD * FS), BF),
    pltpu.VMEM((C, HALF * CS), BF),
    pltpu.VMEM((32, C), F32),
    pltpu.VMEM((32, C), F32),
    DMA((8,)),
]


def extended(ref3, field, halo, edge, first, side):
    rows = field.shape[0]

    def put(i, row):
        left, right = edge[pl.ds(first + i, 1), :], edge[pl.ds(first + i + 16, 1), :]
        store_shifted(ref3, i, side(row.astype(F32)), left, right)

    put(0, halo[0])
    put(rows + 1, halo[1])

    @pl.loop(0, rows)
    def _(r):
        put(r + 1, field[r])


def whole_kernel(
    feat_any, cot_any, wf_any, wc_any, gain, nb_any, ed_any,
    output, grad_features, grad_w_fine, grad_w_coarse, grad_gain, *scratch
):
    scratch = list(scratch)

    def take(n):
        got = scratch[:n]
        del scratch[:n]
        return got

    own_a, own_b, buf_a, buf_b, sa, ra, sb, rb = take(N_SUM)
    own_c, own_d, buf_c, buf_d, sc, rc, sd, rd = take(N_SUM)
    halo1_scratch, halo2_scratch = take(N_HALO), take(N_HALO)
    (
        nb, ed, feat, cot, wf_taps, wc_taps, gco, wtf, wtc, x3, u3, c3, v3, fine, coarse_in, grad_fine,
        ga, gci, gt, ct, edge_h, edge_c, local,
    ) = take(len(WORK_SCRATCH))
    reduce_f = Reduce(take(len(REDUCE_SCRATCH)))
    reduce_c = Reduce(take(len(REDUCE_SCRATCH)))

    loads = [
        pltpu.make_async_copy(src, dst, local.at[i])
        for i, (src, dst) in enumerate(
            (
                (feat_any, feat),
                (cot_any, cot),
                (nb_any, nb),
                (ed_any, ed),
                (wc_any, wc_taps),
                (wf_any, wf_taps),
            )
        )
    ]
    for load in loads:
        load.start()
    barrier_signal()
    halo1 = Halo(feat, gco, halo1_scratch, (nb, ed))
    halo2 = Halo(grad_fine, coarse_in, halo2_scratch, (nb, ed))

    pool, widen = pool_matrix(), spread_matrix()
    for load in loads[:2]:
        load.wait()
    own_a[...] = jnp.zeros_like(own_a)
    own_c[...] = jnp.zeros_like(own_c)

    @pl.loop(0, HALF)
    def _(i):
        gco[i] = dot(pool, rows_of(cot, 2 * i, 2)).astype(BF)
        values = rows_of(feat, 2 * i, 2).astype(F32)
        own_a[0:1, :] += jnp.sum(values, axis=0, keepdims=True)
        own_a[1:2, :] += jnp.sum(values * values, axis=0, keepdims=True)

    barrier_wait()
    sum_start(line_a, own_a, buf_a, sa, ra)
    halo1.start()
    for load in loads[2:]:
        load.wait()
    back_weights(wc_taps, wtc)
    own_b[...] = sum_finish(line_a, own_a, buf_a, sa, ra)
    sum_start(line_b, own_b, buf_b, sb, rb)
    halo1.middle()
    back_weights(wf_taps, wtf)

    first, last, flip_top, flip_bottom = edge_flags(ed)
    halo1.finish((flip_top, flip_bottom))
    edge_c[...] = masked_sides(halo1.sides[...].astype(F32), first, last)

    extended(v3, gco, halo1.hc, edge_c, RD + 2, lambda row: row)
    top, bottom = halo_weights(wtc, flip_top, flip_bottom)
    gci[...] = dot(rows_of(v3, 1, HALF), wtc[1]).reshape(HALF, CS, C)
    gci[1:HALF] += dot(rows_of(v3, 1, HALF - 1), wtc[0]).reshape(HALF - 1, CS, C)
    gci[0 : HALF - 1] += dot(rows_of(v3, 2, HALF - 1), wtc[2]).reshape(HALF - 1, CS, C)
    gci[0] += dot(v3[0], top)
    gci[HALF - 1] += dot(v3[HALF + 1], bottom)

    total = sum_finish(line_b, own_b, buf_b, sb, rb)
    mean, inverse = norm_vectors(total)
    scale = gain[...]

    def hidden(raw):
        act = (raw - mean) * inverse * scale
        return (act * sigmoid(act)).astype(BF).astype(F32)

    edge_h[...] = masked_sides(hidden(halo1.sides[...].astype(F32)), first, last)
    extended(x3, feat, halo1.hf, edge_h, 0, hidden)

    def forward(i):
        acc = dot(rows_of(x3, 2 * i, 2), taps_of(wf_taps, 0))
        acc += dot(rows_of(x3, 2 * i + 1, 2), taps_of(wf_taps, 1))
        acc += dot(rows_of(x3, 2 * i + 2, 2), taps_of(wf_taps, 2))
        out = acc.astype(BF)
        fine[pl.ds(2 * i, 2)] = out.reshape(2, FS, C)
        pooled = 0.25 * dot(pool, out)
        gate = sigmoid(pooled)
        coarse_in[i] = (pooled * gate).astype(BF)
        slope = gate * (1.0 + pooled * (1.0 - gate))
        wide = spread(widen, gci[i] * slope * 0.25)
        for r in range(2):
            grad_fine[2 * i + r] = (cot[2 * i + r].astype(F32) + wide).astype(BF)

    @pl.loop(0, 2)
    def _(i):
        forward((HALF - 1) * i)

    halo2.start()
    pl.loop(1, HALF - 1)(forward)

    for r in range(HALF):
        ct[:, r * CS : (r + 1) * CS] = coarse_in[r].astype(F32).T.astype(BF)
    inner = (HALF - 1) * CS
    over_top = dot(ct[:, 0:CS], v3[0])
    over_bottom = dot(ct[:, inner:], v3[HALF + 1])

    def block(product, m):
        return product[:, m * C : (m + 1) * C]

    for k in (2, 1, 0):
        if k == 0:
            product = dot(ct[:, CS:], rows_of(v3, 1, HALF - 1))
        elif k == 1:
            product = dot(ct[...], rows_of(v3, 1, HALF))
        else:
            product = dot(ct[:, 0:inner], rows_of(v3, 2, HALF - 1))
        for m in range(3):
            term = block(product, m)
            if k == 0:
                term += jnp.where(flip_top, 0.0, block(over_top, m))
                term += jnp.where(flip_bottom, block(over_bottom, 2 - m), 0.0)
            elif k == 2:
                term += jnp.where(flip_bottom, 0.0, block(over_bottom, m))
                term += jnp.where(flip_top, block(over_top, 2 - m), 0.0)
            put_share(reduce_c.shares, 8 - (3 * k + m), term)
        reduce_c.swap_start(2 - k)

    def fine_gradient(k):
        product = dot(gt[...], rows_of(x3, k, RD))
        for m in range(3):
            put_share(reduce_f.shares, 3 * k + m, block(product, m).T)
        reduce_f.swap_start(k)

    for r in range(RD):
        gt[:, r * FS : (r + 1) * FS] = grad_fine[r].astype(F32).T.astype(BF)
    fine_gradient(0)
    halo2.middle()
    fine_gradient(1)
    reduce_c.swap_take()
    fine_gradient(2)
    halo2.finish((flip_top, flip_bottom))
    edge_h[...] = masked_sides(halo2.sides[...].astype(F32), first, last)
    reduce_f.swap_take()

    extended(u3, grad_fine, halo2.hf, edge_h, 0, lambda row: row)
    top, bottom = halo_weights(wtf, flip_top, flip_bottom)
    reduce_c.first_take()
    ga[1 : RD - 1] = jnp.zeros((RD - 2, FS, C), F32)
    ga[0] = dot(u3[0], top)
    ga[RD - 1] = dot(u3[RD + 1], bottom)
    u3[0] = jnp.zeros((FS, 3 * C), BF)
    u3[RD + 1] = jnp.zeros((FS, 3 * C), BF)

    def back(i):
        grad = dot(rows_of(u3, 2 * i, 2), wtf[0])
        grad += dot(rows_of(u3, 2 * i + 1, 2), wtf[1])
        grad += dot(rows_of(u3, 2 * i + 2, 2), wtf[2])
        grad += rows_of(ga, 2 * i, 2)
        normed = (rows_of(feat, 2 * i, 2).astype(F32) - mean) * inverse
        act = normed * scale
        gate = sigmoid(act)
        grad = grad * (gate * (1.0 + act * (1.0 - gate)))
        ga[pl.ds(2 * i, 2)] = grad.reshape(2, FS, C)
        own_c[0:1, :] += jnp.sum(grad * normed, axis=0, keepdims=True)
        own_c[1:2, :] += jnp.sum(grad, axis=0, keepdims=True)

    pl.loop(0, HALF // 2)(back)
    reduce_f.first_take()
    reduce_c.second_take()
    pl.loop(HALF // 2, HALF)(back)
    sum_start(line_a, own_c, buf_c, sc, rc)
    reduce_f.second_take()

    extended(c3, coarse_in, halo2.hc, edge_h, RD + 2, lambda row: row)
    own_d[...] = sum_finish(line_a, own_c, buf_c, sc, rc)
    sum_start(line_b, own_d, buf_d, sd, rd)
    reduce_c.chips_take()

    @pl.loop(0, HALF)
    def _(i):
        out = dot(c3[i], taps_of(wc_taps, 0))
        out += dot(c3[i + 1], taps_of(wc_taps, 1))
        out += dot(c3[i + 2], taps_of(wc_taps, 2))
        wide = spread(widen, out)
        for r in range(2):
            fine[2 * i + r] = (fine[2 * i + r].astype(F32) + wide).astype(BF)

    store_output = pltpu.make_async_copy(fine, output, local.at[7])
    store_output.start()
    reduce_f.chips_take()
    sums = sum_finish(line_b, own_d, buf_d, sd, rd)

    grad_gain[...] = sums[0:1] * (1.0 / CELLS)
    grouped = group_sum(sums * scale) / (CELLS * GROUP)
    group_slope, group_shift = grouped[0:1], grouped[1:2]

    @pl.loop(0, RD)
    def _(r):
        normed = (feat[r].astype(F32) - mean) * inverse
        grad = inverse * (scale * ga[r] - group_shift - normed * group_slope)
        grad_fine[r] = grad.astype(BF)

    store_features = pltpu.make_async_copy(grad_fine, grad_features, local.at[6])
    store_features.start()
    reduce_c.finish(grad_w_coarse)
    reduce_f.finish(grad_w_fine)
    store_features.wait()
    store_output.wait()


def last_kernel(
    features_in, output_in, wf_in, wc_in, gain_in,
    output, grad_features, wf_out, wc_out, gain_out, narrow, sum_v, wide, sems
):
    def rows(ref, q):
        return ref.at[pl.ds(2 * q, 2)]

    def moves(pairs, first):
        return [
            [
                pltpu.make_async_copy(rows(src, q), rows(dst, q), sems.at[first + i, q])
                for i, (src, dst) in enumerate(pairs)
            ]
            for q in range(HALF)
        ]

    loads = moves(((features_in, narrow), (output_in, sum_v)), 0)
    stores = moves(((wide, grad_features), (sum_v, output)), 2)
    for chunk in loads:
        for copy in chunk:
            copy.start()
    wf_out[...] = wf_in[...]
    wc_out[...] = wc_in[...]
    gain_out[...] = gain_in[...]
    for q in range(HALF):
        for load, store in zip(loads[q], stores[q]):
            load.wait()
            if store is stores[q][0]:
                wide[2 * q : 2 * q + 2] = narrow[2 * q : 2 * q + 2].astype(F32)
            store.start()
    for chunk in stores:
        for copy in chunk:
            copy.wait()


def shape(dims, dtype):
    return jax.ShapeDtypeStruct(dims, dtype)


def on_device(features, cotangent, w_fine, w_coarse, gain, neighbors, neighbor_edges):
    outs = [
        shape((RD, FS, C), BF),
        shape((RD, FS, C), F32),
        shape((9, 8, C), F32),
        shape((9, 8, C), F32),
        shape((1, C), F32),
    ]
    narrow = [outs[0], shape((RD, FS, C), BF)] + outs[2:]
    output, grad_features, grad_w_fine, grad_w_coarse, grad_gain = pl.pallas_call(
        whole_kernel,
        in_specs=[ANY] * 4 + [VM] + [ANY] * 2,
        out_specs=[ANY, ANY, VM, VM, VM],
        out_shape=narrow,
        scratch_shapes=SUM_SCRATCH * 2
        + HALO_SCRATCH * 2
        + WORK_SCRATCH
        + REDUCE_SCRATCH * 2,
        compiler_params=pltpu.CompilerParams(
            vmem_limit_bytes=VMEM_LIMIT, collective_id=1, has_side_effects=True
        ),
    )(features[0], cotangent[0], w_fine, w_coarse, gain[None], neighbors.T, neighbor_edges.T)
    output, grad_features, grad_w_fine, grad_w_coarse, grad_gain = pl.pallas_call(
        last_kernel,
        in_specs=[ANY, ANY] + [VM] * 3,
        out_specs=[ANY, ANY] + [VM] * 3,
        out_shape=outs,
        scratch_shapes=[
            pltpu.VMEM((RD, FS, C), BF),
            pltpu.VMEM((RD, FS, C), BF),
            pltpu.VMEM((RD, FS, C), F32),
            DMA((4, HALF)),
        ],
        compiler_params=pltpu.CompilerParams(vmem_limit_bytes=VMEM_LIMIT),
    )(grad_features, output, grad_w_fine, grad_w_coarse, grad_gain)
    return (output[None], grad_features[None], grad_w_fine, grad_w_coarse, grad_gain[0])


def solution(mesh):
    return jax.shard_map(
        on_device,
        mesh=mesh,
        in_specs=(
            P("face", "tile", None, None),
            P("face", "tile", None, None),
            P(),
            P(),
            P(),
            P(),
            P(),
        ),
        out_specs=(
            P("face", "tile", None, None),
            P("face", "tile", None, None),
            P(None, "tile", None),
            P(None, "tile", None),
            P(),
        ),
        check_vma=False,
    )
```
